256 devices in a mesh: ctx: 64 (over z, x, core), head: 4 (over y).
Axes of the slice: x: 4, y: 4, z: 8, core: 2. Of those that a mesh axis runs over, the one named last changes fastest.
Arguments:
- queries: bfloat16 [8192, 2048], P('ctx', 'head'), may hold values from -6 to 6
- keys: bfloat16 [8192, 512], P('ctx', 'head'), may hold values from -6 to 6
- values: bfloat16 [8192, 512], P('ctx', 'head'), may hold values from -6 to 6
- out_grad: bfloat16 [8192, 2048], P('ctx', 'head'), may hold values from -6 to 6
- gate_logits: float32 [8192, 16], P(('ctx', 'head')), may hold values from -1 to 14
- doc_lengths: int32 [16], replicated, may hold values from 1 to 2048, 8192 in all
- span_order: int32 [128], replicated, may hold values from 0 to 127, each once
Outputs:
- query_grad: bfloat16 [8192, 2048], P('ctx', 'head')
- key_grad: bfloat16 [8192, 512], P('ctx', 'head')
- value_grad: bfloat16 [8192, 512], P('ctx', 'head')
- forget_grad: float32 [8192, 16], P('ctx', 'head')
The draws below stay inside these ranges and needn't reach their ends.
Inputs may be any that keep to these rules, and one draw needn't show every extreme that they name: Stored rows b * 64 to (b + 1) * 64 - 1 hold the logical span span_order[b], in order; every span appears once. `doc_lengths`: the lengths sum to 8192; the longest is exactly 2048.
All inputs are finite; a program needn't handle non-finite values.
Results may differ from the reference program's by a relative error of at most 0.0049.
Values may be sent and summed in bfloat16 or wider, within the bound.
No kernel may reach another device: no remote copies, remote signals or barrier semaphores. Data moves between devices by JAX's collectives and lax.ppermute only.
A program may use at most 192 MiB of HBM per device.

```python
import math
import jax
import jax.numpy as jnp
import numpy as np
from jax import lax

ASKER_GROUP_SHARE = 16
KV_HEADS = 4
HD = 128
DOCS = 16
SPAN = 64
STREAM_ELEMENTS = 8192
SPANS = 128
MAXDOC = 2048


def draw_queries(key, part):
    key = jax.random.fold_in(key, 11)
    drawn = jnp.clip(jax.random.normal(key, (STREAM_ELEMENTS, ASKER_GROUP_SHARE, HD), jnp.float32), -4.0, 4.0)
    return drawn.reshape(STREAM_ELEMENTS, ASKER_GROUP_SHARE * HD).astype(jnp.bfloat16)


def draw_keys(key, part):
    key = jax.random.fold_in(key, 31)
    drawn = jnp.clip(jax.random.normal(key, (STREAM_ELEMENTS, KV_HEADS, HD), jnp.float32), -4.0, 4.0)
    return drawn.reshape(STREAM_ELEMENTS, KV_HEADS * HD).astype(jnp.bfloat16)


def draw_gate_logits(key, part):
    key = jax.random.fold_in(key, 23)
    stream_segments = jax.random.split(key, 7)
    fast_share = 0.5
    fast = jax.random.uniform(stream_segments[0], (ASKER_GROUP_SHARE,)) < fast_share
    fast_rate = jnp.exp(jax.random.uniform(stream_segments[1], (ASKER_GROUP_SHARE,), jnp.float32, math.log(1.0 / 50.0), math.log(1.0 / 30.0)))
    slow_rate = jnp.exp(jax.random.uniform(stream_segments[2], (ASKER_GROUP_SHARE,), jnp.float32, math.log(0.2), math.log(0.8))) / STREAM_ELEMENTS
    rate = jnp.where(fast, fast_rate, slow_rate)
    rough = jax.random.uniform(stream_segments[3], (STREAM_ELEMENTS, ASKER_GROUP_SHARE), jnp.float32, 0.5, 1.5)
    factor = jnp.exp(jax.random.uniform(stream_segments[4], (STREAM_ELEMENTS // SPAN, 1, ASKER_GROUP_SHARE), jnp.float32, math.log(0.5), math.log(2.0)))
    factor = jnp.broadcast_to(factor, (STREAM_ELEMENTS // SPAN, SPAN, ASKER_GROUP_SHARE)).reshape(STREAM_ELEMENTS, ASKER_GROUP_SHARE)
    overall_objective = rate[None, :] * rough * factor
    element_batch_entries = jax.random.randint(stream_segments[5], (2, ASKER_GROUP_SHARE), 0, STREAM_ELEMENTS)
    position_array = jnp.arange(STREAM_ELEMENTS, dtype=jnp.int32)
    element_batch = jnp.any(position_array[:, None, None] == element_batch_entries[None, :, :], axis=1)
    element_batch_objective = -jnp.log(jax.random.uniform(stream_segments[6], (STREAM_ELEMENTS, ASKER_GROUP_SHARE), jnp.float32, 0.5, 0.8))
    overall_objective = jnp.where(element_batch, element_batch_objective, overall_objective)
    return -jnp.log(jnp.expm1(overall_objective))


def steps_of(own_key, extent, cuts, low, high):
    def one(position, shards_of):
        steps = jax.random.uniform(jax.random.fold_in(jax.random.fold_in(own_key, 6), position), (shards_of,), jnp.float32, low / len(cuts), high / len(cuts))
        return jnp.repeat(jnp.exp(steps), extent[position] // shards_of).reshape((-1,) + (1,) * (len(extent) - position - 1))

    level = one(*cuts[0])
    for cut in cuts[1:]:
        level = level * one(*cut)
    return level


def length_profile(count, total, bound, lean):
    portions = [(1 << 20) // math.isqrt(rank ** lean) + 1 for rank in range(2, count + 1)]
    rest, counts = total - bound - (count - 1), [1] * (count - 1)
    while rest > 0:
        free = [i for i in range(count - 1) if counts[i] < bound]
        mass, remaining = sum([portions[i] for i in free]), rest
        for i in free:
            extra = min(bound - counts[i], max(1, remaining * portions[i] // mass), rest)
            counts[i] = counts[i] + extra
            rest = rest - extra
    return np.array([bound] + counts)


def ragged_sizes(rng, count, total, bound, lean):
    if count == 2:
        one = jax.random.randint(rng, (), max(1, total - bound), min(bound, total - 1) + 1)
        return jnp.stack([one, total - one])
    tallies = jnp.asarray(length_profile(count, total, bound, lean), jnp.int32)
    couples = (count - 1) // 2
    source_of, receiver = tallies[1:1 + 2 * couples:2], tallies[2:2 + 2 * couples:2]
    room = jnp.minimum(source_of - 1, bound - receiver)
    moved = jax.random.randint(jax.random.fold_in(rng, 1), (couples,), 0, 1 << 20) % (room + 1)
    tallies = tallies.at[1:1 + 2 * couples:2].set(source_of - moved).at[2:2 + 2 * couples:2].set(receiver + moved)
    return tallies[jax.random.permutation(jax.random.fold_in(rng, 2), count)]


def centred(key, dims, scale, bound, pieces=(), held_as=jnp.bfloat16):
    entries = jax.random.normal(key, dims, jnp.float32) * scale
    if len(pieces) > 0:
        entries = steps_of(key, dims, pieces, -0.22, 0.18) * entries
    return jnp.clip(entries, min=-bound, max=bound).astype(held_as)


def setup_inputs(seed: int = 0) -> dict:
    splits = jax.random.split(jax.random.key(seed), 8)
    return {
        "queries": draw_queries(jax.random.fold_in(splits[7], 71), 0),
        "keys": draw_keys(jax.random.fold_in(splits[7], 71), 0),
        "values": centred(splits[2], (STREAM_ELEMENTS, KV_HEADS * HD), 1.0, 6.0, ((0, 64), (1, 4))),
        "out_grad": centred(splits[3], (STREAM_ELEMENTS, ASKER_GROUP_SHARE * HD), 1.0, 6.0, ((0, 64), (1, 4))),
        "gate_logits": draw_gate_logits(jax.random.fold_in(splits[7], 71), 0),
        "doc_lengths": ragged_sizes(splits[5], DOCS, STREAM_ELEMENTS, MAXDOC, 2).astype(jnp.int32),
        "span_order": jax.random.permutation(splits[6], SPANS).astype(jnp.int32),
    }


def token_tables(span_order, doc_lengths, span):
    offsets = jnp.arange(span, dtype=jnp.int32)
    positions = (span_order[:, None] * span + offsets[None, :]).reshape(-1).astype(jnp.int32)
    starts = jnp.cumsum(doc_lengths) - doc_lengths
    documents = lax.optimization_barrier(jnp.sum((positions[:, None] >= starts[None, :]).astype(jnp.int32), axis=1))
    return (positions, documents)

def reference(queries, keys, values, out_grad, gate_logits, doc_lengths, span_order):
    scale = 1.0 / math.sqrt(HD)
    group = ASKER_GROUP_SHARE // KV_HEADS
    block = min(1024, STREAM_ELEMENTS)
    positions, documents = token_tables(span_order, doc_lengths, SPAN)
    log_forget = jax.nn.log_sigmoid(gate_logits.astype(jnp.float32))
    logical = jnp.zeros_like(log_forget).at[positions].set(log_forget)
    decay_sum = jnp.take(jnp.cumsum(logical, axis=0), positions, axis=0)
    query_heads = queries.reshape(STREAM_ELEMENTS, ASKER_GROUP_SHARE, HD).transpose(1, 0, 2)
    grad_heads = out_grad.reshape(STREAM_ELEMENTS, ASKER_GROUP_SHARE, HD).transpose(1, 0, 2)
    key_heads = keys.reshape(STREAM_ELEMENTS, KV_HEADS, HD).transpose(1, 0, 2)
    value_heads = values.reshape(STREAM_ELEMENTS, KV_HEADS, HD).transpose(1, 0, 2)
    starts = jnp.arange(STREAM_ELEMENTS // block, dtype=jnp.int32) * block

    def one_head(head):
        query = query_heads[head]
        grad = grad_heads[head]
        key = key_heads[head // group]
        value = value_heads[head // group]
        decay = decay_sum[:, head]
        key_wide = key.astype(jnp.float32)

        def block_step(carry, begin):
            key_grad, value_grad, column = carry
            query_block = lax.dynamic_slice_in_dim(query, begin, block, 0)
            grad_block = lax.dynamic_slice_in_dim(grad, begin, block, 0)
            decay_block = lax.dynamic_slice_in_dim(decay, begin, block, 0)
            pos_block = lax.dynamic_slice_in_dim(positions, begin, block, 0)
            doc_block = lax.dynamic_slice_in_dim(documents, begin, block, 0)
            live = (positions[None, :] <= pos_block[:, None]) & (documents[None, :] == doc_block[:, None])
            scores = jnp.dot(query_block, key.T, preferred_element_type=jnp.float32) * scale
            scores = scores + decay_block[:, None] - decay[None, :]
            scores = jnp.where(live, scores, -jnp.inf)
            highest = lax.optimization_barrier(jnp.max(scores, axis=1))
            weights = jnp.where(live, jnp.exp(scores - highest[:, None]), 0.0)
            lse = highest + jnp.log(lax.optimization_barrier(jnp.sum(weights, axis=1)))
            probs = jnp.where(live, jnp.exp(scores - lse[:, None]), 0.0)
            slopes = jnp.dot(grad_block, value.T, preferred_element_type=jnp.float32)
            delta = lax.optimization_barrier(jnp.sum(probs * slopes, axis=1))
            dscores = probs * (slopes - delta[:, None])
            query_grad = jnp.dot(dscores, key_wide, precision=lax.Precision.HIGHEST) * scale
            probs_low = probs.astype(jnp.bfloat16)
            dscores_low = dscores.astype(jnp.bfloat16)
            value_grad = value_grad + jnp.dot(probs_low.T, grad_block, preferred_element_type=jnp.float32)
            key_grad = key_grad + jnp.dot(dscores_low.T, query_block, preferred_element_type=jnp.float32)
            column = column + lax.optimization_barrier(jnp.sum(dscores, axis=0))
            return ((key_grad, value_grad, column), query_grad)
        init = (jnp.zeros((STREAM_ELEMENTS, HD), jnp.float32), jnp.zeros((STREAM_ELEMENTS, HD), jnp.float32), jnp.zeros((STREAM_ELEMENTS,), jnp.float32))
        (key_grad, value_grad, column), query_grad = lax.scan(block_step, init, starts)
        return (query_grad.reshape(STREAM_ELEMENTS, HD), key_grad, value_grad, column)
    query_grad, key_grad, value_grad, column = lax.map(one_head, jnp.arange(ASKER_GROUP_SHARE, dtype=jnp.int32))
    query_out = query_grad.transpose(1, 0, 2).reshape(STREAM_ELEMENTS, ASKER_GROUP_SHARE * HD).astype(jnp.bfloat16)
    key_sum = lax.optimization_barrier(jnp.sum(key_grad.reshape(KV_HEADS, group, STREAM_ELEMENTS, HD), axis=1)) * scale
    value_sum = lax.optimization_barrier(jnp.sum(value_grad.reshape(KV_HEADS, group, STREAM_ELEMENTS, HD), axis=1))
    key_out = key_sum.transpose(1, 0, 2).reshape(STREAM_ELEMENTS, KV_HEADS * HD).astype(jnp.bfloat16)
    value_out = value_sum.transpose(1, 0, 2).reshape(STREAM_ELEMENTS, KV_HEADS * HD).astype(jnp.bfloat16)
    decay_grad = -column.T
    logical_grad = jnp.zeros_like(decay_grad).at[positions].set(decay_grad)
    suffix = jnp.flip(jnp.cumsum(jnp.flip(logical_grad, 0), axis=0), 0)
    forget_grad = jnp.take(suffix, positions, axis=0)
    return (query_out, key_out, value_out, forget_grad)
```

```python
import functools
import math

import jax
import jax.numpy as jnp
from jax import lax
from jax.experimental import pallas as pl
from jax.experimental.pallas import tpu as pltpu
from jax.sharding import Mesh, PartitionSpec as P

NZ, NX, NC, NY = 8, 4, 2, 4
ROWS, SPAN, HEADS, HD = 128, 64, 4, 128
DOCS = 16
BLOCKS = NC * NZ
QSPANS = 2 * NX
LANES = HEADS * SPAN
EXTRA = 32
PAIRS = 136
STREAM = 8192
UNROLL = 2
NEG = -1e30
SCALE = 1.0 / math.sqrt(HD)
f32, bf16, i32 = jnp.float32, jnp.bfloat16, jnp.int32
VMEM_LIMIT = 48 * 1024 * 1024
NT = (((1,), (1,)), ((), ()))
TN = (((0,), (0,)), ((), ()))


def three_terms(a):
    high = a.astype(bf16).astype(f32)
    rest = a - high
    middle = rest.astype(bf16).astype(f32)
    return high, middle, rest - middle


def iota(shape, dim):
    return lax.broadcasted_iota(i32, shape, dim)


def same_span_upto(n):
    row, column = iota((n, n), 0), iota((n, n), 1)
    return jnp.where((row <= column) & (row // SPAN == column // SPAN), 1.0, 0.0).astype(f32)


def send_keys_kernel(log_ref, keys_ref, values_ref, out_ref):
    parts = []
    for x in range(NX):
        total = log_ref[x * NY]
        for y in range(1, NY):
            total = total + pltpu.roll(log_ref[x * NY + y], 32 * y, 1)
        parts.append(total)
    logs = jnp.concatenate(
        [parts[0] + pltpu.roll(parts[1], HEADS, 0), parts[2] + pltpu.roll(parts[3], HEADS, 0)], axis=0
    )
    sums = jnp.dot(logs, same_span_upto(ROWS), precision=lax.Precision.HIGHEST, preferred_element_type=f32)
    high, middle, low = three_terms(sums)
    extra = jnp.concatenate(
        [jnp.concatenate([high, middle], axis=1), jnp.concatenate([low, jnp.zeros_like(low)], axis=1)], axis=0
    ).astype(bf16)
    keys, values = keys_ref[...], values_ref[...]
    for i in range(NZ):
        out_ref[i, 0:ROWS, 0:HD] = keys
        out_ref[i, 0:ROWS, HD : 2 * HD] = values
        out_ref[i, ROWS : ROWS + EXTRA, :] = extra


def gather_queries(refs, queries_s, grads_s):
    for k, ref in enumerate(refs):
        for half in range(2):
            rows = slice(half * SPAN, (half + 1) * SPAN)
            for h in range(HEADS):
                to = slice(h * SPAN, (h + 1) * SPAN)
                queries_s[2 * k + half, to, :] = ref[rows, h * HD : (h + 1) * HD]
                grads_s[2 * k + half, to, :] = ref[rows, (HEADS + h) * HD : (HEADS + h + 1) * HD]


def shared_span(x, q):
    return 2 * ((x + NX - q // 2) % NX) + q % 2


def gather_keys(own_ref, peer_ref, kv, c):
    for i in range(NZ):
        kv[c * NZ + i] = own_ref[i, 0:ROWS, :]
        kv[(1 - c) * NZ + i] = peer_ref[i, 0:ROWS, :]


def spans_of_block(order_ref, x, block):
    first = ((block % NZ) * (NX * NC) + x * NC + block // NZ) * 2
    return order_ref[first], order_ref[first + 1]


def span_of_query(order_ref, z, x, c, q):
    return order_ref[((z * NX + (x + NX - q // 2) % NX) * NC + c) * 2 + q % 2]


def block_scores(order_ref, pairs_ref, found, t, x, kv, queries_s, grads_s, bias_ref, code_ref, qdecay_ref, qpos_ref, qdoc_ref):
    pair = pairs_ref[t]
    qspan, block = pair // BLOCKS, pair % BLOCKS
    keys, values = kv[block, :, 0:HD], kv[block, :, HD : 2 * HD]
    queries, grads = queries_s[qspan], grads_s[qspan]
    pick = jnp.where(code_ref[...] == block, 1.0, 0.0).astype(bf16)
    key_decay = jnp.dot(bias_ref[...], pick, preferred_element_type=f32)
    scores = lax.dot_general(keys, queries, NT, preferred_element_type=f32)
    slopes = lax.dot_general(values, grads, NT, preferred_element_type=f32)
    even, odd = spans_of_block(order_ref, x, block)
    even = jnp.where(t < found, even, 2 * STREAM)
    odd = jnp.where(t < found, odd, 2 * STREAM)
    row = iota((ROWS, HD), 0)
    key_pos = row + jnp.where(row < SPAN, even * SPAN, odd * SPAN - SPAN)
    at = pl.ds(qspan, 1)
    live = (key_pos <= qpos_ref[at, :][:, 0:HD]) & (key_pos >= qdoc_ref[at, :][:, 0:HD])
    scores = scores * SCALE + (qdecay_ref[at, :] - key_decay)
    scores = jnp.where(jnp.concatenate([live, live], axis=1), scores, NEG)
    return qspan, block, keys, queries, grads, scores, slopes


def plan_kernel(order_ref, length_ref, column_ref, line_ref, earlier_ref, select_ref, code_ref, qpos_ref, qdoc_ref, pairs_ref):
    z, x, c = lax.axis_index("z"), lax.axis_index("x"), lax.axis_index("core")
    count = BLOCKS * NX * HEADS
    target = jnp.concatenate([column_ref[:, 0:1], column_ref[:, 1:2]], axis=0)
    source = jnp.concatenate([line_ref[0:1, :], line_ref[1:2, :]], axis=1)
    square = (2 * count, 2 * count)
    earlier = (source < target) & (iota(square, 0) % HEADS == iota(square, 1) % HEADS)
    earlier_ref[...] = jnp.where(earlier, 1.0, 0.0).astype(bf16)
    row, column = iota((3 * count, 2 * HD), 0), iota((3 * count, 2 * HD), 1)
    wanted = (column // 64) * count + ((column % 64) // HEADS) * (NX * HEADS) + x * HEADS + column % HEADS
    select_ref[...] = jnp.where((row == wanted) & (column < 192), 1.0, 0.0).astype(bf16)
    row, column = iota((LANES, LANES), 0), iota((LANES, LANES), 1)
    use = (row < 3 * BLOCKS * HEADS) & (row % HEADS == column // SPAN)
    code_ref[...] = jnp.where(use, (row % (BLOCKS * HEADS)) // HEADS, -1)
    row, column = iota((QSPANS, LANES), 0), iota((QSPANS, LANES), 1)
    qpos = column % SPAN
    spans = []
    for q in range(QSPANS):
        spans.append(span_of_query(order_ref, z, x, c, q))
        qpos = qpos + jnp.where(row == q, spans[q] * SPAN, 0)
    starts = [jnp.int32(0)]
    for doc in range(DOCS - 1):
        starts.append(starts[-1] + length_ref[doc])
    qdoc = jnp.zeros((QSPANS, LANES), i32)
    for start in starts:
        qdoc = jnp.where(qpos >= start, start, qdoc)
    qpos_ref[...] = qpos
    qdoc_ref[...] = qdoc
    found = jnp.int32(0)
    for q in range(QSPANS):
        mine, begin = spans[q], jnp.int32(0)
        for start in starts:
            begin = jnp.where(mine * SPAN >= start, start, begin)

        def scan(block, found, q=q, mine=mine, begin=begin):
            even, odd = spans_of_block(order_ref, x, block)
            live = ((even <= mine) & (even * SPAN + SPAN > begin)) | ((odd <= mine) & (odd * SPAN + SPAN > begin))
            pairs_ref[found] = q * BLOCKS + block
            return found + live.astype(i32)

        found = lax.fori_loop(0, BLOCKS, scan, found, unroll=8)
    pairs_ref[found] = 0
    pairs_ref[PAIRS - 1] = found


def stats_kernel(
    order_ref, pairs_ref, earlier_ref, select_ref, code_ref, qpos_ref, qdoc_ref, own_ref, peer_ref, qd0, qd1, qd2, qd3,
    stats_ref, bias_ref, qdecay_ref,
    kv, queries_s, grads_s, decay, high_s, mass_s, cross_s,
):
    z, x, c = lax.axis_index("z"), lax.axis_index("x"), lax.axis_index("core")
    gather_queries((qd0, qd1, qd2, qd3), queries_s, grads_s)
    gather_keys(own_ref, peer_ref, kv, c)
    for i in range(NZ):
        for ref, core in ((own_ref, c), (peer_ref, 1 - c)):
            terms = ref[i, ROWS : ROWS + EXTRA, :].astype(f32)
            decay[core * NZ + i] = terms[0:16, 0:HD] + terms[0:16, HD : 2 * HD] + terms[16:32, 0:HD]
    count = BLOCKS * NX * HEADS
    sums = decay[...].reshape(count, ROWS)
    totals = jnp.concatenate([sums[:, SPAN - 1 : SPAN], sums[:, ROWS - 1 : ROWS]], axis=0)
    t_high, t_middle, t_low = three_terms(totals)
    lane = iota((2 * count, HD), 1)
    zero = jnp.zeros((2 * count, HD), f32)
    t_terms = jnp.where(
        lane == 0, t_high, jnp.where(lane == 1, t_middle, jnp.where(lane == 2, t_low, zero))
    ).astype(bf16)
    before = jnp.dot(earlier_ref[...], t_terms, preferred_element_type=f32)
    before = before[:, 0:1] + before[:, 1:2] + before[:, 2:3]
    sums = sums + jnp.where(iota((count, ROWS), 1) < SPAN, before[0:count], before[count : 2 * count])
    decay[...] = sums.reshape(BLOCKS, NX * HEADS, ROWS)
    terms = jnp.concatenate(three_terms(sums), axis=0).astype(bf16)
    bias_ref[...] = lax.dot_general(terms, select_ref[...], TN, preferred_element_type=f32).astype(bf16)
    mine = c * NZ + z
    for k in range(NX):
        own = decay[mine, pl.ds(((x + NX - k) % NX) * HEADS, HEADS), :]
        for half in range(2):
            for h in range(HEADS):
                qdecay_ref[2 * k + half : 2 * k + half + 1, h * SPAN : (h + 1) * SPAN] = own[
                    h : h + 1, half * SPAN : (half + 1) * SPAN
                ]
    high_s[...] = jnp.full((QSPANS, LANES), NEG, f32)
    mass_s[...] = jnp.zeros((QSPANS, LANES), f32)
    cross_s[...] = jnp.zeros((QSPANS, LANES), f32)
    found = pairs_ref[PAIRS - 1]

    def step(t, carry):
        parts = []
        for u in range(UNROLL):
            qspan, _, _, _, _, scores, slopes = block_scores(
                order_ref, pairs_ref, found, UNROLL * t + u, x, kv, queries_s, grads_s, bias_ref, code_ref,
                qdecay_ref, qpos_ref, qdoc_ref,
            )
            high = jnp.max(scores, axis=0, keepdims=True)
            weights = jnp.exp(scores - high)
            mass = jnp.sum(weights, axis=0, keepdims=True)
            parts.append((qspan, high, mass, jnp.sum(weights * slopes, axis=0, keepdims=True)))
        for qspan, high, mass, cross in parts:
            at = pl.ds(shared_span(x, qspan), 1)
            old = high_s[at, :]
            new = jnp.maximum(old, high)
            before, now = jnp.exp(old - new), jnp.exp(high - new)
            high_s[at, :] = new
            mass_s[at, :] = mass_s[at, :] * before + mass * now
            cross_s[at, :] = cross_s[at, :] * before + cross * now
        return carry

    lax.fori_loop(0, (found + UNROLL - 1) // UNROLL, step, 0)
    for i in range(NX):
        stats_ref[i, 0:8, :] = high_s[...]
        stats_ref[i, 8:16, :] = mass_s[...]
        stats_ref[i, 16:24, :] = cross_s[...]


def grads_kernel(
    order_ref, pairs_ref, stats_ref, bias_ref, qdecay_ref, code_ref, qpos_ref, qdoc_ref, own_ref, peer_ref, qd0, qd1, qd2, qd3,
    dq_ref, own_out, peer_out, own_col, peer_col,
    kv, queries_s, grads_s, lse_s, delta_s, acc, dqt, col,
):
    x, c = lax.axis_index("x"), lax.axis_index("core")
    gather_queries((qd0, qd1, qd2, qd3), queries_s, grads_s)
    gather_keys(own_ref, peer_ref, kv, c)
    high = stats_ref[0, 0:8, :]
    for i in range(1, NX):
        high = jnp.maximum(high, stats_ref[i, 0:8, :])
    mass, cross = jnp.zeros_like(high), jnp.zeros_like(high)
    for i in range(NX):
        factor = jnp.exp(stats_ref[i, 0:8, :] - high)
        mass = mass + stats_ref[i, 8:16, :] * factor
        cross = cross + stats_ref[i, 16:24, :] * factor
    lse_s[...] = high + jnp.log(mass)
    delta_s[...] = cross / mass
    acc[...] = jnp.zeros_like(acc)
    dqt[...] = jnp.zeros_like(dqt)
    col[...] = jnp.zeros_like(col)
    found = pairs_ref[PAIRS - 1]

    def step(t, carry):
        parts = []
        for u in range(UNROLL):
            qspan, block, keys, queries, grads, scores, slopes = block_scores(
                order_ref, pairs_ref, found, UNROLL * t + u, x, kv, queries_s, grads_s, bias_ref, code_ref,
                qdecay_ref, qpos_ref, qdoc_ref,
            )
            at = pl.ds(shared_span(x, qspan), 1)
            probs = jnp.exp(scores - lse_s[at, :])
            dscores = probs * (slopes - delta_s[at, :])
            upper = dscores.astype(bf16)
            lower = (dscores - upper.astype(f32)).astype(bf16)
            heads = iota((LANES, HD), 0) // SPAN + block * HEADS
            pick = jnp.where(iota((LANES, HD), 1) == heads, 1.0, 0.0).astype(bf16)
            both = jnp.dot(upper, jnp.concatenate([queries, pick], axis=1), preferred_element_type=f32)
            dv = jnp.dot(probs.astype(bf16), grads, preferred_element_type=f32)
            column = both[:, HD : 2 * HD] + jnp.dot(lower, pick, preferred_element_type=f32)
            dq = lax.dot_general(keys, upper, TN, preferred_element_type=f32) + lax.dot_general(
                keys, lower, TN, preferred_element_type=f32
            )
            parts.append((qspan, block, both[:, 0:HD], dv, column, dq))
        for qspan, block, dk, dv, column, dq in parts:
            acc[block, :, 0:HD] += dk
            acc[block, :, HD : 2 * HD] += dv
            col[...] += column
            dqt[qspan] += dq
        return carry

    lax.fori_loop(0, (found + UNROLL - 1) // UNROLL, step, 0)
    for q in range(QSPANS):
        whole = dqt[q].T
        begin = (q % 2) * SPAN
        for h in range(HEADS):
            dq_ref[(x + NX - q // 2) % NX, begin : begin + SPAN, h * HD : (h + 1) * HD] = whole[
                h * SPAN : (h + 1) * SPAN
            ].astype(bf16)
    columns = col[...]
    even = three_terms(jnp.sum(columns[0:SPAN], axis=0, keepdims=True))
    odd = three_terms(jnp.sum(columns[SPAN:ROWS], axis=0, keepdims=True))
    row = iota((16, HD), 0)
    rows = jnp.zeros((16, HD), f32)
    for k in range(3):
        rows = jnp.where(row == 2 * k, even[k], jnp.where(row == 2 * k + 1, odd[k], rows))
    rows = rows.astype(bf16)
    for i in range(NX):
        dq_ref[i, ROWS : ROWS + 16, 0:HD] = rows
        dq_ref[i, ROWS : ROWS + 16, HD : 4 * HD] = jnp.zeros((16, 3 * HD), bf16)
    col[...] = columns.T
    half = NZ * HEADS
    own_col[...] = col[pl.ds(pl.multiple_of(c * half, half), half), :]
    peer_col[...] = col[pl.ds(pl.multiple_of((1 - c) * half, half), half), :]
    for i in range(NZ):
        own_out[i] = acc[c * NZ + i]
        peer_out[i] = acc[(1 - c) * NZ + i]


def send_grads_kernel(own_ref, peer_ref, own_col, peer_col, dq_ref, total_ref, query_ref, out_ref):
    query = dq_ref[0, 0:ROWS, :].astype(f32)
    for i in range(1, NX):
        query = query + dq_ref[i, 0:ROWS, :].astype(f32)
    query_ref[...] = (query * SCALE).astype(bf16)
    row = iota((QSPANS, HD), 0)
    totals = jnp.zeros((QSPANS, HD), f32)
    for i in range(NX):
        mine = dq_ref[i, ROWS : ROWS + 16, 0:HD].astype(f32)
        other = total_ref[i].astype(f32)
        for h in range(2):
            a = mine[h : h + 1] + mine[h + 2 : h + 3] + mine[h + 4 : h + 5]
            b = other[h : h + 1] + other[h + 2 : h + 3] + other[h + 4 : h + 5]
            totals = jnp.where(row == 2 * i + h, a + b, totals)
    t_terms = three_terms(totals)
    columns = own_col[...] + peer_col[...]
    zero = jnp.zeros((8, HD), f32)
    right = jnp.concatenate([*t_terms, zero], axis=0)
    for i in range(NZ):
        out_ref[i, 0:ROWS, :] = (own_ref[i] + peer_ref[i]).astype(bf16)
        group = columns[8 * (i // 2) : 8 * (i // 2) + 8]
        if i % 2:
            group = pltpu.roll(group, HEADS, 0)
        left = jnp.concatenate([*three_terms(group), zero], axis=0)
        out_ref[i, ROWS : ROWS + EXTRA, :] = jnp.concatenate([left, right], axis=1).astype(bf16)


def finish_kernel(order_ref, span_ref, in_ref, key_ref, value_ref, forget_ref):
    first = ((lax.axis_index("z") * NX + lax.axis_index("x")) * NC + lax.axis_index("core")) * 2
    total = in_ref[0].astype(f32)
    for i in range(1, NZ):
        total = total + in_ref[i].astype(f32)
    key_ref[...] = (total[0:ROWS, 0:HD] * SCALE).astype(bf16)
    value_ref[...] = total[0:ROWS, HD : 2 * HD].astype(bf16)
    extra = total[ROWS : ROWS + EXTRA]
    extra = extra[0:8] + extra[8:16] + extra[16:24]
    columns, totals = extra[:, 0:HD], extra[:, HD : 2 * HD]
    after = []
    for h in range(2):
        later = span_ref[...] > order_ref[first + h]
        line = jnp.sum(jnp.where(later, totals, 0.0), axis=0, keepdims=True)
        line = jnp.broadcast_to(line, (8, HD))
        for shift in (4, 8, 16, 32):
            line = line + pltpu.roll(line, shift, 1)
        after.append(pltpu.roll(line, HD - 60, 1)[0:1])
    within = lax.dot_general(
        same_span_upto(ROWS), columns, NT, precision=lax.Precision.HIGHEST, preferred_element_type=f32
    )
    row = iota((ROWS, HEADS), 0)
    rest = jnp.where(row < SPAN, after[0][:, 0:HEADS], after[1][:, 0:HEADS])
    forget_ref[...] = -(within[:, 0:HEADS] + rest)


def call(kernel, specs, outs, scratch, flops, *args):
    smem, vmem = pl.BlockSpec(memory_space=pltpu.SMEM), pl.BlockSpec(memory_space=pltpu.VMEM)
    place = {"s": smem, "v": vmem}
    return pl.pallas_call(
        kernel,
        in_specs=[place[k] for k in specs],
        out_specs=[place[k] for k, _, _ in outs],
        out_shape=[jax.ShapeDtypeStruct(shape, dtype) for _, shape, dtype in outs],
        scratch_shapes=[pltpu.VMEM(shape, dtype) for shape, dtype in scratch],
        compiler_params=pltpu.CompilerParams(vmem_limit_bytes=VMEM_LIMIT),
        cost_estimate=pl.CostEstimate(flops=flops, bytes_accessed=4 << 20, transcendentals=0),
    )(*args)


def body(queries, keys, values, out_grad, gate_logits, doc_lengths, span_order):
    swap = [(0, 1), (1, 0)]
    pair_rows = jnp.concatenate([queries, out_grad], axis=1)
    query_rows = [pair_rows]
    for k in range(1, NX):
        query_rows.append(lax.ppermute(pair_rows, "x", [(i, (i + k) % NX) for i in range(NX)]))

    gates, _ = lax.optimization_barrier((gate_logits, pair_rows))
    log_forget = jax.nn.log_sigmoid(gates).T.reshape(NY, HEADS, 32)
    log_forget = jnp.pad(log_forget, ((0, 0), (0, 8 - HEADS), (0, HD - 32)))
    log_forget = jnp.broadcast_to(log_forget[None], (NX, NY, 8, HD)).reshape(NX * NY, 8, HD)
    logs = lax.all_to_all(log_forget, ("x", "head"), 0, 0)
    order4 = span_order.reshape(NZ, NX, NC, 2)
    by_head = jnp.broadcast_to(order4.transpose(3, 2, 0, 1)[..., None], (2, NC, NZ, NX, HEADS))
    order_line = by_head.reshape(2, NC * NZ * NX * HEADS)
    order_column = order_line.T
    order_spans = by_head.transpose(3, 0, 1, 2, 4).reshape(QSPANS, NC * NZ * HEADS)
    order_spans = jnp.pad(order_spans, ((0, 0), (0, HD - NC * NZ * HEADS)), constant_values=-1)

    earlier, select, code, qpos, qdoc, pairs = call(
        plan_kernel,
        "ssvv",
        [
            ("v", (2 * BLOCKS * NX * HEADS, 2 * BLOCKS * NX * HEADS), bf16),
            ("v", (3 * BLOCKS * NX * HEADS, 2 * HD), bf16),
            ("v", (LANES, LANES), i32),
            ("v", (QSPANS, LANES), i32),
            ("v", (QSPANS, LANES), i32),
            ("s", (PAIRS,), i32),
        ],
        [],
        1 << 28,
        span_order, doc_lengths, order_column, order_line,
    )
    message = (NZ, ROWS + EXTRA, 2 * HD)
    keys, values, query_rows, pairs = lax.optimization_barrier((keys, values, query_rows, pairs))
    (key_message,) = call(send_keys_kernel, "vvv", [("v", message, bf16)], [], 0, logs, keys, values)
    own = lax.all_to_all(key_message, "z", 0, 0)
    peer = lax.ppermute(own, "core", swap)

    kv = ((BLOCKS, ROWS, 2 * HD), bf16)
    rows = ((QSPANS, LANES, HD), bf16)
    line = ((QSPANS, LANES), f32)
    stats, bias, qdecay = call(
        stats_kernel,
        "ssvvvvvvvvvvv",
        [("v", (NX, 24, LANES), f32), ("v", (ROWS, 2 * HD), bf16), ("v", (QSPANS, LANES), f32)],
        [kv, rows, rows, ((BLOCKS, NX * HEADS, ROWS), f32), line, line, line],
        1 << 28,
        span_order, pairs, earlier, select, code, qpos, qdoc, own, peer, *query_rows,
    )
    all_stats = lax.all_to_all(stats, "x", 0, 0)
    dq, own_sum, peer_sum, own_col, peer_col = call(
        grads_kernel,
        "ssvvvvvvvvvvvv",
        [
            ("v", (NX, ROWS + 16, HEADS * HD), bf16),
            ("v", (NZ, ROWS, 2 * HD), f32),
            ("v", (NZ, ROWS, 2 * HD), f32),
            ("v", (NZ * HEADS, ROWS), f32),
            ("v", (NZ * HEADS, ROWS), f32),
        ],
        [kv, rows, rows, line, line, ((BLOCKS, ROWS, 2 * HD), f32), ((QSPANS, HD, LANES), f32), ((ROWS, ROWS), f32)],
        1 << 29,
        span_order, pairs, all_stats, bias, qdecay, code, qpos, qdoc, own, peer, *query_rows,
    )
    peer_sum = lax.ppermute(peer_sum, "core", swap)
    peer_col = lax.ppermute(peer_col, "core", swap)
    dq = lax.all_to_all(dq, "x", 0, 0)
    totals = lax.ppermute(dq[:, ROWS : ROWS + 16, 0:HD], "core", swap)
    query_grad, grad_message = call(
        send_grads_kernel,
        "vvvvvv",
        [("v", (ROWS, HEADS * HD), bf16), ("v", message, bf16)],
        [],
        0,
        own_sum, peer_sum, own_col, peer_col, dq, totals,
    )
    back = lax.all_to_all(grad_message, "z", 0, 0)
    key_grad, value_grad, forget_grad = call(
        finish_kernel,
        "svv",
        [("v", (ROWS, HD), bf16), ("v", (ROWS, HD), bf16), ("v", (ROWS, HEADS), f32)],
        [],
        0,
        span_order, order_spans, back,
    )
    return query_grad, key_grad, value_grad, forget_grad


def solution(mesh):
    fine = Mesh(mesh.devices.reshape(NZ, NX, NC, NY), ("z", "x", "core", "head"))
    ctx = ("z", "x", "core")
    rows = P(ctx, "head")
    return jax.shard_map(
        body,
        mesh=fine,
        in_specs=(rows, rows, rows, rows, P((*ctx, "head"), None), P(), P()),
        out_specs=(rows, rows, rows, rows),
        check_vma=False,
    )
```

```python
import functools
import math

import jax
import jax.numpy as jnp
from jax import lax
from jax.experimental import pallas as pl
from jax.experimental.pallas import tpu as pltpu
from jax.sharding import Mesh, PartitionSpec as P

NZ, NX, NC, NY = 8, 4, 2, 4
ROWS, SPAN, HEADS, HD = 128, 64, 4, 128
DOCS = 16
BLOCKS = NC * NZ
QSPANS = 2 * NX
LANES = HEADS * SPAN
EXTRA = 32
PAIRS = 136
STREAM = 8192
UNROLL = 2
NEG = -1e30
SCALE = 1.0 / math.sqrt(HD)
f32, bf16, i32 = jnp.float32, jnp.bfloat16, jnp.int32
VMEM_LIMIT = 48 * 1024 * 1024
NT = (((1,), (1,)), ((), ()))
TN = (((0,), (0,)), ((), ()))


def three_terms(a):
    high = a.astype(bf16).astype(f32)
    rest = a - high
    middle = rest.astype(bf16).astype(f32)
    return high, middle, rest - middle


def iota(shape, dim):
    return lax.broadcasted_iota(i32, shape, dim)


def same_span_upto(n):
    row, column = iota((n, n), 0), iota((n, n), 1)
    return jnp.where((row <= column) & (row // SPAN == column // SPAN), 1.0, 0.0).astype(f32)


def send_keys_kernel(log_ref, keys_ref, values_ref, out_ref):
    parts = []
    for x in range(NX):
        total = log_ref[x * NY]
        for y in range(1, NY):
            total = total + pltpu.roll(log_ref[x * NY + y], 32 * y, 1)
        parts.append(total)
    logs = jnp.concatenate(
        [parts[0] + pltpu.roll(parts[1], HEADS, 0), parts[2] + pltpu.roll(parts[3], HEADS, 0)], axis=0
    )
    sums = jnp.dot(logs, same_span_upto(ROWS), precision=lax.Precision.HIGHEST, preferred_element_type=f32)
    high, middle, low = three_terms(sums)
    extra = jnp.concatenate(
        [jnp.concatenate([high, middle], axis=1), jnp.concatenate([low, jnp.zeros_like(low)], axis=1)], axis=0
    ).astype(bf16)
    keys, values = keys_ref[...], values_ref[...]
    for i in range(NZ):
        out_ref[i, 0:ROWS, 0:HD] = keys
        out_ref[i, 0:ROWS, HD : 2 * HD] = values
        out_ref[i, ROWS : ROWS + EXTRA, :] = extra


def gather_queries(refs, queries_s, grads_s):
    for k, ref in enumerate(refs):
        for half in range(2):
            rows = slice(half * SPAN, (half + 1) * SPAN)
            for h in range(HEADS):
                to = slice(h * SPAN, (h + 1) * SPAN)
                queries_s[2 * k + half, to, :] = ref[rows, h * HD : (h + 1) * HD]
                grads_s[2 * k + half, to, :] = ref[rows, (HEADS + h) * HD : (HEADS + h + 1) * HD]


def shared_span(x, q):
    return 2 * ((x + NX - q // 2) % NX) + q % 2


def gather_keys(own_ref, peer_ref, kv, c):
    for i in range(NZ):
        kv[c * NZ + i] = own_ref[i, 0:ROWS, :]
        kv[(1 - c) * NZ + i] = peer_ref[i, 0:ROWS, :]


def spans_of_block(order_ref, x, block):
    first = ((block % NZ) * (NX * NC) + x * NC + block // NZ) * 2
    return order_ref[first], order_ref[first + 1]


def span_of_query(order_ref, z, x, c, q):
    return order_ref[((z * NX + (x + NX - q // 2) % NX) * NC + c) * 2 + q % 2]


def block_scores(order_ref, pairs_ref, found, t, x, kv, queries_s, grads_s, bias_ref, code_ref, qdecay_ref, qpos_ref, qdoc_ref):
    pair = pairs_ref[t]
    qspan, block = pair // BLOCKS, pair % BLOCKS
    keys, values = kv[block, :, 0:HD], kv[block, :, HD : 2 * HD]
    queries, grads = queries_s[qspan], grads_s[qspan]
    pick = jnp.where(code_ref[...] == block, 1.0, 0.0).astype(bf16)
    key_decay = jnp.dot(bias_ref[...], pick, preferred_element_type=f32)
    scores = lax.dot_general(keys, queries, NT, preferred_element_type=f32)
    slopes = lax.dot_general(values, grads, NT, preferred_element_type=f32)
    even, odd = spans_of_block(order_ref, x, block)
    even = jnp.where(t < found, even, 2 * STREAM)
    odd = jnp.where(t < found, odd, 2 * STREAM)
    row = iota((ROWS, HD), 0)
    key_pos = row + jnp.where(row < SPAN, even * SPAN, odd * SPAN - SPAN)
    at = pl.ds(qspan, 1)
    live = (key_pos <= qpos_ref[at, :][:, 0:HD]) & (key_pos >= qdoc_ref[at, :][:, 0:HD])
    scores = scores * SCALE + (qdecay_ref[at, :] - key_decay)
    scores = jnp.where(jnp.concatenate([live, live], axis=1), scores, NEG)
    return qspan, block, keys, queries, grads, scores, slopes


def plan_kernel(order_ref, length_ref, column_ref, line_ref, earlier_ref, select_ref, code_ref, qpos_ref, qdoc_ref, pairs_ref):
    z, x, c = lax.axis_index("z"), lax.axis_index("x"), lax.axis_index("core")
    count = BLOCKS * NX * HEADS
    target = jnp.concatenate([column_ref[:, 0:1], column_ref[:, 1:2]], axis=0)
    source = jnp.concatenate([line_ref[0:1, :], line_ref[1:2, :]], axis=1)
    square = (2 * count, 2 * count)
    earlier = (source < target) & (iota(square, 0) % HEADS == iota(square, 1) % HEADS)
    earlier_ref[...] = jnp.where(earlier, 1.0, 0.0).astype(bf16)
    row, column = iota((3 * count, 2 * HD), 0), iota((3 * count, 2 * HD), 1)
    wanted = (column // 64) * count + ((column % 64) // HEADS) * (NX * HEADS) + x * HEADS + column % HEADS
    select_ref[...] = jnp.where((row == wanted) & (column < 192), 1.0, 0.0).astype(bf16)
    row, column = iota((LANES, LANES), 0), iota((LANES, LANES), 1)
    use = (row < 3 * BLOCKS * HEADS) & (row % HEADS == column // SPAN)
    code_ref[...] = jnp.where(use, (row % (BLOCKS * HEADS)) // HEADS, -1)
    row, column = iota((QSPANS, LANES), 0), iota((QSPANS, LANES), 1)
    qpos = column % SPAN
    spans = []
    for q in range(QSPANS):
        spans.append(span_of_query(order_ref, z, x, c, q))
        qpos = qpos + jnp.where(row == q, spans[q] * SPAN, 0)
    starts = [jnp.int32(0)]
    for doc in range(DOCS - 1):
        starts.append(starts[-1] + length_ref[doc])
    qdoc = jnp.zeros((QSPANS, LANES), i32)
    for start in starts:
        qdoc = jnp.where(qpos >= start, start, qdoc)
    qpos_ref[...] = qpos
    qdoc_ref[...] = qdoc
    found = jnp.int32(0)
    for q in range(QSPANS):
        mine, begin = spans[q], jnp.int32(0)
        for start in starts:
            begin = jnp.where(mine * SPAN >= start, start, begin)

        def scan(block, found, q=q, mine=mine, begin=begin):
            even, odd = spans_of_block(order_ref, x, block)
            live = ((even <= mine) & (even * SPAN + SPAN > begin)) | ((odd <= mine) & (odd * SPAN + SPAN > begin))
            pairs_ref[found] = q * BLOCKS + block
            return found + live.astype(i32)

        found = lax.fori_loop(0, BLOCKS, scan, found, unroll=8)
    pairs_ref[found] = 0
    pairs_ref[PAIRS - 1] = found


def stats_kernel(
    order_ref, pairs_ref, earlier_ref, select_ref, code_ref, qpos_ref, qdoc_ref, own_ref, peer_ref, qd0, qd1, qd2, qd3,
    stats_ref, bias_ref, qdecay_ref,
    kv, queries_s, grads_s, decay, high_s, mass_s, cross_s,
):
    z, x, c = lax.axis_index("z"), lax.axis_index("x"), lax.axis_index("core")
    gather_queries((qd0, qd1, qd2, qd3), queries_s, grads_s)
    gather_keys(own_ref, peer_ref, kv, c)
    for i in range(NZ):
        for ref, core in ((own_ref, c), (peer_ref, 1 - c)):
            terms = ref[i, ROWS : ROWS + EXTRA, :].astype(f32)
            decay[core * NZ + i] = terms[0:16, 0:HD] + terms[0:16, HD : 2 * HD] + terms[16:32, 0:HD]
    count = BLOCKS * NX * HEADS
    sums = decay[...].reshape(count, ROWS)
    totals = jnp.concatenate([sums[:, SPAN - 1 : SPAN], sums[:, ROWS - 1 : ROWS]], axis=0)
    t_high, t_middle, t_low = three_terms(totals)
    lane = iota((2 * count, HD), 1)
    zero = jnp.zeros((2 * count, HD), f32)
    t_terms = jnp.where(
        lane == 0, t_high, jnp.where(lane == 1, t_middle, jnp.where(lane == 2, t_low, zero))
    ).astype(bf16)
    before = jnp.dot(earlier_ref[...], t_terms, preferred_element_type=f32)
    before = before[:, 0:1] + before[:, 1:2] + before[:, 2:3]
    sums = sums + jnp.where(iota((count, ROWS), 1) < SPAN, before[0:count], before[count : 2 * count])
    decay[...] = sums.reshape(BLOCKS, NX * HEADS, ROWS)
    terms = jnp.concatenate(three_terms(sums), axis=0).astype(bf16)
    bias_ref[...] = lax.dot_general(terms, select_ref[...], TN, preferred_element_type=f32).astype(bf16)
    mine = c * NZ + z
    for k in range(NX):
        own = decay[mine, pl.ds(((x + NX - k) % NX) * HEADS, HEADS), :]
        for half in range(2):
            for h in range(HEADS):
                qdecay_ref[2 * k + half : 2 * k + half + 1, h * SPAN : (h + 1) * SPAN] = own[
                    h : h + 1, half * SPAN : (half + 1) * SPAN
                ]
    high_s[...] = jnp.full((QSPANS, LANES), NEG, f32)
    mass_s[...] = jnp.zeros((QSPANS, LANES), f32)
    cross_s[...] = jnp.zeros((QSPANS, LANES), f32)
    found = pairs_ref[PAIRS - 1]

    def step(t, carry):
        parts = []
        for u in range(UNROLL):
            qspan, _, _, _, _, scores, slopes = block_scores(
                order_ref, pairs_ref, found, UNROLL * t + u, x, kv, queries_s, grads_s, bias_ref, code_ref,
                qdecay_ref, qpos_ref, qdoc_ref,
            )
            high = jnp.max(scores, axis=0, keepdims=True)
            weights = jnp.exp(scores - high)
            mass = jnp.sum(weights, axis=0, keepdims=True)
            parts.append((qspan, high, mass, jnp.sum(weights * slopes, axis=0, keepdims=True)))
        for qspan, high, mass, cross in parts:
            at = pl.ds(shared_span(x, qspan), 1)
            old = high_s[at, :]
            new = jnp.maximum(old, high)
            before, now = jnp.exp(old - new), jnp.exp(high - new)
            high_s[at, :] = new
            mass_s[at, :] = mass_s[at, :] * before + mass * now
            cross_s[at, :] = cross_s[at, :] * before + cross * now
        return carry

    lax.fori_loop(0, (found + UNROLL - 1) // UNROLL, step, 0)
    for i in range(NX):
        stats_ref[i, 0:8, :] = high_s[...]
        stats_ref[i, 8:16, :] = mass_s[...]
        stats_ref[i, 16:24, :] = cross_s[...]


def grads_kernel(
    order_ref, pairs_ref, stats_ref, bias_ref, qdecay_ref, code_ref, qpos_ref, qdoc_ref, own_ref, peer_ref, qd0, qd1, qd2, qd3,
    dq0, dq1, dq2, dq3, total_out, own_out, peer_out, own_col, peer_col,
    kv, queries_s, grads_s, lse_s, delta_s, acc, dqt, col,
):
    x, c = lax.axis_index("x"), lax.axis_index("core")
    gather_queries((qd0, qd1, qd2, qd3), queries_s, grads_s)
    gather_keys(own_ref, peer_ref, kv, c)
    high = stats_ref[0, 0:8, :]
    for i in range(1, NX):
        high = jnp.maximum(high, stats_ref[i, 0:8, :])
    mass, cross = jnp.zeros_like(high), jnp.zeros_like(high)
    for i in range(NX):
        factor = jnp.exp(stats_ref[i, 0:8, :] - high)
        mass = mass + stats_ref[i, 8:16, :] * factor
        cross = cross + stats_ref[i, 16:24, :] * factor
    lse_s[...] = high + jnp.log(mass)
    delta_s[...] = cross / mass
    acc[...] = jnp.zeros_like(acc)
    dqt[...] = jnp.zeros_like(dqt)
    col[...] = jnp.zeros_like(col)
    found = pairs_ref[PAIRS - 1]

    def step(t, carry):
        parts = []
        for u in range(UNROLL):
            qspan, block, keys, queries, grads, scores, slopes = block_scores(
                order_ref, pairs_ref, found, UNROLL * t + u, x, kv, queries_s, grads_s, bias_ref, code_ref,
                qdecay_ref, qpos_ref, qdoc_ref,
            )
            at = pl.ds(shared_span(x, qspan), 1)
            probs = jnp.exp(scores - lse_s[at, :])
            dscores = probs * (slopes - delta_s[at, :])
            upper = dscores.astype(bf16)
            lower = (dscores - upper.astype(f32)).astype(bf16)
            heads = iota((LANES, HD), 0) // SPAN + block * HEADS
            pick = jnp.where(iota((LANES, HD), 1) == heads, 1.0, 0.0).astype(bf16)
            both = jnp.dot(upper, jnp.concatenate([queries, pick], axis=1), preferred_element_type=f32)
            dv = jnp.dot(probs.astype(bf16), grads, preferred_element_type=f32)
            column = both[:, HD : 2 * HD] + jnp.dot(lower, pick, preferred_element_type=f32)
            dq = lax.dot_general(keys, upper, TN, preferred_element_type=f32) + lax.dot_general(
                keys, lower, TN, preferred_element_type=f32
            )
            parts.append((qspan, block, both[:, 0:HD], dv, column, dq))
        for qspan, block, dk, dv, column, dq in parts:
            acc[block, :, 0:HD] += dk
            acc[block, :, HD : 2 * HD] += dv
            col[...] += column
            dqt[qspan] += dq
        return carry

    lax.fori_loop(0, (found + UNROLL - 1) // UNROLL, step, 0)
    for q in range(QSPANS):
        whole = dqt[q].T
        begin = (q % 2) * SPAN
        for h in range(HEADS):
            (dq0, dq1, dq2, dq3)[q // 2][begin : begin + SPAN, h * HD : (h + 1) * HD] = whole[h * SPAN : (h + 1) * SPAN]
    columns = col[...]
    even = jnp.sum(columns[0:SPAN], axis=0, keepdims=True)
    odd = jnp.sum(columns[SPAN:ROWS], axis=0, keepdims=True)
    row = iota((8, HD), 0)
    total_out[...] = jnp.where(row == 0, even, jnp.where(row == 1, odd, 0.0))
    col[...] = columns.T
    half = NZ * HEADS
    own_col[...] = col[pl.ds(pl.multiple_of(c * half, half), half), :]
    peer_col[...] = col[pl.ds(pl.multiple_of((1 - c) * half, half), half), :]
    for i in range(NZ):
        own_out[i] = acc[c * NZ + i]
        peer_out[i] = acc[(1 - c) * NZ + i]


def send_grads_kernel(own_ref, peer_ref, own_col, peer_col, mine_ref, other_ref, out_ref):
    x = lax.axis_index("x")
    row = iota((QSPANS, HD), 0)
    totals = jnp.zeros((QSPANS, HD), f32)
    for k in range(NX):
        both = mine_ref[8 * k : 8 * k + 8, :] + other_ref[8 * k : 8 * k + 8, :]
        at = 2 * ((x + NX - k) % NX)
        totals = jnp.where(row == at, both[0:1], jnp.where(row == at + 1, both[1:2], totals))
    columns = own_col[...] + peer_col[...]
    zero = jnp.zeros((8, HD), f32)
    right = jnp.concatenate([*three_terms(totals), zero], axis=0)
    for i in range(NZ):
        out_ref[i, 0:ROWS, :] = (own_ref[i] + peer_ref[i]).astype(bf16)
        group = columns[8 * (i // 2) : 8 * (i // 2) + 8]
        if i % 2:
            group = pltpu.roll(group, HEADS, 0)
        left = jnp.concatenate([*three_terms(group), zero], axis=0)
        out_ref[i, ROWS : ROWS + EXTRA, :] = jnp.concatenate([left, right], axis=1).astype(bf16)


def finish_kernel(order_ref, span_ref, in_ref, dq0, dq1, dq2, dq3, query_ref, key_ref, value_ref, forget_ref):
    first = ((lax.axis_index("z") * NX + lax.axis_index("x")) * NC + lax.axis_index("core")) * 2
    query_ref[...] = (((dq0[...] + dq1[...]) + (dq2[...] + dq3[...])) * SCALE).astype(bf16)
    total = in_ref[0].astype(f32)
    for i in range(1, NZ):
        total = total + in_ref[i].astype(f32)
    key_ref[...] = (total[0:ROWS, 0:HD] * SCALE).astype(bf16)
    value_ref[...] = total[0:ROWS, HD : 2 * HD].astype(bf16)
    extra = total[ROWS : ROWS + EXTRA]
    extra = extra[0:8] + extra[8:16] + extra[16:24]
    columns, totals = extra[:, 0:HD], extra[:, HD : 2 * HD]
    row, column = iota((8, HD), 0), iota((8, HD), 1)
    after = []
    for h in range(2):
        later = span_ref[...] > order_ref[first + h]
        line = jnp.sum(jnp.where(later, totals, 0.0), axis=0, keepdims=True)
        after.append(jnp.sum(jnp.where(column % HEADS == row, line, 0.0), axis=1, keepdims=True))
    within = lax.dot_general(
        columns, same_span_upto(ROWS), NT, precision=lax.Precision.HIGHEST, preferred_element_type=f32
    )
    within = within + jnp.where(column < SPAN, after[0], after[1])
    forget_ref[...] = -within[0:HEADS]


def call(kernel, specs, outs, scratch, flops, *args):
    smem, vmem = pl.BlockSpec(memory_space=pltpu.SMEM), pl.BlockSpec(memory_space=pltpu.VMEM)
    place = {"s": smem, "v": vmem}
    return pl.pallas_call(
        kernel,
        in_specs=[place[k] for k in specs],
        out_specs=[place[k] for k, _, _ in outs],
        out_shape=[jax.ShapeDtypeStruct(shape, dtype) for _, shape, dtype in outs],
        scratch_shapes=[pltpu.VMEM(shape, dtype) for shape, dtype in scratch],
        compiler_params=pltpu.CompilerParams(vmem_limit_bytes=VMEM_LIMIT),
        cost_estimate=pl.CostEstimate(flops=flops, bytes_accessed=4 << 20, transcendentals=0),
    )(*args)


def body(queries, keys, values, out_grad, gate_logits, doc_lengths, span_order):
    swap = [(0, 1), (1, 0)]
    order4 = span_order.reshape(NZ, NX, NC, 2)
    by_head = jnp.broadcast_to(order4.transpose(3, 2, 0, 1)[..., None], (2, NC, NZ, NX, HEADS))
    order_line = by_head.reshape(2, NC * NZ * NX * HEADS)
    order_column = order_line.T
    order_spans = by_head.transpose(3, 0, 1, 2, 4).reshape(QSPANS, NC * NZ * HEADS)
    order_spans = jnp.pad(order_spans, ((0, 0), (0, HD - NC * NZ * HEADS)), constant_values=-1)
    pair_rows = jnp.concatenate([queries, out_grad], axis=1)

    log_forget = jax.nn.log_sigmoid(gate_logits).T.reshape(NY, HEADS, 32)
    log_forget = jnp.pad(log_forget, ((0, 0), (0, 8 - HEADS), (0, HD - 32)))
    log_forget = jnp.broadcast_to(log_forget[None], (NX, NY, 8, HD)).reshape(NX * NY, 8, HD)
    log_forget, pair_rows, order_line, order_column, order_spans = lax.optimization_barrier(
        (log_forget, pair_rows, order_line, order_column, order_spans)
    )
    logs = lax.all_to_all(log_forget, ("x", "head"), 0, 0)
    message = (NZ, ROWS + EXTRA, 2 * HD)
    (key_message,) = call(send_keys_kernel, "vvv", [("v", message, bf16)], [], 0, logs, keys, values)

    key_message, pair_rows, order_line, doc_lengths = lax.optimization_barrier(
        (key_message, pair_rows, order_line, doc_lengths)
    )
    own = lax.all_to_all(key_message, "z", 0, 0)
    query_rows = [pair_rows]
    for k in range(1, NX):
        query_rows.append(lax.ppermute(pair_rows, "x", [(i, (i + k) % NX) for i in range(NX)]))
    plan = call(
        plan_kernel,
        "ssvv",
        [
            ("v", (2 * BLOCKS * NX * HEADS, 2 * BLOCKS * NX * HEADS), bf16),
            ("v", (3 * BLOCKS * NX * HEADS, 2 * HD), bf16),
            ("v", (LANES, LANES), i32),
            ("v", (QSPANS, LANES), i32),
            ("v", (QSPANS, LANES), i32),
            ("s", (PAIRS,), i32),
        ],
        [],
        1 << 28,
        span_order, doc_lengths, order_column, order_line,
    )
    own, query_rows, plan = lax.optimization_barrier((own, query_rows, plan))
    earlier, select, code, qpos, qdoc, pairs = plan
    peer = lax.ppermute(own, "core", swap)

    kv = ((BLOCKS, ROWS, 2 * HD), bf16)
    rows = ((QSPANS, LANES, HD), bf16)
    line = ((QSPANS, LANES), f32)
    stats, bias, qdecay = call(
        stats_kernel,
        "ssvvvvvvvvvvv",
        [("v", (NX, 24, LANES), f32), ("v", (ROWS, 2 * HD), bf16), ("v", (QSPANS, LANES), f32)],
        [kv, rows, rows, ((BLOCKS, NX * HEADS, ROWS), f32), line, line, line],
        1 << 28,
        span_order, pairs, earlier, select, code, qpos, qdoc, own, peer, *query_rows,
    )
    all_stats = lax.all_to_all(stats, "x", 0, 0)
    dq0, dq1, dq2, dq3, total, own_sum, peer_sum, own_col, peer_col = call(
        grads_kernel,
        "ssvvvvvvvvvvvv",
        [
            *[("v", (ROWS, HEADS * HD), f32)] * NX,
            ("v", (8, ROWS), f32),
            ("v", (NZ, ROWS, 2 * HD), f32),
            ("v", (NZ, ROWS, 2 * HD), f32),
            ("v", (NZ * HEADS, ROWS), f32),
            ("v", (NZ * HEADS, ROWS), f32),
        ],
        [kv, rows, rows, line, line, ((BLOCKS, ROWS, 2 * HD), f32), ((QSPANS, HD, LANES), f32), ((ROWS, ROWS), f32)],
        1 << 29,
        span_order, pairs, all_stats, bias, qdecay, code, qpos, qdoc, own, peer, *query_rows,
    )
    totals = [total]
    for k in range(1, NX):
        totals.append(lax.ppermute(total, "x", [(i, (i + k) % NX) for i in range(NX)]))
    peer_sum = lax.ppermute(peer_sum, "core", swap)
    peer_col = lax.ppermute(peer_col, "core", swap)
    totals, peer_sum, peer_col = lax.optimization_barrier((totals, peer_sum, peer_col))
    totals = jnp.concatenate(totals, axis=0)
    peer_totals = lax.ppermute(totals, "core", swap)
    (grad_message,) = call(
        send_grads_kernel,
        "vvvvvv",
        [("v", message, bf16)],
        [],
        0,
        own_sum, peer_sum, own_col, peer_col, totals, peer_totals,
    )
    grad_message, dq1, dq2, dq3 = lax.optimization_barrier((grad_message, dq1, dq2, dq3))
    back = lax.all_to_all(grad_message, "z", 0, 0)
    parts = [
        lax.ppermute(part, "x", [(i, (i - k) % NX) for i in range(NX)]) for k, part in ((1, dq1), (2, dq2), (3, dq3))
    ]
    back, parts = lax.optimization_barrier((back, parts))
    query_grad, key_grad, value_grad, forget_grad = call(
        finish_kernel,
        "svvvvvv",
        [
            ("v", (ROWS, HEADS * HD), bf16),
            ("v", (ROWS, HD), bf16),
            ("v", (ROWS, HD), bf16),
            ("v", (HEADS, ROWS), f32),
        ],
        [],
        0,
        span_order, order_spans, back, dq0, *parts,
    )
    return query_grad, key_grad, value_grad, forget_grad.T


def solution(mesh):
    fine = Mesh(mesh.devices.reshape(NZ, NX, NC, NY), ("z", "x", "core", "head"))
    ctx = ("z", "x", "core")
    rows = P(ctx, "head")
    return jax.shard_map(
        body,
        mesh=fine,
        in_specs=(rows, rows, rows, rows, P((*ctx, "head"), None), P(), P()),
        out_specs=(rows, rows, rows, rows),
        check_vma=False,
    )
```

```python
import functools
import math

import jax
import jax.numpy as jnp
from jax import lax
from jax.experimental import pallas as pl
from jax.experimental.pallas import tpu as pltpu
from jax.sharding import Mesh, PartitionSpec as P

NZ, NX, NC, NY = 8, 4, 2, 4
ROWS, SPAN, HEADS, HD = 128, 64, 4, 128
DOCS = 16
BLOCKS = NC * NZ
QSPANS = 2 * NX
LANES = HEADS * SPAN
BACK_EXTRA = 16
EXTRA = 32
DEAD = QSPANS * BLOCKS
STREAM = 8192
UNROLL = 2
PAIRS = DEAD + 2 * UNROLL + 1
NEG = -1e30
SCALE = 1.0 / math.sqrt(HD)
f32, bf16, i32 = jnp.float32, jnp.bfloat16, jnp.int32
VMEM_LIMIT = 16 * 1024 * 1024
NT = (((1,), (1,)), ((), ()))
TN = (((0,), (0,)), ((), ()))


def three_terms(a):
    high = a.astype(bf16).astype(f32)
    rest = a - high
    middle = rest.astype(bf16).astype(f32)
    return high, middle, rest - middle


def iota(shape, dim):
    return lax.broadcasted_iota(i32, shape, dim)


def same_span_upto(n):
    row, column = iota((n, n), 0), iota((n, n), 1)
    return jnp.where((row <= column) & (row // SPAN == column // SPAN), 1.0, 0.0).astype(f32)


def send_keys_kernel(log_ref, keys_ref, values_ref, out_ref):
    parts = []
    for x in range(NX):
        total = log_ref[x * NY]
        for y in range(1, NY):
            total = total + pltpu.roll(log_ref[x * NY + y], 32 * y, 1)
        parts.append(total)
    logs = jnp.concatenate(
        [parts[0] + pltpu.roll(parts[1], HEADS, 0), parts[2] + pltpu.roll(parts[3], HEADS, 0)], axis=0
    )
    sums = jnp.dot(logs, same_span_upto(ROWS), precision=lax.Precision.HIGHEST, preferred_element_type=f32)
    high, middle, low = three_terms(sums)
    extra = jnp.concatenate(
        [jnp.concatenate([high, middle], axis=1), jnp.concatenate([low, jnp.zeros_like(low)], axis=1)], axis=0
    ).astype(bf16)
    keys, values = keys_ref[...], values_ref[...]
    for i in range(NZ):
        out_ref[i, 0:ROWS, 0:HD] = keys
        out_ref[i, 0:ROWS, HD : 2 * HD] = values
        out_ref[i, ROWS : ROWS + EXTRA, :] = extra


def gather_queries(refs, queries_ref, grads_ref):
    heads = jnp.where(iota((LANES, HD), 1) % HEADS == iota((LANES, HD), 0) // SPAN, 1.0, 0.0).astype(bf16)
    for k, ref in enumerate(refs):
        for half in range(2):
            rows = slice(half * SPAN, (half + 1) * SPAN)
            queries_ref[2 * k + half, :, HD : 2 * HD] = heads
            for h in range(HEADS):
                to = slice(h * SPAN, (h + 1) * SPAN)
                queries_ref[2 * k + half, to, 0:HD] = ref[rows, h * HD : (h + 1) * HD]
                grads_ref[2 * k + half, to, :] = ref[rows, (HEADS + h) * HD : (HEADS + h + 1) * HD]


def shared_span(x, q):
    return 2 * ((x + NX - q // 2) % NX) + q % 2


def spans_of_block(order_ref, x, block):
    first = ((block % NZ) * (NX * NC) + x * NC + block // NZ) * 2
    return order_ref[first], order_ref[first + 1]


def span_of_query(order_ref, z, x, c, q):
    return order_ref[((z * NX + (x + NX - q // 2) % NX) * NC + c) * 2 + q % 2]


def chunk_scores(order_ref, pairs_ref, t, x, keys_ref, queries_ref, grads_ref, qpos_ref, qdoc_ref):
    pairs = [pairs_ref[2 * t + u] for u in range(2)]
    blocks = [pair % BLOCKS for pair in pairs]
    qspan = (pairs[0] % DEAD) // BLOCKS
    keys = jnp.concatenate([keys_ref[block, :, 0 : 2 * HD] for block in blocks], axis=0)
    values = jnp.concatenate([keys_ref[block, :, 2 * HD : 3 * HD] for block in blocks], axis=0)
    scores = lax.dot_general(keys, queries_ref[qspan], NT, preferred_element_type=f32)
    slopes = lax.dot_general(values, grads_ref[qspan], NT, preferred_element_type=f32)
    at = pl.ds(qspan, 1)
    qpos, qdoc = qpos_ref[at, :][:, 0:HD], qdoc_ref[at, :][:, 0:HD]
    row = iota((ROWS, HD), 0)
    live = []
    for pair, block in zip(pairs, blocks):
        even, odd = spans_of_block(order_ref, x, block)
        even = jnp.where(pair < DEAD, even, 2 * STREAM)
        odd = jnp.where(pair < DEAD, odd, 2 * STREAM)
        key_pos = row + jnp.where(row < SPAN, even * SPAN, odd * SPAN - SPAN)
        half = (key_pos <= qpos) & (key_pos >= qdoc)
        live.append(jnp.concatenate([half, half], axis=1))
    return qspan, blocks, keys, jnp.concatenate(live, axis=0), scores, slopes


def plan_kernel(order_ref, length_ref, column_ref, line_ref, earlier_ref, select_ref, qpos_ref, qdoc_ref, pairs_ref):
    z, x, c = lax.axis_index("z"), lax.axis_index("x"), lax.axis_index("core")
    count = BLOCKS * NX * HEADS
    target = jnp.concatenate([column_ref[:, 0:1], column_ref[:, 1:2]], axis=0)
    source = jnp.concatenate([line_ref[0:1, :], line_ref[1:2, :]], axis=1)
    square = (2 * count, 2 * count)
    earlier = (source < target) & (iota(square, 0) % HEADS == iota(square, 1) % HEADS)
    earlier_ref[...] = jnp.where(earlier, 1.0, 0.0).astype(bf16)
    row, column = iota((3 * count, 2 * HD), 0), iota((3 * count, 2 * HD), 1)
    term = (column % 16) // HEADS
    wanted = term * count + (column // 16) * (NX * HEADS) + x * HEADS + column % HEADS
    select_ref[...] = jnp.where((row == wanted) & (term < 3), 1.0, 0.0).astype(bf16)
    row, column = iota((QSPANS, LANES), 0), iota((QSPANS, LANES), 1)
    qpos = column % SPAN
    spans = []
    for q in range(QSPANS):
        spans.append(span_of_query(order_ref, z, x, c, q))
        qpos = qpos + jnp.where(row == q, spans[q] * SPAN, 0)
    starts = [jnp.int32(0)]
    for doc in range(DOCS - 1):
        starts.append(starts[-1] + length_ref[doc])
    qdoc = jnp.zeros((QSPANS, LANES), i32)
    for start in starts:
        qdoc = jnp.where(qpos >= start, start, qdoc)
    qpos_ref[...] = qpos
    qdoc_ref[...] = qdoc
    found = jnp.int32(0)
    for q in range(QSPANS):
        mine, begin = spans[q], jnp.int32(0)
        for start in starts:
            begin = jnp.where(mine * SPAN >= start, start, begin)

        def scan(block, found, q=q, mine=mine, begin=begin):
            even, odd = spans_of_block(order_ref, x, block)
            live = ((even <= mine) & (even * SPAN + SPAN > begin)) | ((odd <= mine) & (odd * SPAN + SPAN > begin))
            pairs_ref[found] = q * BLOCKS + block
            return found + live.astype(i32)

        found = lax.fori_loop(0, BLOCKS, scan, found, unroll=8)
        pairs_ref[found] = DEAD + q * BLOCKS
        found = found + found % 2
    for i in range(2 * UNROLL):
        pairs_ref[found + i] = DEAD
    pairs_ref[PAIRS - 1] = found


def stats_kernel(
    order_ref, pairs_ref, earlier_ref, select_ref, qpos_ref, qdoc_ref, own_ref, peer_ref, qd0, qd1, qd2, qd3,
    stats_ref, keys_ref, queries_ref, grads_ref, qdecay_ref,
    decay, high_s, mass_s, cross_s,
):
    z, x, c = lax.axis_index("z"), lax.axis_index("x"), lax.axis_index("core")
    gather_queries((qd0, qd1, qd2, qd3), queries_ref, grads_ref)
    for i in range(NZ):
        for ref, core in ((own_ref, c), (peer_ref, 1 - c)):
            block = core * NZ + i
            keys_ref[block, :, 0:HD] = ref[i, 0:ROWS, 0:HD]
            keys_ref[block, :, 2 * HD : 3 * HD] = ref[i, 0:ROWS, HD : 2 * HD]
            terms = ref[i, ROWS : ROWS + EXTRA, :].astype(f32)
            decay[block] = terms[0:16, 0:HD] + terms[0:16, HD : 2 * HD] + terms[16:32, 0:HD]
    count = BLOCKS * NX * HEADS
    sums = decay[...].reshape(count, ROWS)
    totals = jnp.concatenate([sums[:, SPAN - 1 : SPAN], sums[:, ROWS - 1 : ROWS]], axis=0)
    t_high, t_middle, t_low = three_terms(totals)
    lane = iota((2 * count, HD), 1)
    zero = jnp.zeros((2 * count, HD), f32)
    t_terms = jnp.where(
        lane == 0, t_high, jnp.where(lane == 1, t_middle, jnp.where(lane == 2, t_low, zero))
    ).astype(bf16)
    before = jnp.dot(earlier_ref[...], t_terms, preferred_element_type=f32)
    before = before[:, 0:1] + before[:, 1:2] + before[:, 2:3]
    sums = sums + jnp.where(iota((count, ROWS), 1) < SPAN, before[0:count], before[count : 2 * count])
    decay[...] = sums.reshape(BLOCKS, NX * HEADS, ROWS)
    terms = jnp.concatenate(three_terms(sums * (-1.0 / SCALE)), axis=0).astype(bf16)
    terms = lax.dot_general(terms, select_ref[...], TN, preferred_element_type=f32)
    group = iota((ROWS, HD), 1) // 16
    for block in range(BLOCKS):
        tile = terms[:, (block // 8) * HD : (block // 8 + 1) * HD]
        keys_ref[block, :, HD : 2 * HD] = jnp.where(group == block % 8, tile, 0.0).astype(bf16)
    mine = c * NZ + z
    for k in range(NX):
        own = decay[mine, pl.ds(((x + NX - k) % NX) * HEADS, HEADS), :]
        for half in range(2):
            for h in range(HEADS):
                qdecay_ref[2 * k + half : 2 * k + half + 1, h * SPAN : (h + 1) * SPAN] = own[
                    h : h + 1, half * SPAN : (half + 1) * SPAN
                ]
    high_s[...] = jnp.full((QSPANS, LANES), NEG, f32)
    mass_s[...] = jnp.zeros((QSPANS, LANES), f32)
    cross_s[...] = jnp.zeros((QSPANS, LANES), f32)

    def step(t, carry):
        parts = []
        for u in range(UNROLL):
            qspan, _, _, live, scores, slopes = chunk_scores(
                order_ref, pairs_ref, UNROLL * t + u, x, keys_ref, queries_ref, grads_ref, qpos_ref, qdoc_ref
            )
            scores = jnp.where(live, scores * SCALE + qdecay_ref[pl.ds(qspan, 1), :], NEG)
            high = jnp.max(scores, axis=0, keepdims=True)
            weights = jnp.exp(scores - high)
            mass = jnp.sum(weights, axis=0, keepdims=True)
            parts.append((qspan, high, mass, jnp.sum(weights * slopes, axis=0, keepdims=True)))
        for qspan, high, mass, cross in parts:
            at = pl.ds(shared_span(x, qspan), 1)
            old = high_s[at, :]
            new = jnp.maximum(old, high)
            before, now = jnp.exp(old - new), jnp.exp(high - new)
            high_s[at, :] = new
            mass_s[at, :] = mass_s[at, :] * before + mass * now
            cross_s[at, :] = cross_s[at, :] * before + cross * now
        return carry

    lax.fori_loop(0, (pairs_ref[PAIRS - 1] + 2 * UNROLL - 1) // (2 * UNROLL), step, 0)
    for i in range(NX):
        stats_ref[i, 0:8, :] = high_s[...]
        stats_ref[i, 8:16, :] = mass_s[...]
        stats_ref[i, 16:24, :] = cross_s[...]


def grads_kernel(
    order_ref, pairs_ref, stats_ref, keys_ref, queries_ref, grads_ref, qdecay_ref, qpos_ref, qdoc_ref,
    dq0, dq1, dq2, dq3, total_out, own_out, peer_out, own_col, peer_col,
    lse_s, delta_s, acc, dqt, col,
):
    x, c = lax.axis_index("x"), lax.axis_index("core")
    high = stats_ref[0, 0:8, :]
    for i in range(1, NX):
        high = jnp.maximum(high, stats_ref[i, 0:8, :])
    mass, cross = jnp.zeros_like(high), jnp.zeros_like(high)
    for i in range(NX):
        factor = jnp.exp(stats_ref[i, 0:8, :] - high)
        mass = mass + stats_ref[i, 8:16, :] * factor
        cross = cross + stats_ref[i, 16:24, :] * factor
    lse_s[...] = high + jnp.log(mass)
    delta_s[...] = cross / mass
    acc[...] = jnp.zeros_like(acc)
    dqt[...] = jnp.zeros_like(dqt)
    col[...] = jnp.zeros_like(col)

    def step(t, carry):
        parts = []
        for u in range(UNROLL):
            qspan, blocks, keys, live, scores, slopes = chunk_scores(
                order_ref, pairs_ref, UNROLL * t + u, x, keys_ref, queries_ref, grads_ref, qpos_ref, qdoc_ref
            )
            at = pl.ds(shared_span(x, qspan), 1)
            shift = qdecay_ref[pl.ds(qspan, 1), :] - lse_s[at, :]
            probs = jnp.exp(jnp.where(live, scores * SCALE + shift, NEG))
            dscores = probs * (slopes - delta_s[at, :])
            upper = dscores.astype(bf16)
            lower = (dscores - upper.astype(f32)).astype(bf16)
            queries = queries_ref[qspan]
            both = jnp.dot(upper, queries, preferred_element_type=f32)
            dv = jnp.dot(probs.astype(bf16), grads_ref[qspan], preferred_element_type=f32)
            column = both[:, HD : 2 * HD] + jnp.dot(lower, queries[:, HD : 2 * HD], preferred_element_type=f32)
            dq = lax.dot_general(
                jnp.concatenate([keys[:, 0:HD], keys[:, 0:HD]], axis=0),
                jnp.concatenate([upper, lower], axis=0),
                TN,
                preferred_element_type=f32,
            )
            parts.append((qspan, blocks, both[:, 0:HD], dv, column, dq))
        group = iota((ROWS, HD), 1) // HEADS
        for qspan, blocks, dk, dv, column, dq in parts:
            dqt[qspan] += dq
            for u, block in enumerate(blocks):
                rows = slice(u * ROWS, (u + 1) * ROWS)
                acc[block, :, 0:HD] += dk[rows]
                acc[block, :, HD : 2 * HD] += dv[rows]
                col[...] += jnp.where(group == block, column[rows], 0.0)
        return carry

    lax.fori_loop(0, (pairs_ref[PAIRS - 1] + 2 * UNROLL - 1) // (2 * UNROLL), step, 0)
    for q in range(QSPANS):
        whole = dqt[q].T
        begin = (q % 2) * SPAN
        for h in range(HEADS):
            (dq0, dq1, dq2, dq3)[q // 2][begin : begin + SPAN, h * HD : (h + 1) * HD] = whole[h * SPAN : (h + 1) * SPAN]
    columns = col[...]
    even = jnp.sum(columns[0:SPAN], axis=0, keepdims=True)
    odd = jnp.sum(columns[SPAN:ROWS], axis=0, keepdims=True)
    total_out[...] = jnp.broadcast_to(even + pltpu.roll(odd, SPAN, 1), total_out.shape)
    col[...] = columns.T
    half = NZ * HEADS
    own_col[...] = col[pl.ds(pl.multiple_of(c * half, half), half), :]
    peer_col[...] = col[pl.ds(pl.multiple_of((1 - c) * half, half), half), :]
    for i in range(NZ):
        own_out[i] = acc[c * NZ + i]
        peer_out[i] = acc[(1 - c) * NZ + i]


def send_grads_kernel(own_ref, peer_ref, own_col, peer_col, mine_ref, other_ref, out_ref):
    x = lax.axis_index("x")
    row = iota((8, HD), 0)
    totals = jnp.zeros((8, HD), f32)
    for k in range(NX):
        both = mine_ref[8 * k : 8 * k + 8, :] + other_ref[8 * k : 8 * k + 8, :]
        totals = jnp.where(row == 2 * ((x + NX - k) % NX), both, totals)
    high, middle, low = three_terms(totals)
    right = jnp.concatenate([high + pltpu.roll(middle, 1, 0), low], axis=0)
    columns = own_col[...] + peer_col[...]
    for i in range(NZ):
        out_ref[i, 0:ROWS, :] = (own_ref[i] + peer_ref[i]).astype(bf16)
        group = columns[8 * (i // 2) : 8 * (i // 2) + 8]
        if i % 2:
            group = pltpu.roll(group, HEADS, 0)
        high, middle, low = three_terms(group)
        left = jnp.concatenate([jnp.where(row < HEADS, high, pltpu.roll(middle, HEADS, 0)), low], axis=0)
        out_ref[i, ROWS : ROWS + BACK_EXTRA, :] = jnp.concatenate([left, right], axis=1).astype(bf16)


def finish_kernel(order_ref, span_ref, in_ref, dq0, dq1, dq2, dq3, query_ref, key_ref, value_ref, forget_ref):
    first = ((lax.axis_index("z") * NX + lax.axis_index("x")) * NC + lax.axis_index("core")) * 2
    query_ref[...] = (((dq0[...] + dq1[...]) + (dq2[...] + dq3[...])) * SCALE).astype(bf16)
    total = in_ref[0].astype(f32)
    for i in range(1, NZ):
        total = total + in_ref[i].astype(f32)
    key_ref[...] = (total[0:ROWS, 0:HD] * SCALE).astype(bf16)
    value_ref[...] = total[0:ROWS, HD : 2 * HD].astype(bf16)
    extra = total[ROWS : ROWS + BACK_EXTRA]
    left, right = extra[:, 0:HD], extra[:, HD : 2 * HD]
    columns = left[0:8] + pltpu.roll(left[0:8], HEADS, 0) + left[8:16]
    totals = right[0:8] + pltpu.roll(right[0:8], 7, 0) + right[8:16]
    row, column = iota((8, HD), 0), iota((8, HD), 1)
    after = []
    for h in range(2):
        later = span_ref[...] > order_ref[first + h]
        line = jnp.sum(jnp.where(later, totals, 0.0), axis=0, keepdims=True)
        after.append(jnp.sum(jnp.where(column % HEADS == row, line, 0.0), axis=1, keepdims=True))
    within = lax.dot_general(
        columns, same_span_upto(ROWS), NT, precision=lax.Precision.HIGHEST, preferred_element_type=f32
    )
    within = within + jnp.where(column < SPAN, after[0], after[1])
    forget_ref[...] = -within[0:HEADS]


def call(kernel, specs, outs, scratch, flops, *args):
    smem, vmem = pl.BlockSpec(memory_space=pltpu.SMEM), pl.BlockSpec(memory_space=pltpu.VMEM)
    place = {"s": smem, "v": vmem}
    return pl.pallas_call(
        kernel,
        in_specs=[place[k] for k in specs],
        out_specs=[place[k] for k, _, _ in outs],
        out_shape=[jax.ShapeDtypeStruct(shape, dtype) for _, shape, dtype in outs],
        scratch_shapes=[pltpu.VMEM(shape, dtype) for shape, dtype in scratch],
        compiler_params=pltpu.CompilerParams(vmem_limit_bytes=VMEM_LIMIT),
        cost_estimate=pl.CostEstimate(flops=flops, bytes_accessed=4 << 20, transcendentals=0),
    )(*args)


def body(queries, keys, values, out_grad, gate_logits, doc_lengths, span_order):
    swap = [(0, 1), (1, 0)]
    log_forget = jax.nn.log_sigmoid(gate_logits).T.reshape(NY, HEADS, 32)
    log_forget = jnp.pad(log_forget, ((0, 0), (0, 8 - HEADS), (0, HD - 32)))
    log_forget = jnp.broadcast_to(log_forget[None], (NX, NY, 8, HD)).reshape(NX * NY, 8, HD)
    logs = lax.all_to_all(log_forget, ("x", "head"), 0, 0)
    message = (NZ, ROWS + EXTRA, 2 * HD)
    (key_message,) = call(send_keys_kernel, "vvv", [("v", message, bf16)], [], 0, logs, keys, values)

    key_message, queries, out_grad, span_order, doc_lengths = lax.optimization_barrier(
        (key_message, queries, out_grad, span_order, doc_lengths)
    )
    pair_rows = jnp.concatenate([queries, out_grad], axis=1)
    order4 = span_order.reshape(NZ, NX, NC, 2).transpose(3, 2, 0, 1)
    order_line = jnp.broadcast_to(order4[..., None], (2, NC, NZ, NX, HEADS)).reshape(2, NC * NZ * NX * HEADS)
    order_column = order_line.T
    order_spans = jnp.broadcast_to(order4.transpose(3, 0, 1, 2)[..., None], (NX, 2, NC, NZ, HEADS)).reshape(NX, 1, HD)
    order_spans = jnp.concatenate([order_spans, jnp.full_like(order_spans, -1)], axis=1).reshape(2 * NX, HD)
    own = lax.all_to_all(key_message, "z", 0, 0)
    query_rows = [pair_rows]
    for k in range(1, NX):
        query_rows.append(lax.ppermute(pair_rows, "x", [(i, (i + k) % NX) for i in range(NX)]))
    plan = call(
        plan_kernel,
        "ssvv",
        [
            ("v", (2 * BLOCKS * NX * HEADS, 2 * BLOCKS * NX * HEADS), bf16),
            ("v", (3 * BLOCKS * NX * HEADS, 2 * HD), bf16),
            ("v", (QSPANS, LANES), i32),
            ("v", (QSPANS, LANES), i32),
            ("s", (PAIRS,), i32),
        ],
        [],
        1 << 28,
        span_order, doc_lengths, order_column, order_line,
    )
    own, query_rows, plan, order_spans = lax.optimization_barrier((own, query_rows, plan, order_spans))
    earlier, select, qpos, qdoc, pairs = plan
    peer = lax.ppermute(own, "core", swap)

    line = ((QSPANS, LANES), f32)
    stats, *rows, qdecay = call(
        stats_kernel,
        "ssvvvvvvvvvv",
        [
            ("v", (NX, 24, LANES), f32),
            ("v", (BLOCKS, ROWS, 3 * HD), bf16),
            ("v", (QSPANS, LANES, 2 * HD), bf16),
            ("v", (QSPANS, LANES, HD), bf16),
            ("v", (QSPANS, LANES), f32),
        ],
        [((BLOCKS, NX * HEADS, ROWS), f32), line, line, line],
        1 << 28,
        span_order, pairs, earlier, select, qpos, qdoc, own, peer, *query_rows,
    )
    all_stats = lax.all_to_all(stats, "x", 0, 0)
    dq0, dq1, dq2, dq3, total, own_sum, peer_sum, own_col, peer_col = call(
        grads_kernel,
        "ssvvvvvvv",
        [
            *[("v", (ROWS, HEADS * HD), f32)] * NX,
            ("v", (8, ROWS), f32),
            ("v", (NZ, ROWS, 2 * HD), f32),
            ("v", (NZ, ROWS, 2 * HD), f32),
            ("v", (NZ * HEADS, ROWS), f32),
            ("v", (NZ * HEADS, ROWS), f32),
        ],
        [line, line, ((BLOCKS, ROWS, 2 * HD), f32), ((QSPANS, HD, LANES), f32), ((ROWS, ROWS), f32)],
        1 << 29,
        span_order, pairs, all_stats, *rows, qdecay, qpos, qdoc,
    )
    totals = [total]
    for k in range(1, NX):
        totals.append(lax.ppermute(total, "x", [(i, (i + k) % NX) for i in range(NX)]))
    peer_sum = lax.ppermute(peer_sum, "core", swap)
    peer_col = lax.ppermute(peer_col, "core", swap)
    totals, peer_sum, peer_col = lax.optimization_barrier((totals, peer_sum, peer_col))
    totals = jnp.concatenate(totals, axis=0)
    peer_totals = lax.ppermute(totals, "core", swap)
    (grad_message,) = call(
        send_grads_kernel,
        "vvvvvv",
        [("v", (NZ, ROWS + BACK_EXTRA, 2 * HD), bf16)],
        [],
        0,
        own_sum, peer_sum, own_col, peer_col, totals, peer_totals,
    )
    grad_message, dq1, dq2, dq3 = lax.optimization_barrier((grad_message, dq1, dq2, dq3))
    back = lax.all_to_all(grad_message, "z", 0, 0)
    parts = [
        lax.ppermute(part, "x", [(i, (i - k) % NX) for i in range(NX)]) for k, part in ((1, dq1), (2, dq2), (3, dq3))
    ]
    back, parts = lax.optimization_barrier((back, parts))
    query_grad, key_grad, value_grad, forget_grad = call(
        finish_kernel,
        "svvvvvv",
        [
            ("v", (ROWS, HEADS * HD), bf16),
            ("v", (ROWS, HD), bf16),
            ("v", (ROWS, HD), bf16),
            ("v", (HEADS, ROWS), f32),
        ],
        [],
        0,
        span_order, order_spans, back, dq0, *parts,
    )
    return query_grad, key_grad, value_grad, forget_grad.T


def solution(mesh):
    fine = Mesh(mesh.devices.reshape(NZ, NX, NC, NY), ("z", "x", "core", "head"))
    ctx = ("z", "x", "core")
    rows = P(ctx, "head")
    return jax.shard_map(
        body,
        mesh=fine,
        in_specs=(rows, rows, rows, rows, P((*ctx, "head"), None), P(), P()),
        out_specs=(rows, rows, rows, rows),
        check_vma=False,
    )
```

```python
import functools
import math

import jax
import jax.numpy as jnp
from jax import lax
from jax.experimental import pallas as pl
from jax.experimental.pallas import tpu as pltpu
from jax.sharding import Mesh, PartitionSpec as P

NZ, NX, NC, NY = 8, 4, 2, 4
ROWS, SPAN, HEADS, HD = 128, 64, 4, 128
DOCS = 16
BLOCKS = NC * NZ
KEY_ROWS = BLOCKS * 8
SOURCES = BLOCKS * NX * HEADS
TARGETS = 2 * KEY_ROWS + 2 * NX * HEADS
QSPANS = 2 * NX
LANES = HEADS * SPAN
EXTRA = 16
DEAD = QSPANS * BLOCKS
STREAM = 8192
UNROLL = 2
PAIRS = DEAD + 2 * UNROLL + 1
CHUNKS = DEAD // 2 + UNROLL
TOGETHER = 8
NEG = -1e30
SCALE = 1.0 / math.sqrt(HD)
f32, bf16, i32 = jnp.float32, jnp.bfloat16, jnp.int32
VMEM_LIMIT = 16 * 1024 * 1024
NT = (((1,), (1,)), ((), ()))
TN = (((0,), (0,)), ((), ()))


def three_terms(a):
    high = a.astype(bf16).astype(f32)
    rest = a - high
    middle = rest.astype(bf16).astype(f32)
    return high, middle, rest - middle


def exact_dot(a, ones):
    terms = jnp.concatenate(three_terms(a), axis=0).astype(bf16)
    terms = jnp.dot(terms, ones.astype(bf16), preferred_element_type=f32)
    rows = a.shape[0]
    return terms[0:rows] + terms[rows : 2 * rows] + terms[2 * rows : 3 * rows]


def iota(shape, dim):
    return lax.broadcasted_iota(i32, shape, dim)


def same_span_upto(n):
    row, column = iota((n, n), 0), iota((n, n), 1)
    return jnp.where((row <= column) & (row // SPAN == column // SPAN), 1.0, 0.0).astype(f32)


def same_span_from(n):
    row, column = iota((n, n), 0), iota((n, n), 1)
    return jnp.where((row >= column) & (row // SPAN == column // SPAN), 1.0, 0.0).astype(f32)


def send_keys_kernel(log_ref, rows_ref, out_ref, sums_ref):
    parts = []
    for x in range(NX):
        total = log_ref[x * NY]
        for y in range(1, NY):
            total = total + pltpu.roll(log_ref[x * NY + y], 32 * y, 1)
        parts.append(total)
    logs = jnp.concatenate(
        [parts[0] + pltpu.roll(parts[1], HEADS, 0), parts[2] + pltpu.roll(parts[3], HEADS, 0)], axis=0
    )
    sums = exact_dot(logs, same_span_upto(ROWS))
    sums_ref[...] = sums
    x = lax.axis_index("x")
    row = iota((8, HD), 0)
    own = jnp.zeros((8, HD), f32)
    for h in range(HEADS):
        own = jnp.where(row == h, sums_ref[pl.ds(x * HEADS + h, 1), :], own)
    high, middle, low = three_terms(own)
    left = jnp.concatenate([high + pltpu.roll(middle, HEADS, 0), low], axis=0)
    terms = jnp.concatenate(three_terms(sums), axis=1).astype(bf16)
    row, column = iota((3 * HD, HD), 0), iota((3 * HD, HD), 1)
    wanted = (column // 2) * HD + (column % 2) * SPAN + SPAN - 1
    pick = jnp.where((row == wanted) & (column < 6), 1.0, 0.0).astype(bf16)
    right = jnp.dot(terms, pick, preferred_element_type=f32)
    extra = jnp.concatenate([left, right], axis=1).astype(bf16)
    rows = rows_ref[...]
    for i in range(NZ):
        out_ref[i, 0:ROWS, :] = rows
        out_ref[i, ROWS : ROWS + EXTRA, :] = extra


def gather_queries(refs, queries_ref, grads_ref):
    heads = jnp.where(iota((LANES, HD), 1) % HEADS == iota((LANES, HD), 0) // SPAN, 1.0, 0.0).astype(bf16)
    for k, ref in enumerate(refs):
        for half in range(2):
            rows = slice(half * SPAN, (half + 1) * SPAN)
            queries_ref[2 * k + half, :, HD : 2 * HD] = heads
            for h in range(HEADS):
                to = slice(h * SPAN, (h + 1) * SPAN)
                queries_ref[2 * k + half, to, 0:HD] = ref[rows, h * HD : (h + 1) * HD]
                grads_ref[2 * k + half, to, :] = ref[rows, (HEADS + h) * HD : (HEADS + h + 1) * HD]


def shared_span(x, q):
    return 2 * ((x + NX - q // 2) % NX) + q % 2


def spans_of_block(order_ref, x, block):
    first = ((block % NZ) * (NX * NC) + x * NC + block // NZ) * 2
    return order_ref[first], order_ref[first + 1]


def span_of_query(order_ref, z, x, c, q):
    return order_ref[((z * NX + (x + NX - q // 2) % NX) * NC + c) * 2 + q % 2]


def chunk_scores(order_ref, pairs_ref, t, x, keys_ref, queries_ref, grads_ref, qpos_ref, qdoc_ref):
    pairs = [pairs_ref[2 * t + u] for u in range(2)]
    blocks = [pair % BLOCKS for pair in pairs]
    qspan = (pairs[0] % DEAD) // BLOCKS
    keys = jnp.concatenate([keys_ref[block, :, 0 : 2 * HD] for block in blocks], axis=0)
    values = jnp.concatenate([keys_ref[block, :, 2 * HD : 3 * HD] for block in blocks], axis=0)
    scores = lax.dot_general(keys, queries_ref[qspan], NT, preferred_element_type=f32)
    slopes = lax.dot_general(values, grads_ref[qspan], NT, preferred_element_type=f32)
    at = pl.ds(qspan, 1)
    qpos, qdoc = qpos_ref[at, :][:, 0:HD], qdoc_ref[at, :][:, 0:HD]
    row = iota((ROWS, HD), 0)
    live = []
    for pair, block in zip(pairs, blocks):
        even, odd = spans_of_block(order_ref, x, block)
        even = jnp.where(pair < DEAD, even, 2 * STREAM)
        odd = jnp.where(pair < DEAD, odd, 2 * STREAM)
        key_pos = row + jnp.where(row < SPAN, even * SPAN, odd * SPAN - SPAN)
        half = (key_pos <= qpos) & (key_pos >= qdoc)
        live.append(jnp.concatenate([half, half], axis=1))
    return qspan, blocks, keys, jnp.concatenate(live, axis=0), scores, slopes


def plan_kernel(order_ref, length_ref, line_ref, earlier_ref, select_ref, qpos_ref, qdoc_ref, pairs_ref):
    z, x, c = lax.axis_index("z"), lax.axis_index("x"), lax.axis_index("core")
    row = iota((KEY_ROWS, 1), 0)
    targets = []
    for half in range(2):
        target = jnp.zeros((KEY_ROWS, 1), i32)
        for block in range(BLOCKS):
            target = jnp.where(row // 8 == block, spans_of_block(order_ref, x, block)[half], target)
        targets.append(target)
    row = iota((NX * HEADS, 1), 0)
    for half in range(2):
        target = jnp.zeros((NX * HEADS, 1), i32)
        for i in range(NX):
            target = jnp.where(row // HEADS == i, order_ref[((z * NX + i) * NC + c) * 2 + half], target)
        targets.append(target)
    target = jnp.concatenate(targets, axis=0)
    source = jnp.concatenate([line_ref[0:1, :], line_ref[1:2, :]], axis=1)
    shape = (TARGETS, 2 * SOURCES)
    earlier = (source < target) & (iota(shape, 0) % HEADS == iota(shape, 1) % HEADS)
    earlier_ref[...] = jnp.where(earlier, 1.0, 0.0).astype(bf16)
    row, column = iota((3 * KEY_ROWS, 2 * HD), 0), iota((3 * KEY_ROWS, 2 * HD), 1)
    term = (column % 16) // HEADS
    wanted = term * KEY_ROWS + (column // 16) * 8 + column % HEADS
    select_ref[...] = jnp.where((row == wanted) & (term < 3), 1.0, 0.0).astype(bf16)
    row, column = iota((QSPANS, LANES), 0), iota((QSPANS, LANES), 1)
    qpos = column % SPAN
    spans = []
    for q in range(QSPANS):
        spans.append(span_of_query(order_ref, z, x, c, q))
        qpos = qpos + jnp.where(row == q, spans[q] * SPAN, 0)
    starts = [jnp.int32(0)]
    for doc in range(DOCS - 1):
        starts.append(starts[-1] + length_ref[doc])
    qdoc = jnp.zeros((QSPANS, LANES), i32)
    for start in starts:
        qdoc = jnp.where(qpos >= start, start, qdoc)
    qpos_ref[...] = qpos
    qdoc_ref[...] = qdoc
    found = jnp.int32(0)
    for q in range(QSPANS):
        mine, begin = spans[q], jnp.int32(0)
        for start in starts:
            begin = jnp.where(mine * SPAN >= start, start, begin)

        def scan(block, found, q=q, mine=mine, begin=begin):
            even, odd = spans_of_block(order_ref, x, block)
            live = ((even <= mine) & (even * SPAN + SPAN > begin)) | ((odd <= mine) & (odd * SPAN + SPAN > begin))
            pairs_ref[found] = q * BLOCKS + block
            return found + live.astype(i32)

        found = lax.fori_loop(0, BLOCKS, scan, found, unroll=8)
        pairs_ref[found] = DEAD + q * BLOCKS
        found = found + found % 2
    for i in range(2 * UNROLL):
        pairs_ref[found + i] = DEAD
    pairs_ref[PAIRS - 1] = found


def stats_kernel(
    order_ref, pairs_ref, earlier_ref, select_ref, qpos_ref, qdoc_ref, sums_ref, own_ref, peer_ref, qd0, qd1, qd2, qd3,
    stats_ref, keys_ref, queries_ref, grads_ref, qdecay_ref, part_ref, part_high_ref,
    decay, totals, qsums, high_s, mass_s, cross_s,
):
    z, x, c = lax.axis_index("z"), lax.axis_index("x"), lax.axis_index("core")
    gather_queries((qd0, qd1, qd2, qd3), queries_ref, grads_ref)
    for i in range(NZ):
        for ref, core in ((own_ref, c), (peer_ref, 1 - c)):
            block = core * NZ + i
            keys_ref[block, :, 0:HD] = ref[i, 0:ROWS, 0:HD]
            keys_ref[block, :, 2 * HD : 3 * HD] = ref[i, 0:ROWS, HD : 2 * HD]
            totals[block] = ref[i, ROWS : ROWS + EXTRA, HD : 2 * HD]
            terms = ref[i, ROWS : ROWS + EXTRA, 0:HD].astype(f32)
            decay[block] = terms[0:8] + pltpu.roll(terms[0:8], HEADS, 0) + terms[8:16]
    sources = totals[...].reshape(SOURCES, HD)
    first = jnp.dot(earlier_ref[:, 0:SOURCES], sources, preferred_element_type=f32)
    second = jnp.dot(earlier_ref[:, SOURCES : 2 * SOURCES], sources, preferred_element_type=f32)
    lane = iota((TARGETS, HD), 1)
    both = jnp.where(lane < 6, jnp.where(lane % 2 == 0, first, second), 0.0)
    before = jnp.sum(both, axis=1, keepdims=True)
    left = iota((KEY_ROWS, ROWS), 1) < SPAN
    sums = decay[...].reshape(KEY_ROWS, ROWS) + jnp.where(left, before[0:KEY_ROWS], before[KEY_ROWS : 2 * KEY_ROWS])
    own, rows = before[2 * KEY_ROWS :], NX * HEADS
    qsums[...] = sums_ref[...] + jnp.where(iota((rows, ROWS), 1) < SPAN, own[0:rows], own[rows : 2 * rows])
    terms = jnp.concatenate(three_terms(sums * (-1.0 / SCALE)), axis=0).astype(bf16)
    terms = lax.dot_general(terms, select_ref[...], TN, preferred_element_type=f32)
    group = iota((ROWS, HD), 1) // 16
    for block in range(BLOCKS):
        tile = terms[:, (block // 8) * HD : (block // 8 + 1) * HD]
        keys_ref[block, :, HD : 2 * HD] = jnp.where(group == block % 8, tile, 0.0).astype(bf16)
    for k in range(NX):
        for h in range(HEADS):
            own = qsums[pl.ds(((x + NX - k) % NX) * HEADS + h, 1), :]
            for half in range(2):
                qdecay_ref[2 * k + half : 2 * k + half + 1, h * SPAN : (h + 1) * SPAN] = own[
                    :, half * SPAN : (half + 1) * SPAN
                ]
    high_s[...] = jnp.full((QSPANS, LANES), NEG, f32)
    mass_s[...] = jnp.zeros((QSPANS, LANES), f32)
    cross_s[...] = jnp.zeros((QSPANS, LANES), f32)

    def step(t, carry):
        parts = []
        for u in range(UNROLL):
            qspan, _, _, live, scores, slopes = chunk_scores(
                order_ref, pairs_ref, UNROLL * t + u, x, keys_ref, queries_ref, grads_ref, qpos_ref, qdoc_ref
            )
            scores = jnp.where(live, scores * SCALE + qdecay_ref[pl.ds(qspan, 1), :], NEG)
            high = jnp.max(scores, axis=0, keepdims=True)
            weights = jnp.exp(scores - high)
            sums, row = jnp.zeros((8, LANES), f32), iota((8, LANES), 0)
            for first, array in ((0, weights), (4, weights * slopes)):
                for i in range(4):
                    one = jnp.sum(array[i * SPAN : (i + 1) * SPAN], axis=0, keepdims=True)
                    sums = jnp.where(row == first + i, one, sums)
            part_ref[UNROLL * t + u] = sums
            part_high_ref[UNROLL * t + u] = jnp.broadcast_to(high, (8, LANES))
            parts.append(
                (qspan, high, jnp.sum(sums[0:4], axis=0, keepdims=True), jnp.sum(sums[4:8], axis=0, keepdims=True))
            )
        for qspan, high, mass, cross in parts:
            at = pl.ds(shared_span(x, qspan), 1)
            old = high_s[at, :]
            new = jnp.maximum(old, high)
            before, now = jnp.exp(old - new), jnp.exp(high - new)
            high_s[at, :] = new
            mass_s[at, :] = mass_s[at, :] * before + mass * now
            cross_s[at, :] = cross_s[at, :] * before + cross * now
        return carry

    lax.fori_loop(0, (pairs_ref[PAIRS - 1] + 2 * UNROLL - 1) // (2 * UNROLL), step, 0)
    for i in range(NX):
        stats_ref[i, 0:8, :] = high_s[...]
        stats_ref[i, 8:16, :] = mass_s[...]
        stats_ref[i, 16:24, :] = cross_s[...]


def totals_kernel(pairs_ref, stats_ref, part_ref, part_high_ref, total_ref, lse_ref, delta_ref):
    x = lax.axis_index("x")
    high = stats_ref[0, 0:8, :]
    for i in range(1, NX):
        high = jnp.maximum(high, stats_ref[i, 0:8, :])
    mass, cross = jnp.zeros_like(high), jnp.zeros_like(high)
    for i in range(NX):
        factor = jnp.exp(stats_ref[i, 0:8, :] - high)
        mass = mass + stats_ref[i, 8:16, :] * factor
        cross = cross + stats_ref[i, 16:24, :] * factor
    lse_ref[...] = high + jnp.log(mass)
    delta_ref[...] = cross / mass
    heads = jnp.where(iota((LANES, HD), 1) % HEADS == iota((LANES, HD), 0) // SPAN, 1.0, 0.0).astype(f32)
    chunks = pairs_ref[PAIRS - 1] // 2
    row = iota((8, LANES), 0)
    group = iota((1, HD), 1) // HEADS

    def step(t, total):
        rows, blocks = [], []
        for u in range(TOGETHER):
            chunk = jnp.minimum(TOGETHER * t + u, chunks - 1)
            first, second = pairs_ref[2 * chunk], pairs_ref[2 * chunk + 1]
            at = pl.ds(shared_span(x, (first % DEAD) // BLOCKS), 1)
            scale = jnp.exp(part_high_ref[chunk] - lse_ref[at, :])
            rows.append(scale * part_ref[chunk] * jnp.where(row < 4, -delta_ref[at, :], 1.0))
            none = jnp.where(TOGETHER * t + u < chunks, 0, HD)
            blocks.append((first % BLOCKS + none, second % BLOCKS + none))
        sums = exact_dot(jnp.concatenate(rows, axis=0), heads)
        for u in range(TOGETHER):
            for i in range(4):
                one = sums[8 * u + i : 8 * u + i + 1] + sums[8 * u + i + 4 : 8 * u + i + 5]
                total = total + jnp.where(group == blocks[u][i // 2] + (i % 2) * BLOCKS, one, 0.0)
        return total

    total = lax.fori_loop(0, (chunks + TOGETHER - 1) // TOGETHER, step, jnp.zeros((1, HD), f32))
    total_ref[...] = jnp.broadcast_to(total, total_ref.shape)


def grads_kernel(
    order_ref, pairs_ref, lse_ref, delta_ref, keys_ref, queries_ref, grads_ref, qdecay_ref, qpos_ref, qdoc_ref,
    dq0, dq1, dq2, dq3, own_out, peer_out, own_col, peer_col,
    acc, dqt, col,
):
    x, c = lax.axis_index("x"), lax.axis_index("core")
    acc[...] = jnp.zeros_like(acc)
    dqt[...] = jnp.zeros_like(dqt)
    col[...] = jnp.zeros_like(col)

    def step(t, carry):
        parts = []
        for u in range(UNROLL):
            qspan, blocks, keys, live, scores, slopes = chunk_scores(
                order_ref, pairs_ref, UNROLL * t + u, x, keys_ref, queries_ref, grads_ref, qpos_ref, qdoc_ref
            )
            at = pl.ds(shared_span(x, qspan), 1)
            shift = qdecay_ref[pl.ds(qspan, 1), :] - lse_ref[at, :]
            probs = jnp.exp(jnp.where(live, scores * SCALE + shift, NEG))
            dscores = probs * (slopes - delta_ref[at, :])
            upper = dscores.astype(bf16)
            lower = (dscores - upper.astype(f32)).astype(bf16)
            queries = queries_ref[qspan]
            both = jnp.dot(upper, queries, preferred_element_type=f32)
            dv = jnp.dot(probs.astype(bf16), grads_ref[qspan], preferred_element_type=f32)
            column = both[:, HD : 2 * HD] + jnp.dot(lower, queries[:, HD : 2 * HD], preferred_element_type=f32)
            dq = lax.dot_general(
                jnp.concatenate([keys[:, 0:HD], keys[:, 0:HD]], axis=0),
                jnp.concatenate([upper, lower], axis=0),
                TN,
                preferred_element_type=f32,
            )
            parts.append((qspan, blocks, both[:, 0:HD], dv, column, dq))
        group = iota((ROWS, HD), 1) // HEADS
        for qspan, blocks, dk, dv, column, dq in parts:
            dqt[qspan] += dq
            for u, block in enumerate(blocks):
                rows = slice(u * ROWS, (u + 1) * ROWS)
                acc[block, :, 0:HD] += dk[rows]
                acc[block, :, HD : 2 * HD] += dv[rows]
                col[...] += jnp.where(group == block, column[rows], 0.0)
        return carry

    lax.fori_loop(0, (pairs_ref[PAIRS - 1] + 2 * UNROLL - 1) // (2 * UNROLL), step, 0)
    for q in range(QSPANS):
        whole = dqt[q].T
        begin = (q % 2) * SPAN
        for h in range(HEADS):
            (dq0, dq1, dq2, dq3)[q // 2][begin : begin + SPAN, h * HD : (h + 1) * HD] = whole[h * SPAN : (h + 1) * SPAN]
    col[...] = col[...].T
    half = NZ * HEADS
    own_col[...] = col[pl.ds(pl.multiple_of(c * half, half), half), :]
    peer_col[...] = col[pl.ds(pl.multiple_of((1 - c) * half, half), half), :]
    for i in range(NZ):
        own_out[i] = acc[c * NZ + i]
        peer_out[i] = acc[(1 - c) * NZ + i]


def send_grads_kernel(own_ref, peer_ref, own_col, peer_col, mine_ref, other_ref, out_ref):
    x = lax.axis_index("x")
    row = iota((8, HD), 0)
    totals = jnp.zeros((8, HD), f32)
    for k in range(NX):
        both = mine_ref[8 * k : 8 * k + 8, :] + other_ref[8 * k : 8 * k + 8, :]
        totals = jnp.where(row == 2 * ((x + NX - k) % NX), both, totals)
    high, middle, low = three_terms(totals)
    right = jnp.concatenate([high + pltpu.roll(middle, 1, 0), low], axis=0)
    columns = own_col[...] + peer_col[...]
    for i in range(NZ):
        out_ref[i, 0:ROWS, :] = (own_ref[i] + peer_ref[i]).astype(bf16)
        group = columns[8 * (i // 2) : 8 * (i // 2) + 8]
        if i % 2:
            group = pltpu.roll(group, HEADS, 0)
        high, middle, low = three_terms(group)
        left = jnp.concatenate([jnp.where(row < HEADS, high, pltpu.roll(middle, HEADS, 0)), low], axis=0)
        out_ref[i, ROWS : ROWS + EXTRA, :] = jnp.concatenate([left, right], axis=1).astype(bf16)


def sum_queries_kernel(dq0, dq1, dq2, dq3, query_ref):
    query_ref[...] = (((dq0[...] + dq1[...]) + (dq2[...] + dq3[...])) * SCALE).astype(bf16)


def finish_kernel(order_ref, span_ref, in_ref, key_ref, value_ref, forget_ref):
    first = ((lax.axis_index("z") * NX + lax.axis_index("x")) * NC + lax.axis_index("core")) * 2
    total = in_ref[0].astype(f32)
    for i in range(1, NZ):
        total = total + in_ref[i].astype(f32)
    key_ref[...] = (total[0:ROWS, 0:HD] * SCALE).astype(bf16)
    value_ref[...] = total[0:ROWS, HD : 2 * HD].astype(bf16)
    extra = total[ROWS : ROWS + EXTRA]
    left, right = extra[:, 0:HD], extra[:, HD : 2 * HD]
    columns = left[0:8] + pltpu.roll(left[0:8], HEADS, 0) + left[8:16]
    totals = right[0:8] + pltpu.roll(right[0:8], 7, 0) + right[8:16]
    row, column = iota((8, HD), 0), iota((8, HD), 1)
    after = []
    for h in range(2):
        later = span_ref[...] > order_ref[first + h]
        line = jnp.sum(jnp.where(later, totals, 0.0), axis=0, keepdims=True)
        after.append(jnp.sum(jnp.where(column % HEADS == row, line, 0.0), axis=1, keepdims=True))
    within = exact_dot(columns, same_span_from(ROWS))
    within = within + jnp.where(column < SPAN, after[0], after[1])
    forget_ref[...] = -within[0:HEADS]


def call(kernel, specs, outs, scratch, flops, *args):
    place = {"s": pl.BlockSpec(memory_space=pltpu.SMEM), "v": pl.BlockSpec(memory_space=pltpu.VMEM)}
    return pl.pallas_call(
        kernel,
        in_specs=[place[k] for k in specs],
        out_specs=[place[k] for k, _, _ in outs],
        out_shape=[jax.ShapeDtypeStruct(shape, dtype) for _, shape, dtype in outs],
        scratch_shapes=[pltpu.VMEM(shape, dtype) for shape, dtype in scratch],
        compiler_params=pltpu.CompilerParams(vmem_limit_bytes=VMEM_LIMIT),
        cost_estimate=pl.CostEstimate(flops=flops, bytes_accessed=4 << 20, transcendentals=0),
    )(*args)


def body(queries, keys, values, out_grad, gate_logits, doc_lengths, span_order):
    swap = [(0, 1), (1, 0)]
    log_forget = jax.nn.log_sigmoid(gate_logits).T.reshape(NY, HEADS, 32)
    log_forget = jnp.pad(log_forget, ((0, 0), (0, 8 - HEADS), (0, HD - 32)))
    log_forget = jnp.broadcast_to(log_forget[None], (NX, NY, 8, HD)).reshape(NX * NY, 8, HD)
    log_forget, keys, values = lax.optimization_barrier((log_forget, keys, values))
    logs = lax.all_to_all(log_forget, ("x", "head"), 0, 0)
    key_rows = jnp.concatenate([keys, values], axis=1)
    logs, key_rows = lax.optimization_barrier((logs, key_rows))
    message = (NZ, ROWS + EXTRA, 2 * HD)
    key_message, own_sums = call(
        send_keys_kernel,
        "vv",
        [("v", message, bf16), ("v", (NX * HEADS, ROWS), f32)],
        [],
        0,
        logs, key_rows,
    )

    key_message, queries, out_grad, span_order, doc_lengths = lax.optimization_barrier(
        (key_message, queries, out_grad, span_order, doc_lengths)
    )
    pair_rows = jnp.concatenate([queries, out_grad], axis=1)
    order4 = span_order.reshape(NZ, NX, NC, 2).transpose(3, 2, 0, 1)
    order_line = jnp.broadcast_to(order4[..., None], (2, NC, NZ, NX, HEADS)).reshape(2, NC * NZ * NX * HEADS)
    order_spans = jnp.broadcast_to(order4.transpose(3, 0, 1, 2)[..., None], (NX, 2, NC, NZ, HEADS)).reshape(NX, 1, HD)
    order_spans = jnp.concatenate([order_spans, jnp.full_like(order_spans, -1)], axis=1).reshape(2 * NX, HD)
    own = lax.all_to_all(key_message, "z", 0, 0)
    query_rows = [pair_rows]
    for k in range(1, NX):
        query_rows.append(lax.ppermute(pair_rows, "x", [(i, (i + k) % NX) for i in range(NX)]))
    plan = call(
        plan_kernel,
        "ssv",
        [
            ("v", (TARGETS, 2 * SOURCES), bf16),
            ("v", (3 * KEY_ROWS, 2 * HD), bf16),
            ("v", (QSPANS, LANES), i32),
            ("v", (QSPANS, LANES), i32),
            ("s", (PAIRS,), i32),
        ],
        [],
        1 << 28,
        span_order, doc_lengths, order_line,
    )
    own, query_rows, plan, order_spans = lax.optimization_barrier((own, query_rows, plan, order_spans))
    earlier, select, qpos, qdoc, pairs = plan
    peer = lax.ppermute(own, "core", swap)

    line = ((QSPANS, LANES), f32)
    stats, *rows, qdecay, part, part_high = call(
        stats_kernel,
        "ssvvvvvvvvvvv",
        [
            ("v", (NX, 24, LANES), f32),
            ("v", (BLOCKS, ROWS, 3 * HD), bf16),
            ("v", (QSPANS, LANES, 2 * HD), bf16),
            ("v", (QSPANS, LANES, HD), bf16),
            ("v", (QSPANS, LANES), f32),
            ("v", (CHUNKS, 8, LANES), f32),
            ("v", (CHUNKS, 8, LANES), f32),
        ],
        [((BLOCKS, 8, ROWS), f32), ((BLOCKS, EXTRA, HD), bf16), ((NX * HEADS, ROWS), f32), line, line, line],
        1 << 28,
        span_order, pairs, earlier, select, qpos, qdoc, own_sums, own, peer, *query_rows,
    )
    all_stats = lax.all_to_all(stats, "x", 0, 0)
    total, lse, delta = call(
        totals_kernel,
        "svvv",
        [("v", (8, HD), f32), ("v", (QSPANS, LANES), f32), ("v", (QSPANS, LANES), f32)],
        [],
        0,
        pairs, all_stats, part, part_high,
    )
    totals = [total]
    for k in range(1, NX):
        totals.append(lax.ppermute(total, "x", [(i, (i + k) % NX) for i in range(NX)]))
    results = call(
        grads_kernel,
        "ssvvvvvvvv",
        [
            *[("v", (ROWS, HEADS * HD), f32)] * NX,
            ("v", (NZ, ROWS, 2 * HD), f32),
            ("v", (NZ, ROWS, 2 * HD), f32),
            ("v", (NZ * HEADS, ROWS), f32),
            ("v", (NZ * HEADS, ROWS), f32),
        ],
        [((BLOCKS, ROWS, 2 * HD), f32), ((QSPANS, HD, LANES), f32), ((ROWS, ROWS), f32)],
        1 << 29,
        span_order, pairs, lse, delta, *rows, qdecay, qpos, qdoc,
    )
    totals, results = lax.optimization_barrier((totals, results))
    dq0, dq1, dq2, dq3, own_sum, peer_sum, own_col, peer_col = results
    peer_sum = lax.ppermute(peer_sum, "core", swap)
    peer_col = lax.ppermute(peer_col, "core", swap)
    totals = jnp.concatenate(totals, axis=0)
    peer_totals = lax.ppermute(totals, "core", swap)
    (grad_message,) = call(
        send_grads_kernel,
        "vvvvvv",
        [("v", (NZ, ROWS + EXTRA, 2 * HD), bf16)],
        [],
        0,
        own_sum, peer_sum, own_col, peer_col, totals, peer_totals,
    )
    grad_message, dq1, dq2, dq3 = lax.optimization_barrier((grad_message, dq1, dq2, dq3))
    back = lax.all_to_all(grad_message, "z", 0, 0)
    parts = [
        lax.ppermute(part, "x", [(i, (i - k) % NX) for i in range(NX)]) for k, part in ((1, dq1), (2, dq2), (3, dq3))
    ]
    (query_grad,) = call(
        sum_queries_kernel, "vvvv", [("v", (ROWS, HEADS * HD), bf16)], [], 0, dq0, *parts
    )
    back, query_grad = lax.optimization_barrier((back, query_grad))
    key_grad, value_grad, forget_grad = call(
        finish_kernel,
        "svv",
        [
            ("v", (ROWS, HD), bf16),
            ("v", (ROWS, HD), bf16),
            ("v", (HEADS, ROWS), f32),
        ],
        [],
        0,
        span_order, order_spans, back,
    )
    return query_grad, key_grad, value_grad, forget_grad.T


def solution(mesh):
    fine = Mesh(mesh.devices.reshape(NZ, NX, NC, NY), ("z", "x", "core", "head"))
    ctx = ("z", "x", "core")
    rows = P(ctx, "head")
    return jax.shard_map(
        body,
        mesh=fine,
        in_specs=(rows, rows, rows, rows, P((*ctx, "head"), None), P(), P()),
        out_specs=(rows, rows, rows, rows),
        check_vma=False,
    )
```

```python
import functools
import math

import jax
import jax.numpy as jnp
from jax import lax
from jax.experimental import pallas as pl
from jax.experimental.pallas import tpu as pltpu
from jax.sharding import Mesh, PartitionSpec as P

NZ, NX, NC, NY = 8, 4, 2, 4
ROWS, SPAN, HEADS, HD = 128, 64, 4, 128
DOCS = 16
BLOCKS = NC * NZ
KEY_ROWS = BLOCKS * 8
SOURCES = BLOCKS * NX * HEADS
TARGETS = 2 * KEY_ROWS + 2 * NX * HEADS
QSPANS = 2 * NX
LANES = HEADS * SPAN
EXTRA = 16
DEAD = QSPANS * BLOCKS
STREAM = 8192
UNROLL = 4
PAIRS = DEAD + 2 * UNROLL + 1
CHUNKS = DEAD // 2 + UNROLL
TOGETHER = 8
NEG = -1e30
SCALE = 1.0 / math.sqrt(HD)
f32, bf16, i32 = jnp.float32, jnp.bfloat16, jnp.int32
VMEM_LIMIT = 16 * 1024 * 1024
NT = (((1,), (1,)), ((), ()))
TN = (((0,), (0,)), ((), ()))


def three_terms(a):
    high = a.astype(bf16).astype(f32)
    rest = a - high
    middle = rest.astype(bf16).astype(f32)
    return high, middle, rest - middle


def exact_dot(a, ones):
    terms = jnp.concatenate(three_terms(a), axis=0).astype(bf16)
    terms = jnp.dot(terms, ones.astype(bf16), preferred_element_type=f32)
    rows = a.shape[0]
    return terms[0:rows] + terms[rows : 2 * rows] + terms[2 * rows : 3 * rows]


def iota(shape, dim):
    return lax.broadcasted_iota(i32, shape, dim)


def same_span_upto(n):
    row, column = iota((n, n), 0), iota((n, n), 1)
    return jnp.where((row <= column) & (row // SPAN == column // SPAN), 1.0, 0.0).astype(f32)


def same_span_from(n):
    row, column = iota((n, n), 0), iota((n, n), 1)
    return jnp.where((row >= column) & (row // SPAN == column // SPAN), 1.0, 0.0).astype(f32)


def send_gates_kernel(gate_ref, out_ref):
    gates = gate_ref[...]
    small = jnp.exp(-jnp.abs(gates))
    w = 1.0 + small
    one = w == 1.0
    log_one_plus = jnp.where(one, small, jnp.log(w) * (small / jnp.where(one, 1.0, w - 1.0)))
    logs = jnp.minimum(gates, 0.0) - log_one_plus
    logs = jnp.concatenate([logs, jnp.zeros((NY * HEADS, HD - logs.shape[1]), f32)], axis=1)
    row = iota((8, HD), 0)
    for y in range(NY):
        group = logs[8 * (y // 2) : 8 * (y // 2) + 8]
        if y % 2:
            group = pltpu.roll(group, HEADS, 0)
        group = jnp.where(row < HEADS, group, 0.0)
        for x in range(NX):
            out_ref[x * NY + y] = group


def send_keys_kernel(log_ref, rows_ref, out_ref, sums_ref):
    parts = []
    for x in range(NX):
        total = log_ref[x * NY]
        for y in range(1, NY):
            total = total + pltpu.roll(log_ref[x * NY + y], 32 * y, 1)
        parts.append(total)
    logs = jnp.concatenate(
        [parts[0] + pltpu.roll(parts[1], HEADS, 0), parts[2] + pltpu.roll(parts[3], HEADS, 0)], axis=0
    )
    sums = exact_dot(logs, same_span_upto(ROWS))
    sums_ref[...] = sums
    x = lax.axis_index("x")
    row = iota((8, HD), 0)
    own = jnp.zeros((8, HD), f32)
    for h in range(HEADS):
        own = jnp.where(row == h, sums_ref[pl.ds(x * HEADS + h, 1), :], own)
    high, middle, low = three_terms(own)
    left = jnp.concatenate([high + pltpu.roll(middle, HEADS, 0), low], axis=0)
    terms = jnp.concatenate(three_terms(sums), axis=1).astype(bf16)
    row, column = iota((3 * HD, HD), 0), iota((3 * HD, HD), 1)
    wanted = (column // 2) * HD + (column % 2) * SPAN + SPAN - 1
    pick = jnp.where((row == wanted) & (column < 6), 1.0, 0.0).astype(bf16)
    right = jnp.dot(terms, pick, preferred_element_type=f32)
    extra = jnp.concatenate([left, right], axis=1).astype(bf16)
    rows = rows_ref[...]
    for i in range(NZ):
        out_ref[i, 0:ROWS, :] = rows
        out_ref[i, ROWS : ROWS + EXTRA, :] = extra


def gather_queries(refs, queries_ref, grads_ref):
    heads = jnp.where(iota((LANES, HD), 1) % HEADS == iota((LANES, HD), 0) // SPAN, 1.0, 0.0).astype(bf16)
    for k, ref in enumerate(refs):
        for half in range(2):
            rows = slice(half * SPAN, (half + 1) * SPAN)
            queries_ref[2 * k + half, :, HD : 2 * HD] = heads
            for h in range(HEADS):
                to = slice(h * SPAN, (h + 1) * SPAN)
                queries_ref[2 * k + half, to, 0:HD] = ref[rows, h * HD : (h + 1) * HD]
                grads_ref[2 * k + half, to, :] = ref[rows, (HEADS + h) * HD : (HEADS + h + 1) * HD]


def shared_span(x, q):
    return 2 * ((x + NX - q // 2) % NX) + q % 2


def spans_of_block(order_ref, x, block):
    first = ((block % NZ) * (NX * NC) + x * NC + block // NZ) * 2
    return order_ref[first], order_ref[first + 1]


def span_of_query(order_ref, z, x, c, q):
    return order_ref[((z * NX + (x + NX - q // 2) % NX) * NC + c) * 2 + q % 2]


def chunk_scores(order_ref, pairs_ref, t, x, keys_ref, queries_ref, grads_ref, qpos_ref, qdoc_ref):
    pairs = [pairs_ref[2 * t + u] for u in range(2)]
    blocks = [pair % BLOCKS for pair in pairs]
    qspan = (pairs[0] % DEAD) // BLOCKS
    keys = jnp.concatenate([keys_ref[block, :, 0 : 2 * HD] for block in blocks], axis=0)
    values = jnp.concatenate([keys_ref[block, :, 2 * HD : 3 * HD] for block in blocks], axis=0)
    scores = lax.dot_general(keys, queries_ref[qspan], NT, preferred_element_type=f32)
    slopes = lax.dot_general(values, grads_ref[qspan], NT, preferred_element_type=f32)
    at = pl.ds(qspan, 1)
    qpos, qdoc = qpos_ref[at, :][:, 0:HD], qdoc_ref[at, :][:, 0:HD]
    row = iota((ROWS, HD), 0)
    live = []
    for pair, block in zip(pairs, blocks):
        even, odd = spans_of_block(order_ref, x, block)
        even = jnp.where(pair < DEAD, even, 2 * STREAM)
        odd = jnp.where(pair < DEAD, odd, 2 * STREAM)
        key_pos = row + jnp.where(row < SPAN, even * SPAN, odd * SPAN - SPAN)
        half = (key_pos <= qpos) & (key_pos >= qdoc)
        live.append(jnp.concatenate([half, half], axis=1))
    return qspan, blocks, keys, jnp.concatenate(live, axis=0), scores, slopes


def plan_kernel(order_ref, length_ref, line_ref, earlier_ref, select_ref, qpos_ref, qdoc_ref, pairs_ref):
    z, x, c = lax.axis_index("z"), lax.axis_index("x"), lax.axis_index("core")
    row = iota((KEY_ROWS, 1), 0)
    targets = []
    for half in range(2):
        target = jnp.zeros((KEY_ROWS, 1), i32)
        for block in range(BLOCKS):
            target = jnp.where(row // 8 == block, spans_of_block(order_ref, x, block)[half], target)
        targets.append(target)
    row = iota((NX * HEADS, 1), 0)
    for half in range(2):
        target = jnp.zeros((NX * HEADS, 1), i32)
        for i in range(NX):
            target = jnp.where(row // HEADS == i, order_ref[((z * NX + i) * NC + c) * 2 + half], target)
        targets.append(target)
    target = jnp.concatenate(targets, axis=0)
    source = jnp.concatenate([line_ref[0:1, :], line_ref[1:2, :]], axis=1)
    shape = (TARGETS, 2 * SOURCES)
    earlier = (source < target) & (iota(shape, 0) % HEADS == iota(shape, 1) % HEADS)
    earlier_ref[...] = jnp.where(earlier, 1.0, 0.0).astype(bf16)
    row, column = iota((3 * KEY_ROWS, 2 * HD), 0), iota((3 * KEY_ROWS, 2 * HD), 1)
    term = (column % 16) // HEADS
    wanted = term * KEY_ROWS + (column // 16) * 8 + column % HEADS
    select_ref[...] = jnp.where((row == wanted) & (term < 3), 1.0, 0.0).astype(bf16)
    row, column = iota((QSPANS, LANES), 0), iota((QSPANS, LANES), 1)
    qpos = column % SPAN
    spans = []
    for q in range(QSPANS):
        spans.append(span_of_query(order_ref, z, x, c, q))
        qpos = qpos + jnp.where(row == q, spans[q] * SPAN, 0)
    starts = [jnp.int32(0)]
    for doc in range(DOCS - 1):
        starts.append(starts[-1] + length_ref[doc])
    qdoc = jnp.zeros((QSPANS, LANES), i32)
    for start in starts:
        qdoc = jnp.where(qpos >= start, start, qdoc)
    qpos_ref[...] = qpos
    qdoc_ref[...] = qdoc
    found = jnp.int32(0)
    for q in range(QSPANS):
        mine, begin = spans[q], jnp.int32(0)
        for start in starts:
            begin = jnp.where(mine * SPAN >= start, start, begin)

        def scan(block, found, q=q, mine=mine, begin=begin):
            even, odd = spans_of_block(order_ref, x, block)
            live = ((even <= mine) & (even * SPAN + SPAN > begin)) | ((odd <= mine) & (odd * SPAN + SPAN > begin))
            pairs_ref[found] = q * BLOCKS + block
            return found + live.astype(i32)

        found = lax.fori_loop(0, BLOCKS, scan, found, unroll=8)
        pairs_ref[found] = DEAD + q * BLOCKS
        found = found + found % 2
    for i in range(2 * UNROLL):
        pairs_ref[found + i] = DEAD
    pairs_ref[PAIRS - 1] = found


def stats_kernel(
    order_ref, pairs_ref, earlier_ref, select_ref, qpos_ref, qdoc_ref, sums_ref, own_ref, peer_ref, qd0, qd1, qd2, qd3,
    stats_ref, keys_ref, queries_ref, grads_ref, qdecay_ref, part_ref, part_high_ref,
    decay, totals, qsums, high_s, mass_s, cross_s,
):
    z, x, c = lax.axis_index("z"), lax.axis_index("x"), lax.axis_index("core")
    gather_queries((qd0, qd1, qd2, qd3), queries_ref, grads_ref)
    for i in range(NZ):
        for ref, core in ((own_ref, c), (peer_ref, 1 - c)):
            block = core * NZ + i
            keys_ref[block, :, 0:HD] = ref[i, 0:ROWS, 0:HD]
            keys_ref[block, :, 2 * HD : 3 * HD] = ref[i, 0:ROWS, HD : 2 * HD]
            totals[block] = ref[i, ROWS : ROWS + EXTRA, HD : 2 * HD]
            terms = ref[i, ROWS : ROWS + EXTRA, 0:HD].astype(f32)
            decay[block] = terms[0:8] + pltpu.roll(terms[0:8], HEADS, 0) + terms[8:16]
    sources = totals[...].reshape(SOURCES, HD)
    first = jnp.dot(earlier_ref[:, 0:SOURCES], sources, preferred_element_type=f32)
    second = jnp.dot(earlier_ref[:, SOURCES : 2 * SOURCES], sources, preferred_element_type=f32)
    lane = iota((TARGETS, HD), 1)
    both = jnp.where(lane < 6, jnp.where(lane % 2 == 0, first, second), 0.0)
    before = jnp.sum(both, axis=1, keepdims=True)
    left = iota((KEY_ROWS, ROWS), 1) < SPAN
    sums = decay[...].reshape(KEY_ROWS, ROWS) + jnp.where(left, before[0:KEY_ROWS], before[KEY_ROWS : 2 * KEY_ROWS])
    own, rows = before[2 * KEY_ROWS :], NX * HEADS
    qsums[...] = sums_ref[...] + jnp.where(iota((rows, ROWS), 1) < SPAN, own[0:rows], own[rows : 2 * rows])
    terms = jnp.concatenate(three_terms(sums * (-1.0 / SCALE)), axis=0).astype(bf16)
    terms = lax.dot_general(terms, select_ref[...], TN, preferred_element_type=f32)
    group = iota((ROWS, HD), 1) // 16
    for block in range(BLOCKS):
        tile = terms[:, (block // 8) * HD : (block // 8 + 1) * HD]
        keys_ref[block, :, HD : 2 * HD] = jnp.where(group == block % 8, tile, 0.0).astype(bf16)
    for k in range(NX):
        for h in range(HEADS):
            own = qsums[pl.ds(((x + NX - k) % NX) * HEADS + h, 1), :]
            for half in range(2):
                qdecay_ref[2 * k + half : 2 * k + half + 1, h * SPAN : (h + 1) * SPAN] = own[
                    :, half * SPAN : (half + 1) * SPAN
                ]
    high_s[...] = jnp.full((QSPANS, LANES), NEG, f32)
    mass_s[...] = jnp.zeros((QSPANS, LANES), f32)
    cross_s[...] = jnp.zeros((QSPANS, LANES), f32)

    def step(t, carry):
        parts = []
        for u in range(UNROLL):
            qspan, _, _, live, scores, slopes = chunk_scores(
                order_ref, pairs_ref, UNROLL * t + u, x, keys_ref, queries_ref, grads_ref, qpos_ref, qdoc_ref
            )
            scores = jnp.where(live, scores * SCALE + qdecay_ref[pl.ds(qspan, 1), :], NEG)
            high = jnp.max(scores, axis=0, keepdims=True)
            weights = jnp.exp(scores - high)
            sums, row = jnp.zeros((8, LANES), f32), iota((8, LANES), 0)
            for first, array in ((0, weights), (4, weights * slopes)):
                for i in range(4):
                    one = jnp.sum(array[i * SPAN : (i + 1) * SPAN], axis=0, keepdims=True)
                    sums = jnp.where(row == first + i, one, sums)
            part_ref[UNROLL * t + u] = sums
            part_high_ref[UNROLL * t + u] = jnp.broadcast_to(high, (8, LANES))
            parts.append(
                (qspan, high, jnp.sum(sums[0:4], axis=0, keepdims=True), jnp.sum(sums[4:8], axis=0, keepdims=True))
            )
        for qspan, high, mass, cross in parts:
            at = pl.ds(shared_span(x, qspan), 1)
            old = high_s[at, :]
            new = jnp.maximum(old, high)
            before, now = jnp.exp(old - new), jnp.exp(high - new)
            high_s[at, :] = new
            mass_s[at, :] = mass_s[at, :] * before + mass * now
            cross_s[at, :] = cross_s[at, :] * before + cross * now
        return carry

    lax.fori_loop(0, (pairs_ref[PAIRS - 1] + 2 * UNROLL - 1) // (2 * UNROLL), step, 0)
    stats_ref[0:8, :] = high_s[...]
    stats_ref[8:16, :] = mass_s[...]
    stats_ref[16:24, :] = cross_s[...]


def totals_kernel(pairs_ref, stats0, stats1, stats2, stats3, part_ref, part_high_ref, total_ref, lse_ref, delta_ref):
    x = lax.axis_index("x")
    stats = [(ref[0:8, :], ref[8:16, :], ref[16:24, :]) for ref in (stats0, stats1, stats2, stats3)]
    high = stats[0][0]
    for one, _, _ in stats[1:]:
        high = jnp.maximum(high, one)
    mass, cross = jnp.zeros_like(high), jnp.zeros_like(high)
    for one, one_mass, one_cross in stats:
        factor = jnp.exp(one - high)
        mass = mass + one_mass * factor
        cross = cross + one_cross * factor
    lse_ref[...] = high + jnp.log(mass)
    delta_ref[...] = cross / mass
    heads = jnp.where(iota((LANES, HD), 1) % HEADS == iota((LANES, HD), 0) // SPAN, 1.0, 0.0).astype(f32)
    chunks = pairs_ref[PAIRS - 1] // 2
    row = iota((8, LANES), 0)
    group = iota((1, HD), 1) // HEADS

    def step(t, total):
        rows, blocks = [], []
        for u in range(TOGETHER):
            chunk = jnp.minimum(TOGETHER * t + u, chunks - 1)
            first, second = pairs_ref[2 * chunk], pairs_ref[2 * chunk + 1]
            at = pl.ds(shared_span(x, (first % DEAD) // BLOCKS), 1)
            scale = jnp.exp(part_high_ref[chunk] - lse_ref[at, :])
            rows.append(scale * part_ref[chunk] * jnp.where(row < 4, -delta_ref[at, :], 1.0))
            none = jnp.where(TOGETHER * t + u < chunks, 0, HD)
            blocks.append((first % BLOCKS + none, second % BLOCKS + none))
        sums = exact_dot(jnp.concatenate(rows, axis=0), heads)
        for u in range(TOGETHER):
            for i in range(4):
                one = sums[8 * u + i : 8 * u + i + 1] + sums[8 * u + i + 4 : 8 * u + i + 5]
                total = total + jnp.where(group == blocks[u][i // 2] + (i % 2) * BLOCKS, one, 0.0)
        return total

    total = lax.fori_loop(0, (chunks + TOGETHER - 1) // TOGETHER, step, jnp.zeros((1, HD), f32))
    total_ref[...] = jnp.broadcast_to(total, total_ref.shape)


def grads_kernel(
    order_ref, pairs_ref, lse_ref, delta_ref, keys_ref, queries_ref, grads_ref, qdecay_ref, qpos_ref, qdoc_ref,
    dq0, dq1, dq2, dq3, own_out, peer_out, own_col, peer_col,
    acc, dqt, col,
):
    x, c = lax.axis_index("x"), lax.axis_index("core")
    acc[...] = jnp.zeros_like(acc)
    dqt[...] = jnp.zeros_like(dqt)
    col[...] = jnp.zeros_like(col)

    def step(t, carry):
        parts = []
        for u in range(UNROLL):
            qspan, blocks, keys, live, scores, slopes = chunk_scores(
                order_ref, pairs_ref, UNROLL * t + u, x, keys_ref, queries_ref, grads_ref, qpos_ref, qdoc_ref
            )
            at = pl.ds(shared_span(x, qspan), 1)
            shift = qdecay_ref[pl.ds(qspan, 1), :] - lse_ref[at, :]
            probs = jnp.exp(jnp.where(live, scores * SCALE + shift, NEG))
            dscores = probs * (slopes - delta_ref[at, :])
            upper = dscores.astype(bf16)
            lower = (dscores - upper.astype(f32)).astype(bf16)
            queries = queries_ref[qspan]
            both = jnp.dot(upper, queries, preferred_element_type=f32)
            dv = jnp.dot(probs.astype(bf16), grads_ref[qspan], preferred_element_type=f32)
            column = both[:, HD : 2 * HD] + jnp.dot(lower, queries[:, HD : 2 * HD], preferred_element_type=f32)
            dq = lax.dot_general(
                jnp.concatenate([keys[:, 0:HD], keys[:, 0:HD]], axis=0),
                jnp.concatenate([upper, lower], axis=0),
                TN,
                preferred_element_type=f32,
            )
            parts.append((qspan, blocks, both[:, 0:HD], dv, column, dq))
        group = iota((ROWS, HD), 1) // HEADS
        for qspan, blocks, dk, dv, column, dq in parts:
            dqt[qspan] += dq
            for u, block in enumerate(blocks):
                rows = slice(u * ROWS, (u + 1) * ROWS)
                acc[block, :, 0:HD] += dk[rows]
                acc[block, :, HD : 2 * HD] += dv[rows]
                col[...] += jnp.where(group == block, column[rows], 0.0)
        return carry

    lax.fori_loop(0, (pairs_ref[PAIRS - 1] + 2 * UNROLL - 1) // (2 * UNROLL), step, 0)
    for q in range(QSPANS):
        whole = dqt[q].T
        begin = (q % 2) * SPAN
        for h in range(HEADS):
            (dq0, dq1, dq2, dq3)[q // 2][begin : begin + SPAN, h * HD : (h + 1) * HD] = whole[h * SPAN : (h + 1) * SPAN]
    col[...] = col[...].T
    half = NZ * HEADS
    own_col[...] = col[pl.ds(pl.multiple_of(c * half, half), half), :]
    peer_col[...] = col[pl.ds(pl.multiple_of((1 - c) * half, half), half), :]
    for i in range(NZ):
        own_out[i] = acc[c * NZ + i]
        peer_out[i] = acc[(1 - c) * NZ + i]


def send_grads_kernel(own_ref, peer_ref, own_col, peer_col, mine_ref, other_ref, out_ref):
    x = lax.axis_index("x")
    row = iota((8, HD), 0)
    totals = jnp.zeros((8, HD), f32)
    for k in range(NX):
        both = mine_ref[8 * k : 8 * k + 8, :] + other_ref[8 * k : 8 * k + 8, :]
        totals = jnp.where(row == 2 * ((x + NX - k) % NX), both, totals)
    high, middle, low = three_terms(totals)
    right = jnp.concatenate([high + pltpu.roll(middle, 1, 0), low], axis=0)
    columns = own_col[...] + peer_col[...]
    for i in range(NZ):
        out_ref[i, 0:ROWS, :] = (own_ref[i] + peer_ref[i]).astype(bf16)
        group = columns[8 * (i // 2) : 8 * (i // 2) + 8]
        if i % 2:
            group = pltpu.roll(group, HEADS, 0)
        high, middle, low = three_terms(group)
        left = jnp.concatenate([jnp.where(row < HEADS, high, pltpu.roll(middle, HEADS, 0)), low], axis=0)
        out_ref[i, ROWS : ROWS + EXTRA, :] = jnp.concatenate([left, right], axis=1).astype(bf16)


def sum_queries_kernel(dq0, dq1, dq2, dq3, query_ref):
    query_ref[...] = (((dq0[...] + dq1[...]) + (dq2[...] + dq3[...])) * SCALE).astype(bf16)


def finish_kernel(order_ref, span_ref, in_ref, key_ref, value_ref, forget_ref):
    first = ((lax.axis_index("z") * NX + lax.axis_index("x")) * NC + lax.axis_index("core")) * 2
    total = in_ref[0].astype(f32)
    for i in range(1, NZ):
        total = total + in_ref[i].astype(f32)
    key_ref[...] = (total[0:ROWS, 0:HD] * SCALE).astype(bf16)
    value_ref[...] = total[0:ROWS, HD : 2 * HD].astype(bf16)
    extra = total[ROWS : ROWS + EXTRA]
    left, right = extra[:, 0:HD], extra[:, HD : 2 * HD]
    columns = left[0:8] + pltpu.roll(left[0:8], HEADS, 0) + left[8:16]
    totals = right[0:8] + pltpu.roll(right[0:8], 7, 0) + right[8:16]
    row, column = iota((8, HD), 0), iota((8, HD), 1)
    after = []
    for h in range(2):
        later = span_ref[...] > order_ref[first + h]
        line = jnp.sum(jnp.where(later, totals, 0.0), axis=0, keepdims=True)
        after.append(jnp.sum(jnp.where(column % HEADS == row, line, 0.0), axis=1, keepdims=True))
    within = exact_dot(columns, same_span_from(ROWS))
    within = within + jnp.where(column < SPAN, after[0], after[1])
    forget_ref[...] = -within[0:HEADS]


def call(kernel, specs, outs, scratch, flops, *args):
    place = {"s": pl.BlockSpec(memory_space=pltpu.SMEM), "v": pl.BlockSpec(memory_space=pltpu.VMEM)}
    return pl.pallas_call(
        kernel,
        in_specs=[place[k] for k in specs],
        out_specs=[place[k] for k, _, _ in outs],
        out_shape=[jax.ShapeDtypeStruct(shape, dtype) for _, shape, dtype in outs],
        scratch_shapes=[pltpu.VMEM(shape, dtype) for shape, dtype in scratch],
        compiler_params=pltpu.CompilerParams(vmem_limit_bytes=VMEM_LIMIT),
        cost_estimate=pl.CostEstimate(flops=flops, bytes_accessed=4 << 20, transcendentals=0),
    )(*args)


def body(queries, keys, values, out_grad, gate_logits, doc_lengths, span_order):
    swap = [(0, 1), (1, 0)]
    (log_forget,) = call(send_gates_kernel, "v", [("v", (NX * NY, 8, HD), f32)], [], 0, gate_logits.T)
    log_forget, keys, values = lax.optimization_barrier((log_forget, keys, values))
    logs = lax.all_to_all(log_forget, ("x", "head"), 0, 0)
    key_rows = jnp.concatenate([keys, values], axis=1)
    logs, key_rows = lax.optimization_barrier((logs, key_rows))
    message = (NZ, ROWS + EXTRA, 2 * HD)
    key_message, own_sums = call(
        send_keys_kernel,
        "vv",
        [("v", message, bf16), ("v", (NX * HEADS, ROWS), f32)],
        [],
        0,
        logs, key_rows,
    )

    key_message, queries, out_grad, span_order, doc_lengths = lax.optimization_barrier(
        (key_message, queries, out_grad, span_order, doc_lengths)
    )
    pair_rows = jnp.concatenate([queries, out_grad], axis=1)
    order4 = span_order.reshape(NZ, NX, NC, 2).transpose(3, 2, 0, 1)
    order_line = jnp.broadcast_to(order4[..., None], (2, NC, NZ, NX, HEADS)).reshape(2, NC * NZ * NX * HEADS)
    order_spans = jnp.broadcast_to(order4.transpose(3, 0, 1, 2)[..., None], (NX, 2, NC, NZ, HEADS)).reshape(NX, 1, HD)
    order_spans = jnp.concatenate([order_spans, jnp.full_like(order_spans, -1)], axis=1).reshape(2 * NX, HD)
    own = lax.all_to_all(key_message, "z", 0, 0)
    query_rows = [pair_rows]
    for k in range(1, NX):
        query_rows.append(lax.ppermute(pair_rows, "x", [(i, (i + k) % NX) for i in range(NX)]))
    plan = call(
        plan_kernel,
        "ssv",
        [
            ("v", (TARGETS, 2 * SOURCES), bf16),
            ("v", (3 * KEY_ROWS, 2 * HD), bf16),
            ("v", (QSPANS, LANES), i32),
            ("v", (QSPANS, LANES), i32),
            ("s", (PAIRS,), i32),
        ],
        [],
        1 << 28,
        span_order, doc_lengths, order_line,
    )
    own, query_rows, plan, order_spans = lax.optimization_barrier((own, query_rows, plan, order_spans))
    earlier, select, qpos, qdoc, pairs = plan
    peer = lax.ppermute(own, "core", swap)

    line = ((QSPANS, LANES), f32)
    stats, *rows, qdecay, part, part_high = call(
        stats_kernel,
        "ssvvvvvvvvvvv",
        [
            ("v", (24, LANES), f32),
            ("v", (BLOCKS, ROWS, 3 * HD), bf16),
            ("v", (QSPANS, LANES, 2 * HD), bf16),
            ("v", (QSPANS, LANES, HD), bf16),
            ("v", (QSPANS, LANES), f32),
            ("v", (CHUNKS, 8, LANES), f32),
            ("v", (CHUNKS, 8, LANES), f32),
        ],
        [((BLOCKS, 8, ROWS), f32), ((BLOCKS, EXTRA, HD), bf16), ((NX * HEADS, ROWS), f32), line, line, line],
        1 << 28,
        span_order, pairs, earlier, select, qpos, qdoc, own_sums, own, peer, *query_rows,
    )
    all_stats = [stats]
    for k in range(1, NX):
        all_stats.append(lax.ppermute(stats, "x", [(i, (i + k) % NX) for i in range(NX)]))
    total, lse, delta = call(
        totals_kernel,
        "svvvvvv",
        [("v", (8, HD), f32), ("v", (QSPANS, LANES), f32), ("v", (QSPANS, LANES), f32)],
        [],
        0,
        pairs, *all_stats, part, part_high,
    )
    totals = [total]
    for k in range(1, NX):
        totals.append(lax.ppermute(total, "x", [(i, (i + k) % NX) for i in range(NX)]))
    results = call(
        grads_kernel,
        "ssvvvvvvvv",
        [
            *[("v", (ROWS, HEADS * HD), f32)] * NX,
            ("v", (NZ, ROWS, 2 * HD), f32),
            ("v", (NZ, ROWS, 2 * HD), f32),
            ("v", (NZ * HEADS, ROWS), f32),
            ("v", (NZ * HEADS, ROWS), f32),
        ],
        [((BLOCKS, ROWS, 2 * HD), f32), ((QSPANS, HD, LANES), f32), ((ROWS, ROWS), f32)],
        1 << 29,
        span_order, pairs, lse, delta, *rows, qdecay, qpos, qdoc,
    )
    totals, results = lax.optimization_barrier((totals, results))
    dq0, dq1, dq2, dq3, own_sum, peer_sum, own_col, peer_col = results
    peer_sum = lax.ppermute(peer_sum, "core", swap)
    peer_col = lax.ppermute(peer_col, "core", swap)
    totals = jnp.concatenate(totals, axis=0)
    peer_totals = lax.ppermute(totals, "core", swap)
    (grad_message,) = call(
        send_grads_kernel,
        "vvvvvv",
        [("v", (NZ, ROWS + EXTRA, 2 * HD), bf16)],
        [],
        0,
        own_sum, peer_sum, own_col, peer_col, totals, peer_totals,
    )
    grad_message, dq1, dq2, dq3 = lax.optimization_barrier((grad_message, dq1, dq2, dq3))
    back = lax.all_to_all(grad_message, "z", 0, 0)
    parts = [
        lax.ppermute(part, "x", [(i, (i - k) % NX) for i in range(NX)]) for k, part in ((1, dq1), (2, dq2), (3, dq3))
    ]
    (query_grad,) = call(
        sum_queries_kernel, "vvvv", [("v", (ROWS, HEADS * HD), bf16)], [], 0, dq0, *parts
    )
    back, query_grad = lax.optimization_barrier((back, query_grad))
    key_grad, value_grad, forget_grad = call(
        finish_kernel,
        "svv",
        [
            ("v", (ROWS, HD), bf16),
            ("v", (ROWS, HD), bf16),
            ("v", (HEADS, ROWS), f32),
        ],
        [],
        0,
        span_order, order_spans, back,
    )
    return query_grad, key_grad, value_grad, forget_grad.T


def solution(mesh):
    fine = Mesh(mesh.devices.reshape(NZ, NX, NC, NY), ("z", "x", "core", "head"))
    ctx = ("z", "x", "core")
    rows = P(ctx, "head")
    return jax.shard_map(
        body,
        mesh=fine,
        in_specs=(rows, rows, rows, rows, P((*ctx, "head"), None), P(), P()),
        out_specs=(rows, rows, rows, rows),
        check_vma=False,
    )
```

```python
import functools
import math

import jax
import jax.numpy as jnp
from jax import lax
from jax.experimental import pallas as pl
from jax.experimental.pallas import tpu as pltpu
from jax.sharding import Mesh, PartitionSpec as P

NZ, NX, NC, NY = 8, 4, 2, 4
ROWS, SPAN, HEADS, HD = 128, 64, 4, 128
DOCS = 16
BLOCKS = NC * NZ
KEY_ROWS = BLOCKS * 8
SOURCES = BLOCKS * NX * HEADS
TARGETS = 2 * KEY_ROWS + 2 * NX * HEADS
QSPANS = 2 * NX
LANES = HEADS * SPAN
EXTRA = 16
KSPANS = 2 * BLOCKS
WIDE = 4
DEAD = QSPANS * KSPANS
STREAM = 8192
UNROLL = 4
PAIRS = DEAD + WIDE * UNROLL + 1
CHUNKS = DEAD // WIDE + UNROLL
TOGETHER = 8
NEG = -1e30
SCALE = 1.0 / math.sqrt(HD)
f32, bf16, i32 = jnp.float32, jnp.bfloat16, jnp.int32
VMEM_LIMIT = 16 * 1024 * 1024
NT = (((1,), (1,)), ((), ()))
TN = (((0,), (0,)), ((), ()))


def three_terms(a):
    high = a.astype(bf16).astype(f32)
    rest = a - high
    middle = rest.astype(bf16).astype(f32)
    return high, middle, rest - middle


def exact_dot(a, ones):
    terms = jnp.concatenate(three_terms(a), axis=0).astype(bf16)
    terms = jnp.dot(terms, ones.astype(bf16), preferred_element_type=f32)
    rows = a.shape[0]
    return terms[0:rows] + terms[rows : 2 * rows] + terms[2 * rows : 3 * rows]


def iota(shape, dim):
    return lax.broadcasted_iota(i32, shape, dim)


def same_span_upto(n):
    row, column = iota((n, n), 0), iota((n, n), 1)
    return jnp.where((row <= column) & (row // SPAN == column // SPAN), 1.0, 0.0).astype(f32)


def same_span_from(n):
    row, column = iota((n, n), 0), iota((n, n), 1)
    return jnp.where((row >= column) & (row // SPAN == column // SPAN), 1.0, 0.0).astype(f32)


def send_gates_kernel(gate_ref, out_ref):
    gates = gate_ref[...]
    small = jnp.exp(-jnp.abs(gates))
    w = 1.0 + small
    one = w == 1.0
    log_one_plus = jnp.where(one, small, jnp.log(w) * (small / jnp.where(one, 1.0, w - 1.0)))
    logs = jnp.minimum(gates, 0.0) - log_one_plus
    logs = jnp.concatenate([logs, jnp.zeros((NY * HEADS, HD - logs.shape[1]), f32)], axis=1)
    row = iota((8, HD), 0)
    for y in range(NY):
        group = logs[8 * (y // 2) : 8 * (y // 2) + 8]
        if y % 2:
            group = pltpu.roll(group, HEADS, 0)
        group = jnp.where(row < HEADS, group, 0.0)
        for x in range(NX):
            out_ref[x * NY + y] = group


def send_keys_kernel(log_ref, rows_ref, out_ref, sums_ref):
    parts = []
    for x in range(NX):
        total = log_ref[x * NY]
        for y in range(1, NY):
            total = total + pltpu.roll(log_ref[x * NY + y], 32 * y, 1)
        parts.append(total)
    logs = jnp.concatenate(
        [parts[0] + pltpu.roll(parts[1], HEADS, 0), parts[2] + pltpu.roll(parts[3], HEADS, 0)], axis=0
    )
    sums = exact_dot(logs, same_span_upto(ROWS))
    sums_ref[...] = sums
    x = lax.axis_index("x")
    row = iota((8, HD), 0)
    own = jnp.zeros((8, HD), f32)
    for h in range(HEADS):
        own = jnp.where(row == h, sums_ref[pl.ds(x * HEADS + h, 1), :], own)
    high, middle, low = three_terms(own)
    left = jnp.concatenate([high + pltpu.roll(middle, HEADS, 0), low], axis=0)
    terms = jnp.concatenate(three_terms(sums), axis=1).astype(bf16)
    row, column = iota((3 * HD, HD), 0), iota((3 * HD, HD), 1)
    wanted = (column // 2) * HD + (column % 2) * SPAN + SPAN - 1
    pick = jnp.where((row == wanted) & (column < 6), 1.0, 0.0).astype(bf16)
    right = jnp.dot(terms, pick, preferred_element_type=f32)
    extra = jnp.concatenate([left, right], axis=1).astype(bf16)
    rows = rows_ref[...]
    for i in range(NZ):
        out_ref[i, 0:ROWS, :] = rows
        out_ref[i, ROWS : ROWS + EXTRA, :] = extra


def gather_queries(refs, queries_ref, grads_ref):
    heads = jnp.where(iota((LANES, HD), 1) % HEADS == iota((LANES, HD), 0) // SPAN, 1.0, 0.0).astype(bf16)
    for k, ref in enumerate(refs):
        for half in range(2):
            rows = slice(half * SPAN, (half + 1) * SPAN)
            queries_ref[2 * k + half, :, HD : 2 * HD] = heads
            for h in range(HEADS):
                to = slice(h * SPAN, (h + 1) * SPAN)
                queries_ref[2 * k + half, to, 0:HD] = ref[rows, h * HD : (h + 1) * HD]
                grads_ref[2 * k + half, to, :] = ref[rows, (HEADS + h) * HD : (HEADS + h + 1) * HD]


def shared_span(x, q):
    return 2 * ((x + NX - q // 2) % NX) + q % 2


def spans_of_block(order_ref, x, block):
    first = ((block % NZ) * (NX * NC) + x * NC + block // NZ) * 2
    return order_ref[first], order_ref[first + 1]


def order_of_key(order_ref, x, span):
    block = span // 2
    return order_ref[((block % NZ) * (NX * NC) + x * NC + block // NZ) * 2 + span % 2]


def span_of_query(order_ref, z, x, c, q):
    return order_ref[((z * NX + (x + NX - q // 2) % NX) * NC + c) * 2 + q % 2]


def chunk_scores(order_ref, pairs_ref, t, x, keys_ref, queries_ref, grads_ref, qpos_ref, qdoc_ref):
    pairs = [pairs_ref[WIDE * t + u] for u in range(WIDE)]
    spans = [pair % KSPANS for pair in pairs]
    qspan = (pairs[0] % DEAD) // KSPANS
    keys = jnp.concatenate([keys_ref[span, :, 0 : 2 * HD] for span in spans], axis=0)
    values = jnp.concatenate([keys_ref[span, :, 2 * HD : 3 * HD] for span in spans], axis=0)
    scores = lax.dot_general(keys, queries_ref[qspan], NT, preferred_element_type=f32)
    slopes = lax.dot_general(values, grads_ref[qspan], NT, preferred_element_type=f32)
    at = pl.ds(qspan, 1)
    qpos, qdoc = qpos_ref[at, :][:, 0:HD], qdoc_ref[at, :][:, 0:HD]
    row = iota((SPAN, HD), 0)
    live = []
    for pair, span in zip(pairs, spans):
        key_pos = row + jnp.where(pair < DEAD, order_of_key(order_ref, x, span), 2 * STREAM) * SPAN
        half = (key_pos <= qpos) & (key_pos >= qdoc)
        live.append(jnp.concatenate([half, half], axis=1))
    return qspan, spans, keys, jnp.concatenate(live, axis=0), scores, slopes


def plan_kernel(order_ref, length_ref, line_ref, earlier_ref, select_ref, qpos_ref, qdoc_ref, pairs_ref):
    z, x, c = lax.axis_index("z"), lax.axis_index("x"), lax.axis_index("core")
    row = iota((KEY_ROWS, 1), 0)
    targets = []
    for half in range(2):
        target = jnp.zeros((KEY_ROWS, 1), i32)
        for block in range(BLOCKS):
            target = jnp.where(row // 8 == block, spans_of_block(order_ref, x, block)[half], target)
        targets.append(target)
    row = iota((NX * HEADS, 1), 0)
    for half in range(2):
        target = jnp.zeros((NX * HEADS, 1), i32)
        for i in range(NX):
            target = jnp.where(row // HEADS == i, order_ref[((z * NX + i) * NC + c) * 2 + half], target)
        targets.append(target)
    target = jnp.concatenate(targets, axis=0)
    source = jnp.concatenate([line_ref[0:1, :], line_ref[1:2, :]], axis=1)
    shape = (TARGETS, 2 * SOURCES)
    earlier = (source < target) & (iota(shape, 0) % HEADS == iota(shape, 1) % HEADS)
    earlier_ref[...] = jnp.where(earlier, 1.0, 0.0).astype(bf16)
    row, column = iota((3 * KEY_ROWS, 2 * HD), 0), iota((3 * KEY_ROWS, 2 * HD), 1)
    term = (column % 16) // HEADS
    wanted = term * KEY_ROWS + (column // 16) * 8 + column % HEADS
    select_ref[...] = jnp.where((row == wanted) & (term < 3), 1.0, 0.0).astype(bf16)
    row, column = iota((QSPANS, LANES), 0), iota((QSPANS, LANES), 1)
    qpos = column % SPAN
    spans = []
    for q in range(QSPANS):
        spans.append(span_of_query(order_ref, z, x, c, q))
        qpos = qpos + jnp.where(row == q, spans[q] * SPAN, 0)
    starts = [jnp.int32(0)]
    for doc in range(DOCS - 1):
        starts.append(starts[-1] + length_ref[doc])
    qdoc = jnp.zeros((QSPANS, LANES), i32)
    for start in starts:
        qdoc = jnp.where(qpos >= start, start, qdoc)
    qpos_ref[...] = qpos
    qdoc_ref[...] = qdoc
    found = jnp.int32(0)
    for q in range(QSPANS):
        mine, begin = spans[q], jnp.int32(0)
        for start in starts:
            begin = jnp.where(mine * SPAN >= start, start, begin)

        def scan(span, found, q=q, mine=mine, begin=begin):
            order = order_of_key(order_ref, x, span)
            pairs_ref[found] = q * KSPANS + span
            return found + ((order <= mine) & (order * SPAN + SPAN > begin)).astype(i32)

        found = lax.fori_loop(0, KSPANS, scan, found, unroll=8)
        for i in range(WIDE - 1):
            pairs_ref[found + i] = DEAD + q * KSPANS
        found = (found + WIDE - 1) // WIDE * WIDE
    for i in range(WIDE * UNROLL):
        pairs_ref[found + i] = DEAD
    pairs_ref[PAIRS - 1] = found


def stats_kernel(
    order_ref, pairs_ref, earlier_ref, select_ref, qpos_ref, qdoc_ref, sums_ref, own_ref, peer_ref, qd0, qd1, qd2, qd3,
    stats_ref, keys_ref, queries_ref, grads_ref, qdecay_ref, part_ref, part_high_ref,
    decay, totals, qsums, high_s, mass_s, cross_s,
):
    z, x, c = lax.axis_index("z"), lax.axis_index("x"), lax.axis_index("core")
    gather_queries((qd0, qd1, qd2, qd3), queries_ref, grads_ref)
    for i in range(NZ):
        for ref, core in ((own_ref, c), (peer_ref, 1 - c)):
            block = core * NZ + i
            for half in range(2):
                rows = slice(half * SPAN, (half + 1) * SPAN)
                keys_ref[2 * block + half, :, 0:HD] = ref[i, rows, 0:HD]
                keys_ref[2 * block + half, :, 2 * HD : 3 * HD] = ref[i, rows, HD : 2 * HD]
            totals[block] = ref[i, ROWS : ROWS + EXTRA, HD : 2 * HD]
            terms = ref[i, ROWS : ROWS + EXTRA, 0:HD].astype(f32)
            decay[block] = terms[0:8] + pltpu.roll(terms[0:8], HEADS, 0) + terms[8:16]
    sources = totals[...].reshape(SOURCES, HD)
    first = jnp.dot(earlier_ref[:, 0:SOURCES], sources, preferred_element_type=f32)
    second = jnp.dot(earlier_ref[:, SOURCES : 2 * SOURCES], sources, preferred_element_type=f32)
    lane = iota((TARGETS, HD), 1)
    both = jnp.where(lane < 6, jnp.where(lane % 2 == 0, first, second), 0.0)
    before = jnp.sum(both, axis=1, keepdims=True)
    left = iota((KEY_ROWS, ROWS), 1) < SPAN
    sums = decay[...].reshape(KEY_ROWS, ROWS) + jnp.where(left, before[0:KEY_ROWS], before[KEY_ROWS : 2 * KEY_ROWS])
    own, rows = before[2 * KEY_ROWS :], NX * HEADS
    qsums[...] = sums_ref[...] + jnp.where(iota((rows, ROWS), 1) < SPAN, own[0:rows], own[rows : 2 * rows])
    terms = jnp.concatenate(three_terms(sums * (-1.0 / SCALE)), axis=0).astype(bf16)
    terms = lax.dot_general(terms, select_ref[...], TN, preferred_element_type=f32)
    group = iota((ROWS, HD), 1) // 16
    for block in range(BLOCKS):
        tile = terms[:, (block // 8) * HD : (block // 8 + 1) * HD]
        tile = jnp.where(group == block % 8, tile, 0.0).astype(bf16)
        for half in range(2):
            keys_ref[2 * block + half, :, HD : 2 * HD] = tile[half * SPAN : (half + 1) * SPAN]
    for k in range(NX):
        for h in range(HEADS):
            own = qsums[pl.ds(((x + NX - k) % NX) * HEADS + h, 1), :]
            for half in range(2):
                qdecay_ref[2 * k + half : 2 * k + half + 1, h * SPAN : (h + 1) * SPAN] = own[
                    :, half * SPAN : (half + 1) * SPAN
                ]
    high_s[...] = jnp.full((QSPANS, LANES), NEG, f32)
    mass_s[...] = jnp.zeros((QSPANS, LANES), f32)
    cross_s[...] = jnp.zeros((QSPANS, LANES), f32)

    def step(t, carry):
        parts = []
        for u in range(UNROLL):
            qspan, _, _, live, scores, slopes = chunk_scores(
                order_ref, pairs_ref, UNROLL * t + u, x, keys_ref, queries_ref, grads_ref, qpos_ref, qdoc_ref
            )
            scores = jnp.where(live, scores * SCALE + qdecay_ref[pl.ds(qspan, 1), :], NEG)
            high = jnp.max(scores, axis=0, keepdims=True)
            weights = jnp.exp(scores - high)
            sums, row = jnp.zeros((8, LANES), f32), iota((8, LANES), 0)
            for first, array in ((0, weights), (4, weights * slopes)):
                for i in range(4):
                    one = jnp.sum(array[i * SPAN : (i + 1) * SPAN], axis=0, keepdims=True)
                    sums = jnp.where(row == first + i, one, sums)
            part_ref[UNROLL * t + u] = sums
            part_high_ref[UNROLL * t + u] = jnp.broadcast_to(high, (8, LANES))
            parts.append(
                (qspan, high, jnp.sum(sums[0:4], axis=0, keepdims=True), jnp.sum(sums[4:8], axis=0, keepdims=True))
            )
        for qspan, high, mass, cross in parts:
            at = pl.ds(shared_span(x, qspan), 1)
            old = high_s[at, :]
            new = jnp.maximum(old, high)
            before, now = jnp.exp(old - new), jnp.exp(high - new)
            high_s[at, :] = new
            mass_s[at, :] = mass_s[at, :] * before + mass * now
            cross_s[at, :] = cross_s[at, :] * before + cross * now
        return carry

    lax.fori_loop(0, (pairs_ref[PAIRS - 1] // WIDE + UNROLL - 1) // UNROLL, step, 0)
    stats_ref[0:8, :] = high_s[...]
    stats_ref[8:16, :] = mass_s[...]
    stats_ref[16:24, :] = cross_s[...]


def totals_kernel(pairs_ref, stats0, stats1, stats2, stats3, part_ref, part_high_ref, total_ref, lse_ref, delta_ref):
    x = lax.axis_index("x")
    stats = [(ref[0:8, :], ref[8:16, :], ref[16:24, :]) for ref in (stats0, stats1, stats2, stats3)]
    high = stats[0][0]
    for one, _, _ in stats[1:]:
        high = jnp.maximum(high, one)
    mass, cross = jnp.zeros_like(high), jnp.zeros_like(high)
    for one, one_mass, one_cross in stats:
        factor = jnp.exp(one - high)
        mass = mass + one_mass * factor
        cross = cross + one_cross * factor
    lse_ref[...] = high + jnp.log(mass)
    delta_ref[...] = cross / mass
    heads = jnp.where(iota((LANES, HD), 1) % HEADS == iota((LANES, HD), 0) // SPAN, 1.0, 0.0).astype(f32)
    chunks = pairs_ref[PAIRS - 1] // WIDE
    row = iota((8, LANES), 0)
    group = iota((1, HD), 1) // HEADS

    def step(t, total):
        rows, places = [], []
        for u in range(TOGETHER):
            chunk = jnp.minimum(TOGETHER * t + u, chunks - 1)
            at = pl.ds(shared_span(x, (pairs_ref[WIDE * chunk] % DEAD) // KSPANS), 1)
            scale = jnp.exp(part_high_ref[chunk] - lse_ref[at, :])
            rows.append(scale * part_ref[chunk] * jnp.where(row < 4, -delta_ref[at, :], 1.0))
            none = jnp.where(TOGETHER * t + u < chunks, 0, HD)
            spans = [pairs_ref[WIDE * chunk + i] % KSPANS for i in range(WIDE)]
            places.append([span // 2 + (span % 2) * BLOCKS + none for span in spans])
        sums = exact_dot(jnp.concatenate(rows, axis=0), heads)
        for u in range(TOGETHER):
            for i in range(WIDE):
                one = sums[8 * u + i : 8 * u + i + 1] + sums[8 * u + i + 4 : 8 * u + i + 5]
                total = total + jnp.where(group == places[u][i], one, 0.0)
        return total

    total = lax.fori_loop(0, (chunks + TOGETHER - 1) // TOGETHER, step, jnp.zeros((1, HD), f32))
    total_ref[...] = jnp.broadcast_to(total, total_ref.shape)


def grads_kernel(
    order_ref, pairs_ref, lse_ref, delta_ref, keys_ref, queries_ref, grads_ref, qdecay_ref, qpos_ref, qdoc_ref,
    dq0, dq1, dq2, dq3, own_out, peer_out, own_col, peer_col,
    acc, dqt, col,
):
    x, c = lax.axis_index("x"), lax.axis_index("core")
    acc[...] = jnp.zeros_like(acc)
    dqt[...] = jnp.zeros_like(dqt)
    col[...] = jnp.zeros_like(col)

    def step(t, carry):
        parts = []
        for u in range(UNROLL):
            qspan, spans, keys, live, scores, slopes = chunk_scores(
                order_ref, pairs_ref, UNROLL * t + u, x, keys_ref, queries_ref, grads_ref, qpos_ref, qdoc_ref
            )
            at = pl.ds(shared_span(x, qspan), 1)
            shift = qdecay_ref[pl.ds(qspan, 1), :] - lse_ref[at, :]
            probs = jnp.exp(jnp.where(live, scores * SCALE + shift, NEG))
            dscores = probs * (slopes - delta_ref[at, :])
            upper = dscores.astype(bf16)
            lower = (dscores - upper.astype(f32)).astype(bf16)
            queries = queries_ref[qspan]
            both = jnp.dot(upper, queries, preferred_element_type=f32)
            dv = jnp.dot(probs.astype(bf16), grads_ref[qspan], preferred_element_type=f32)
            column = both[:, HD : 2 * HD] + jnp.dot(lower, queries[:, HD : 2 * HD], preferred_element_type=f32)
            dq = lax.dot_general(
                jnp.concatenate([keys[:, 0:HD], keys[:, 0:HD]], axis=0),
                jnp.concatenate([upper, lower], axis=0),
                TN,
                preferred_element_type=f32,
            )
            parts.append((qspan, spans, both[:, 0:HD], dv, column, dq))
        group = iota((SPAN, HD), 1) // HEADS
        for qspan, spans, dk, dv, column, dq in parts:
            dqt[qspan] += dq
            for u, span in enumerate(spans):
                rows = slice(u * SPAN, (u + 1) * SPAN)
                acc[span, :, 0:HD] += dk[rows]
                acc[span, :, HD : 2 * HD] += dv[rows]
                col[span % 2] += jnp.where(group == span // 2, column[rows], 0.0)
        return carry

    lax.fori_loop(0, (pairs_ref[PAIRS - 1] // WIDE + UNROLL - 1) // UNROLL, step, 0)
    for q in range(QSPANS):
        whole = dqt[q].T
        begin = (q % 2) * SPAN
        for h in range(HEADS):
            (dq0, dq1, dq2, dq3)[q // 2][begin : begin + SPAN, h * HD : (h + 1) * HD] = whole[h * SPAN : (h + 1) * SPAN]
    turned = col[...].reshape(ROWS, HD).T.reshape(2, SPAN, HD)
    col[...] = turned
    half = NZ * HEADS
    own_col[...] = col[0, pl.ds(pl.multiple_of(c * half, half), half), :]
    peer_col[...] = col[0, pl.ds(pl.multiple_of((1 - c) * half, half), half), :]
    for i in range(NZ):
        for part in range(2):
            rows = slice(part * SPAN, (part + 1) * SPAN)
            own_out[i, rows, :] = acc[2 * (c * NZ + i) + part]
            peer_out[i, rows, :] = acc[2 * ((1 - c) * NZ + i) + part]


def send_grads_kernel(own_ref, peer_ref, own_col, peer_col, mine_ref, other_ref, out_ref):
    x = lax.axis_index("x")
    row = iota((8, HD), 0)
    totals = jnp.zeros((8, HD), f32)
    for k in range(NX):
        both = mine_ref[8 * k : 8 * k + 8, :] + other_ref[8 * k : 8 * k + 8, :]
        totals = jnp.where(row == 2 * ((x + NX - k) % NX), both, totals)
    high, middle, low = three_terms(totals)
    right = jnp.concatenate([high + pltpu.roll(middle, 1, 0), low], axis=0)
    columns = own_col[...] + peer_col[...]
    for i in range(NZ):
        out_ref[i, 0:ROWS, :] = (own_ref[i] + peer_ref[i]).astype(bf16)
        group = columns[8 * (i // 2) : 8 * (i // 2) + 8]
        if i % 2:
            group = pltpu.roll(group, HEADS, 0)
        high, middle, low = three_terms(group)
        left = jnp.concatenate([jnp.where(row < HEADS, high, pltpu.roll(middle, HEADS, 0)), low], axis=0)
        out_ref[i, ROWS : ROWS + EXTRA, :] = jnp.concatenate([left, right], axis=1).astype(bf16)


def sum_queries_kernel(dq0, dq1, dq2, dq3, query_ref):
    query_ref[...] = (((dq0[...] + dq1[...]) + (dq2[...] + dq3[...])) * SCALE).astype(bf16)


def finish_kernel(order_ref, span_ref, in_ref, key_ref, value_ref, forget_ref):
    first = ((lax.axis_index("z") * NX + lax.axis_index("x")) * NC + lax.axis_index("core")) * 2
    total = in_ref[0].astype(f32)
    for i in range(1, NZ):
        total = total + in_ref[i].astype(f32)
    key_ref[...] = (total[0:ROWS, 0:HD] * SCALE).astype(bf16)
    value_ref[...] = total[0:ROWS, HD : 2 * HD].astype(bf16)
    extra = total[ROWS : ROWS + EXTRA]
    left, right = extra[:, 0:HD], extra[:, HD : 2 * HD]
    columns = left[0:8] + pltpu.roll(left[0:8], HEADS, 0) + left[8:16]
    totals = right[0:8] + pltpu.roll(right[0:8], 7, 0) + right[8:16]
    row, column = iota((8, HD), 0), iota((8, HD), 1)
    after = []
    for h in range(2):
        later = span_ref[...] > order_ref[first + h]
        line = jnp.sum(jnp.where(later, totals, 0.0), axis=0, keepdims=True)
        after.append(jnp.sum(jnp.where(column % HEADS == row, line, 0.0), axis=1, keepdims=True))
    within = exact_dot(columns, same_span_from(ROWS))
    within = within + jnp.where(column < SPAN, after[0], after[1])
    forget_ref[...] = -within[0:HEADS]


def call(kernel, specs, outs, scratch, flops, *args):
    place = {"s": pl.BlockSpec(memory_space=pltpu.SMEM), "v": pl.BlockSpec(memory_space=pltpu.VMEM)}
    return pl.pallas_call(
        kernel,
        in_specs=[place[k] for k in specs],
        out_specs=[place[k] for k, _, _ in outs],
        out_shape=[jax.ShapeDtypeStruct(shape, dtype) for _, shape, dtype in outs],
        scratch_shapes=[pltpu.VMEM(shape, dtype) for shape, dtype in scratch],
        compiler_params=pltpu.CompilerParams(vmem_limit_bytes=VMEM_LIMIT),
        cost_estimate=pl.CostEstimate(flops=flops, bytes_accessed=4 << 20, transcendentals=0),
    )(*args)


def body(queries, keys, values, out_grad, gate_logits, doc_lengths, span_order):
    swap = [(0, 1), (1, 0)]
    (log_forget,) = call(send_gates_kernel, "v", [("v", (NX * NY, 8, HD), f32)], [], 0, gate_logits.T)
    log_forget, keys, values = lax.optimization_barrier((log_forget, keys, values))
    logs = lax.all_to_all(log_forget, ("x", "head"), 0, 0)
    key_rows = jnp.concatenate([keys, values], axis=1)
    logs, key_rows = lax.optimization_barrier((logs, key_rows))
    message = (NZ, ROWS + EXTRA, 2 * HD)
    key_message, own_sums = call(
        send_keys_kernel,
        "vv",
        [("v", message, bf16), ("v", (NX * HEADS, ROWS), f32)],
        [],
        0,
        logs, key_rows,
    )

    key_message, queries, out_grad, span_order, doc_lengths = lax.optimization_barrier(
        (key_message, queries, out_grad, span_order, doc_lengths)
    )
    pair_rows = jnp.concatenate([queries, out_grad], axis=1)
    order4 = span_order.reshape(NZ, NX, NC, 2).transpose(3, 2, 0, 1)
    order_line = jnp.broadcast_to(order4[..., None], (2, NC, NZ, NX, HEADS)).reshape(2, NC * NZ * NX * HEADS)
    order_spans = jnp.broadcast_to(order4.transpose(3, 0, 1, 2)[..., None], (NX, 2, NC, NZ, HEADS)).reshape(NX, 1, HD)
    order_spans = jnp.concatenate([order_spans, jnp.full_like(order_spans, -1)], axis=1).reshape(2 * NX, HD)
    own = lax.all_to_all(key_message, "z", 0, 0)
    query_rows = [pair_rows]
    for k in range(1, NX):
        query_rows.append(lax.ppermute(pair_rows, "x", [(i, (i + k) % NX) for i in range(NX)]))
    plan = call(
        plan_kernel,
        "ssv",
        [
            ("v", (TARGETS, 2 * SOURCES), bf16),
            ("v", (3 * KEY_ROWS, 2 * HD), bf16),
            ("v", (QSPANS, LANES), i32),
            ("v", (QSPANS, LANES), i32),
            ("s", (PAIRS,), i32),
        ],
        [],
        1 << 28,
        span_order, doc_lengths, order_line,
    )
    own, query_rows, plan, order_spans = lax.optimization_barrier((own, query_rows, plan, order_spans))
    earlier, select, qpos, qdoc, pairs = plan
    peer = lax.ppermute(own, "core", swap)

    line = ((QSPANS, LANES), f32)
    stats, *rows, qdecay, part, part_high = call(
        stats_kernel,
        "ssvvvvvvvvvvv",
        [
            ("v", (24, LANES), f32),
            ("v", (KSPANS, SPAN, 3 * HD), bf16),
            ("v", (QSPANS, LANES, 2 * HD), bf16),
            ("v", (QSPANS, LANES, HD), bf16),
            ("v", (QSPANS, LANES), f32),
            ("v", (CHUNKS, 8, LANES), f32),
            ("v", (CHUNKS, 8, LANES), f32),
        ],
        [((BLOCKS, 8, ROWS), f32), ((BLOCKS, EXTRA, HD), bf16), ((NX * HEADS, ROWS), f32), line, line, line],
        1 << 28,
        span_order, pairs, earlier, select, qpos, qdoc, own_sums, own, peer, *query_rows,
    )
    all_stats = [stats]
    for k in range(1, NX):
        all_stats.append(lax.ppermute(stats, "x", [(i, (i + k) % NX) for i in range(NX)]))
    total, lse, delta = call(
        totals_kernel,
        "svvvvvv",
        [("v", (8, HD), f32), ("v", (QSPANS, LANES), f32), ("v", (QSPANS, LANES), f32)],
        [],
        0,
        pairs, *all_stats, part, part_high,
    )
    totals = [total]
    for k in range(1, NX):
        totals.append(lax.ppermute(total, "x", [(i, (i + k) % NX) for i in range(NX)]))
    results = call(
        grads_kernel,
        "ssvvvvvvvv",
        [
            *[("v", (ROWS, HEADS * HD), f32)] * NX,
            ("v", (NZ, ROWS, 2 * HD), f32),
            ("v", (NZ, ROWS, 2 * HD), f32),
            ("v", (NZ * HEADS, ROWS), f32),
            ("v", (NZ * HEADS, ROWS), f32),
        ],
        [((KSPANS, SPAN, 2 * HD), f32), ((QSPANS, HD, LANES), f32), ((2, SPAN, HD), f32)],
        1 << 29,
        span_order, pairs, lse, delta, *rows, qdecay, qpos, qdoc,
    )
    totals, results = lax.optimization_barrier((totals, results))
    dq0, dq1, dq2, dq3, own_sum, peer_sum, own_col, peer_col = results
    peer_sum = lax.ppermute(peer_sum, "core", swap)
    peer_col = lax.ppermute(peer_col, "core", swap)
    totals = jnp.concatenate(totals, axis=0)
    peer_totals = lax.ppermute(totals, "core", swap)
    (grad_message,) = call(
        send_grads_kernel,
        "vvvvvv",
        [("v", (NZ, ROWS + EXTRA, 2 * HD), bf16)],
        [],
        0,
        own_sum, peer_sum, own_col, peer_col, totals, peer_totals,
    )
    grad_message, dq1, dq2, dq3 = lax.optimization_barrier((grad_message, dq1, dq2, dq3))
    back = lax.all_to_all(grad_message, "z", 0, 0)
    parts = [
        lax.ppermute(part, "x", [(i, (i - k) % NX) for i in range(NX)]) for k, part in ((1, dq1), (2, dq2), (3, dq3))
    ]
    (query_grad,) = call(
        sum_queries_kernel, "vvvv", [("v", (ROWS, HEADS * HD), bf16)], [], 0, dq0, *parts
    )
    back, query_grad = lax.optimization_barrier((back, query_grad))
    key_grad, value_grad, forget_grad = call(
        finish_kernel,
        "svv",
        [
            ("v", (ROWS, HD), bf16),
            ("v", (ROWS, HD), bf16),
            ("v", (HEADS, ROWS), f32),
        ],
        [],
        0,
        span_order, order_spans, back,
    )
    return query_grad, key_grad, value_grad, forget_grad.T


def solution(mesh):
    fine = Mesh(mesh.devices.reshape(NZ, NX, NC, NY), ("z", "x", "core", "head"))
    ctx = ("z", "x", "core")
    rows = P(ctx, "head")
    return jax.shard_map(
        body,
        mesh=fine,
        in_specs=(rows, rows, rows, rows, P((*ctx, "head"), None), P(), P()),
        out_specs=(rows, rows, rows, rows),
        check_vma=False,
    )
```

```python
import functools
import math

import jax
import jax.numpy as jnp
from jax import lax
from jax.experimental import pallas as pl
from jax.experimental.pallas import tpu as pltpu
from jax.sharding import Mesh, PartitionSpec as P

NZ, NX, NC, NY = 8, 4, 2, 4
ROWS, SPAN, HEADS, HD = 128, 64, 4, 128
DOCS = 16
BLOCKS = NC * NZ
KEY_ROWS = BLOCKS * 8
SOURCES = BLOCKS * NX * HEADS
TARGETS = 2 * KEY_ROWS + 2 * NX * HEADS
QSPANS = 2 * NX
LANES = HEADS * SPAN
EXTRA = 16
KSPANS = 2 * BLOCKS
WIDE = 4
DEAD = QSPANS * KSPANS
STREAM = 8192
UNROLL = 4
PAIRS = DEAD + WIDE * UNROLL + 1
CHUNKS = DEAD // WIDE + UNROLL
TOGETHER = 8
NEG = -1e30
SCALE = 1.0 / math.sqrt(HD)
f32, bf16, i32 = jnp.float32, jnp.bfloat16, jnp.int32
VMEM_LIMIT = 16 * 1024 * 1024
NT = (((1,), (1,)), ((), ()))
TN = (((0,), (0,)), ((), ()))


def three_terms(a):
    high = a.astype(bf16).astype(f32)
    rest = a - high
    middle = rest.astype(bf16).astype(f32)
    return high, middle, rest - middle


def exact_dot(a, ones):
    terms = jnp.concatenate(three_terms(a), axis=0).astype(bf16)
    terms = jnp.dot(terms, ones.astype(bf16), preferred_element_type=f32)
    rows = a.shape[0]
    return terms[0:rows] + terms[rows : 2 * rows] + terms[2 * rows : 3 * rows]


def iota(shape, dim):
    return lax.broadcasted_iota(i32, shape, dim)


def same_span_upto(n):
    row, column = iota((n, n), 0), iota((n, n), 1)
    return jnp.where((row <= column) & (row // SPAN == column // SPAN), 1.0, 0.0).astype(f32)


def same_span_from(n):
    row, column = iota((n, n), 0), iota((n, n), 1)
    return jnp.where((row >= column) & (row // SPAN == column // SPAN), 1.0, 0.0).astype(f32)


def send_gates_kernel(gate_ref, out_ref):
    gates = gate_ref[...]
    small = jnp.exp(-jnp.abs(gates))
    w = 1.0 + small
    one = w == 1.0
    log_one_plus = jnp.where(one, small, jnp.log(w) * (small / jnp.where(one, 1.0, w - 1.0)))
    logs = jnp.minimum(gates, 0.0) - log_one_plus
    logs = jnp.concatenate([logs, jnp.zeros((NY * HEADS, HD - logs.shape[1]), f32)], axis=1)
    row = iota((8, HD), 0)
    for y in range(NY):
        group = logs[8 * (y // 2) : 8 * (y // 2) + 8]
        if y % 2:
            group = pltpu.roll(group, HEADS, 0)
        group = jnp.where(row < HEADS, group, 0.0)
        for x in range(NX):
            out_ref[x * NY + y] = group


def send_keys_kernel(log_ref, rows_ref, out_ref, sums_ref):
    parts = []
    for x in range(NX):
        total = log_ref[x * NY]
        for y in range(1, NY):
            total = total + pltpu.roll(log_ref[x * NY + y], 32 * y, 1)
        parts.append(total)
    logs = jnp.concatenate(
        [parts[0] + pltpu.roll(parts[1], HEADS, 0), parts[2] + pltpu.roll(parts[3], HEADS, 0)], axis=0
    )
    sums = exact_dot(logs, same_span_upto(ROWS))
    sums_ref[...] = sums
    x = lax.axis_index("x")
    row = iota((8, HD), 0)
    own = jnp.zeros((8, HD), f32)
    for h in range(HEADS):
        own = jnp.where(row == h, sums_ref[pl.ds(x * HEADS + h, 1), :], own)
    high, middle, low = three_terms(own)
    left = jnp.concatenate([high + pltpu.roll(middle, HEADS, 0), low], axis=0)
    terms = jnp.concatenate(three_terms(sums), axis=1).astype(bf16)
    row, column = iota((3 * HD, HD), 0), iota((3 * HD, HD), 1)
    wanted = (column // 2) * HD + (column % 2) * SPAN + SPAN - 1
    pick = jnp.where((row == wanted) & (column < 6), 1.0, 0.0).astype(bf16)
    right = jnp.dot(terms, pick, preferred_element_type=f32)
    extra = jnp.concatenate([left, right], axis=1).astype(bf16)
    rows = rows_ref[...]
    for i in range(NZ):
        out_ref[i, 0:ROWS, :] = rows
        out_ref[i, ROWS : ROWS + EXTRA, :] = extra


def gather_queries_kernel(qd0, qd1, qd2, qd3, queries_ref, grads_ref):
    heads = jnp.where(iota((LANES, HD), 1) % HEADS == iota((LANES, HD), 0) // SPAN, 1.0, 0.0).astype(bf16)
    for k, ref in enumerate((qd0, qd1, qd2, qd3)):
        for half in range(2):
            rows = slice(half * SPAN, (half + 1) * SPAN)
            queries_ref[2 * k + half, :, HD : 2 * HD] = heads
            for h in range(HEADS):
                to = slice(h * SPAN, (h + 1) * SPAN)
                queries_ref[2 * k + half, to, 0:HD] = ref[rows, h * HD : (h + 1) * HD]
                grads_ref[2 * k + half, to, :] = ref[rows, (HEADS + h) * HD : (HEADS + h + 1) * HD]


def shared_span(x, q):
    return 2 * ((x + NX - q // 2) % NX) + q % 2


def spans_of_block(order_ref, x, block):
    first = ((block % NZ) * (NX * NC) + x * NC + block // NZ) * 2
    return order_ref[first], order_ref[first + 1]


def order_of_key(order_ref, x, span):
    block = span // 2
    return order_ref[((block % NZ) * (NX * NC) + x * NC + block // NZ) * 2 + span % 2]


def span_of_query(order_ref, z, x, c, q):
    return order_ref[((z * NX + (x + NX - q // 2) % NX) * NC + c) * 2 + q % 2]


def chunk_scores(order_ref, pairs_ref, t, x, keys_ref, queries_ref, grads_ref, qpos_ref, qdoc_ref):
    pairs = [pairs_ref[WIDE * t + u] for u in range(WIDE)]
    spans = [pair % KSPANS for pair in pairs]
    qspan = (pairs[0] % DEAD) // KSPANS
    keys = jnp.concatenate([keys_ref[span, :, 0 : 2 * HD] for span in spans], axis=0)
    values = jnp.concatenate([keys_ref[span, :, 2 * HD : 3 * HD] for span in spans], axis=0)
    scores = lax.dot_general(keys, queries_ref[qspan], NT, preferred_element_type=f32)
    slopes = lax.dot_general(values, grads_ref[qspan], NT, preferred_element_type=f32)
    at = pl.ds(qspan, 1)
    qpos, qdoc = qpos_ref[at, :][:, 0:HD], qdoc_ref[at, :][:, 0:HD]
    row = iota((SPAN, HD), 0)
    live = []
    for pair, span in zip(pairs, spans):
        key_pos = row + jnp.where(pair < DEAD, order_of_key(order_ref, x, span), 2 * STREAM) * SPAN
        half = (key_pos <= qpos) & (key_pos >= qdoc)
        live.append(jnp.concatenate([half, half], axis=1))
    return qspan, spans, keys, jnp.concatenate(live, axis=0), scores, slopes


def plan_kernel(order_ref, length_ref, line_ref, earlier_ref, select_ref, qpos_ref, qdoc_ref, pairs_ref):
    z, x, c = lax.axis_index("z"), lax.axis_index("x"), lax.axis_index("core")
    row = iota((KEY_ROWS, 1), 0)
    targets = []
    for half in range(2):
        target = jnp.zeros((KEY_ROWS, 1), i32)
        for block in range(BLOCKS):
            target = jnp.where(row // 8 == block, spans_of_block(order_ref, x, block)[half], target)
        targets.append(target)
    row = iota((NX * HEADS, 1), 0)
    for half in range(2):
        target = jnp.zeros((NX * HEADS, 1), i32)
        for i in range(NX):
            target = jnp.where(row // HEADS == i, order_ref[((z * NX + i) * NC + c) * 2 + half], target)
        targets.append(target)
    target = jnp.concatenate(targets, axis=0)
    source = jnp.concatenate([line_ref[0:1, :], line_ref[1:2, :]], axis=1)
    shape = (TARGETS, 2 * SOURCES)
    earlier = (source < target) & (iota(shape, 0) % HEADS == iota(shape, 1) % HEADS)
    earlier_ref[...] = jnp.where(earlier, 1.0, 0.0).astype(bf16)
    row, column = iota((3 * KEY_ROWS, 2 * HD), 0), iota((3 * KEY_ROWS, 2 * HD), 1)
    term = (column % 16) // HEADS
    wanted = term * KEY_ROWS + (column // 16) * 8 + column % HEADS
    select_ref[...] = jnp.where((row == wanted) & (term < 3), 1.0, 0.0).astype(bf16)
    row, column = iota((QSPANS, LANES), 0), iota((QSPANS, LANES), 1)
    qpos = column % SPAN
    spans = []
    for q in range(QSPANS):
        spans.append(span_of_query(order_ref, z, x, c, q))
        qpos = qpos + jnp.where(row == q, spans[q] * SPAN, 0)
    starts = [jnp.int32(0)]
    for doc in range(DOCS - 1):
        starts.append(starts[-1] + length_ref[doc])
    qdoc = jnp.zeros((QSPANS, LANES), i32)
    for start in starts:
        qdoc = jnp.where(qpos >= start, start, qdoc)
    qpos_ref[...] = qpos
    qdoc_ref[...] = qdoc
    found = jnp.int32(0)
    for q in range(QSPANS):
        mine, begin = spans[q], jnp.int32(0)
        for start in starts:
            begin = jnp.where(mine * SPAN >= start, start, begin)

        def scan(span, found, q=q, mine=mine, begin=begin):
            order = order_of_key(order_ref, x, span)
            pairs_ref[found] = q * KSPANS + span
            return found + ((order <= mine) & (order * SPAN + SPAN > begin)).astype(i32)

        found = lax.fori_loop(0, KSPANS, scan, found, unroll=8)
        for i in range(WIDE - 1):
            pairs_ref[found + i] = DEAD + q * KSPANS
        found = (found + WIDE - 1) // WIDE * WIDE
    for i in range(WIDE * UNROLL):
        pairs_ref[found + i] = DEAD
    pairs_ref[PAIRS - 1] = found


def stats_kernel(
    order_ref, pairs_ref, earlier_ref, select_ref, qpos_ref, qdoc_ref, sums_ref, own_ref, peer_ref, queries_ref, grads_ref,
    stats_ref, keys_ref, qdecay_ref, part_ref, part_high_ref,
    decay, totals, qsums, high_s, mass_s, cross_s,
):
    z, x, c = lax.axis_index("z"), lax.axis_index("x"), lax.axis_index("core")
    for i in range(NZ):
        for ref, core in ((own_ref, c), (peer_ref, 1 - c)):
            block = core * NZ + i
            for half in range(2):
                rows = slice(half * SPAN, (half + 1) * SPAN)
                keys_ref[2 * block + half, :, 0:HD] = ref[i, rows, 0:HD]
                keys_ref[2 * block + half, :, 2 * HD : 3 * HD] = ref[i, rows, HD : 2 * HD]
            totals[block] = ref[i, ROWS : ROWS + EXTRA, HD : 2 * HD]
            terms = ref[i, ROWS : ROWS + EXTRA, 0:HD].astype(f32)
            decay[block] = terms[0:8] + pltpu.roll(terms[0:8], HEADS, 0) + terms[8:16]
    sources = totals[...].reshape(SOURCES, HD)
    first = jnp.dot(earlier_ref[:, 0:SOURCES], sources, preferred_element_type=f32)
    second = jnp.dot(earlier_ref[:, SOURCES : 2 * SOURCES], sources, preferred_element_type=f32)
    lane = iota((TARGETS, HD), 1)
    both = jnp.where(lane < 6, jnp.where(lane % 2 == 0, first, second), 0.0)
    before = jnp.sum(both, axis=1, keepdims=True)
    left = iota((KEY_ROWS, ROWS), 1) < SPAN
    sums = decay[...].reshape(KEY_ROWS, ROWS) + jnp.where(left, before[0:KEY_ROWS], before[KEY_ROWS : 2 * KEY_ROWS])
    own, rows = before[2 * KEY_ROWS :], NX * HEADS
    qsums[...] = sums_ref[...] + jnp.where(iota((rows, ROWS), 1) < SPAN, own[0:rows], own[rows : 2 * rows])
    terms = jnp.concatenate(three_terms(sums * (-1.0 / SCALE)), axis=0).astype(bf16)
    terms = lax.dot_general(terms, select_ref[...], TN, preferred_element_type=f32)
    group = iota((ROWS, HD), 1) // 16
    for block in range(BLOCKS):
        tile = terms[:, (block // 8) * HD : (block // 8 + 1) * HD]
        tile = jnp.where(group == block % 8, tile, 0.0).astype(bf16)
        for half in range(2):
            keys_ref[2 * block + half, :, HD : 2 * HD] = tile[half * SPAN : (half + 1) * SPAN]
    for k in range(NX):
        for h in range(HEADS):
            own = qsums[pl.ds(((x + NX - k) % NX) * HEADS + h, 1), :]
            for half in range(2):
                qdecay_ref[2 * k + half : 2 * k + half + 1, h * SPAN : (h + 1) * SPAN] = own[
                    :, half * SPAN : (half + 1) * SPAN
                ]
    high_s[...] = jnp.full((QSPANS, LANES), NEG, f32)
    mass_s[...] = jnp.zeros((QSPANS, LANES), f32)
    cross_s[...] = jnp.zeros((QSPANS, LANES), f32)

    def step(t, carry):
        parts = []
        for u in range(UNROLL):
            qspan, _, _, live, scores, slopes = chunk_scores(
                order_ref, pairs_ref, UNROLL * t + u, x, keys_ref, queries_ref, grads_ref, qpos_ref, qdoc_ref
            )
            scores = jnp.where(live, scores * SCALE + qdecay_ref[pl.ds(qspan, 1), :], NEG)
            high = jnp.max(scores, axis=0, keepdims=True)
            weights = jnp.exp(scores - high)
            sums, row = jnp.zeros((8, LANES), f32), iota((8, LANES), 0)
            for first, array in ((0, weights), (4, weights * slopes)):
                for i in range(4):
                    one = jnp.sum(array[i * SPAN : (i + 1) * SPAN], axis=0, keepdims=True)
                    sums = jnp.where(row == first + i, one, sums)
            part_ref[UNROLL * t + u] = sums
            part_high_ref[UNROLL * t + u] = jnp.broadcast_to(high, (8, LANES))
            parts.append(
                (qspan, high, jnp.sum(sums[0:4], axis=0, keepdims=True), jnp.sum(sums[4:8], axis=0, keepdims=True))
            )
        for qspan, high, mass, cross in parts:
            at = pl.ds(shared_span(x, qspan), 1)
            old = high_s[at, :]
            new = jnp.maximum(old, high)
            before, now = jnp.exp(old - new), jnp.exp(high - new)
            high_s[at, :] = new
            mass_s[at, :] = mass_s[at, :] * before + mass * now
            cross_s[at, :] = cross_s[at, :] * before + cross * now
        return carry

    lax.fori_loop(0, (pairs_ref[PAIRS - 1] // WIDE + UNROLL - 1) // UNROLL, step, 0)
    stats_ref[0:8, :] = high_s[...]
    stats_ref[8:16, :] = mass_s[...]
    stats_ref[16:24, :] = cross_s[...]


def totals_kernel(pairs_ref, stats0, stats1, stats2, stats3, part_ref, part_high_ref, total_ref, lse_ref, delta_ref):
    x = lax.axis_index("x")
    stats = [(ref[0:8, :], ref[8:16, :], ref[16:24, :]) for ref in (stats0, stats1, stats2, stats3)]
    high = stats[0][0]
    for one, _, _ in stats[1:]:
        high = jnp.maximum(high, one)
    mass, cross = jnp.zeros_like(high), jnp.zeros_like(high)
    for one, one_mass, one_cross in stats:
        factor = jnp.exp(one - high)
        mass = mass + one_mass * factor
        cross = cross + one_cross * factor
    lse_ref[...] = high + jnp.log(mass)
    delta_ref[...] = cross / mass
    heads = jnp.where(iota((LANES, HD), 1) % HEADS == iota((LANES, HD), 0) // SPAN, 1.0, 0.0).astype(f32)
    chunks = pairs_ref[PAIRS - 1] // WIDE
    row = iota((8, LANES), 0)
    group = iota((1, HD), 1) // HEADS

    def step(t, total):
        rows, places = [], []
        for u in range(TOGETHER):
            chunk = jnp.minimum(TOGETHER * t + u, chunks - 1)
            at = pl.ds(shared_span(x, (pairs_ref[WIDE * chunk] % DEAD) // KSPANS), 1)
            scale = jnp.exp(part_high_ref[chunk] - lse_ref[at, :])
            rows.append(scale * part_ref[chunk] * jnp.where(row < 4, -delta_ref[at, :], 1.0))
            none = jnp.where(TOGETHER * t + u < chunks, 0, HD)
            spans = [pairs_ref[WIDE * chunk + i] % KSPANS for i in range(WIDE)]
            places.append([span // 2 + (span % 2) * BLOCKS + none for span in spans])
        sums = exact_dot(jnp.concatenate(rows, axis=0), heads)
        for u in range(TOGETHER):
            for i in range(WIDE):
                one = sums[8 * u + i : 8 * u + i + 1] + sums[8 * u + i + 4 : 8 * u + i + 5]
                total = total + jnp.where(group == places[u][i], one, 0.0)
        return total

    total = lax.fori_loop(0, (chunks + TOGETHER - 1) // TOGETHER, step, jnp.zeros((1, HD), f32))
    total_ref[...] = jnp.broadcast_to(total, total_ref.shape)


def grads_kernel(
    order_ref, pairs_ref, lse_ref, delta_ref, keys_ref, queries_ref, grads_ref, qdecay_ref, qpos_ref, qdoc_ref,
    dq0, dq1, dq2, dq3, own_out, peer_out, own_col, peer_col,
    acc, dqt, col,
):
    x, c = lax.axis_index("x"), lax.axis_index("core")
    acc[...] = jnp.zeros_like(acc)
    dqt[...] = jnp.zeros_like(dqt)
    col[...] = jnp.zeros_like(col)

    def step(t, carry):
        parts = []
        for u in range(UNROLL):
            qspan, spans, keys, live, scores, slopes = chunk_scores(
                order_ref, pairs_ref, UNROLL * t + u, x, keys_ref, queries_ref, grads_ref, qpos_ref, qdoc_ref
            )
            at = pl.ds(shared_span(x, qspan), 1)
            shift = qdecay_ref[pl.ds(qspan, 1), :] - lse_ref[at, :]
            probs = jnp.exp(jnp.where(live, scores * SCALE + shift, NEG))
            dscores = probs * (slopes - delta_ref[at, :])
            upper = dscores.astype(bf16)
            lower = (dscores - upper.astype(f32)).astype(bf16)
            queries = queries_ref[qspan]
            both = jnp.dot(upper, queries, preferred_element_type=f32)
            dv = jnp.dot(probs.astype(bf16), grads_ref[qspan], preferred_element_type=f32)
            column = both[:, HD : 2 * HD] + jnp.dot(lower, queries[:, HD : 2 * HD], preferred_element_type=f32)
            dq = lax.dot_general(
                jnp.concatenate([keys[:, 0:HD], keys[:, 0:HD]], axis=0),
                jnp.concatenate([upper, lower], axis=0),
                TN,
                preferred_element_type=f32,
            )
            parts.append((qspan, spans, both[:, 0:HD], dv, column, dq))
        group = iota((SPAN, HD), 1) // HEADS
        for qspan, spans, dk, dv, column, dq in parts:
            dqt[qspan] += dq
            for u, span in enumerate(spans):
                rows = slice(u * SPAN, (u + 1) * SPAN)
                acc[span, :, 0:HD] += dk[rows]
                acc[span, :, HD : 2 * HD] += dv[rows]
                col[span % 2] += jnp.where(group == span // 2, column[rows], 0.0)
        return carry

    lax.fori_loop(0, (pairs_ref[PAIRS - 1] // WIDE + UNROLL - 1) // UNROLL, step, 0)
    for q in range(QSPANS):
        whole = dqt[q].T
        begin = (q % 2) * SPAN
        for h in range(HEADS):
            (dq0, dq1, dq2, dq3)[q // 2][begin : begin + SPAN, h * HD : (h + 1) * HD] = whole[h * SPAN : (h + 1) * SPAN]
    turned = col[...].reshape(ROWS, HD).T.reshape(2, SPAN, HD)
    col[...] = turned
    half = NZ * HEADS
    own_col[...] = col[0, pl.ds(pl.multiple_of(c * half, half), half), :]
    peer_col[...] = col[0, pl.ds(pl.multiple_of((1 - c) * half, half), half), :]
    for i in range(NZ):
        for part in range(2):
            rows = slice(part * SPAN, (part + 1) * SPAN)
            own_out[i, rows, :] = acc[2 * (c * NZ + i) + part]
            peer_out[i, rows, :] = acc[2 * ((1 - c) * NZ + i) + part]


def send_grads_kernel(own_ref, peer_ref, own_col, peer_col, mine_ref, other_ref, out_ref):
    x = lax.axis_index("x")
    row = iota((8, HD), 0)
    totals = jnp.zeros((8, HD), f32)
    for k in range(NX):
        both = mine_ref[8 * k : 8 * k + 8, :] + other_ref[8 * k : 8 * k + 8, :]
        totals = jnp.where(row == 2 * ((x + NX - k) % NX), both, totals)
    high, middle, low = three_terms(totals)
    right = jnp.concatenate([high + pltpu.roll(middle, 1, 0), low], axis=0)
    columns = own_col[...] + peer_col[...]
    for i in range(NZ):
        out_ref[i, 0:ROWS, :] = (own_ref[i] + peer_ref[i]).astype(bf16)
        group = columns[8 * (i // 2) : 8 * (i // 2) + 8]
        if i % 2:
            group = pltpu.roll(group, HEADS, 0)
        high, middle, low = three_terms(group)
        left = jnp.concatenate([jnp.where(row < HEADS, high, pltpu.roll(middle, HEADS, 0)), low], axis=0)
        out_ref[i, ROWS : ROWS + EXTRA, :] = jnp.concatenate([left, right], axis=1).astype(bf16)


def sum_queries_kernel(dq0, dq1, dq2, dq3, query_ref):
    query_ref[...] = (((dq0[...] + dq1[...]) + (dq2[...] + dq3[...])) * SCALE).astype(bf16)


def finish_kernel(order_ref, span_ref, in_ref, key_ref, value_ref, forget_ref):
    first = ((lax.axis_index("z") * NX + lax.axis_index("x")) * NC + lax.axis_index("core")) * 2
    total = in_ref[0].astype(f32)
    for i in range(1, NZ):
        total = total + in_ref[i].astype(f32)
    key_ref[...] = (total[0:ROWS, 0:HD] * SCALE).astype(bf16)
    value_ref[...] = total[0:ROWS, HD : 2 * HD].astype(bf16)
    extra = total[ROWS : ROWS + EXTRA]
    left, right = extra[:, 0:HD], extra[:, HD : 2 * HD]
    columns = left[0:8] + pltpu.roll(left[0:8], HEADS, 0) + left[8:16]
    totals = right[0:8] + pltpu.roll(right[0:8], 7, 0) + right[8:16]
    row, column = iota((8, HD), 0), iota((8, HD), 1)
    after = []
    for h in range(2):
        later = span_ref[...] > order_ref[first + h]
        line = jnp.sum(jnp.where(later, totals, 0.0), axis=0, keepdims=True)
        after.append(jnp.sum(jnp.where(column % HEADS == row, line, 0.0), axis=1, keepdims=True))
    within = exact_dot(columns, same_span_from(ROWS))
    within = within + jnp.where(column < SPAN, after[0], after[1])
    forget_ref[...] = -within[0:HEADS]


def call(kernel, specs, outs, scratch, flops, *args):
    place = {"s": pl.BlockSpec(memory_space=pltpu.SMEM), "v": pl.BlockSpec(memory_space=pltpu.VMEM)}
    return pl.pallas_call(
        kernel,
        in_specs=[place[k] for k in specs],
        out_specs=[place[k] for k, _, _ in outs],
        out_shape=[jax.ShapeDtypeStruct(shape, dtype) for _, shape, dtype in outs],
        scratch_shapes=[pltpu.VMEM(shape, dtype) for shape, dtype in scratch],
        compiler_params=pltpu.CompilerParams(vmem_limit_bytes=VMEM_LIMIT),
        cost_estimate=pl.CostEstimate(flops=flops, bytes_accessed=4 << 20, transcendentals=0),
    )(*args)


def body(queries, keys, values, out_grad, gate_logits, doc_lengths, span_order):
    swap = [(0, 1), (1, 0)]
    (log_forget,) = call(send_gates_kernel, "v", [("v", (NX * NY, 8, HD), f32)], [], 0, gate_logits.T)
    log_forget, keys, values = lax.optimization_barrier((log_forget, keys, values))
    logs = lax.all_to_all(log_forget, ("x", "head"), 0, 0)
    key_rows = jnp.concatenate([keys, values], axis=1)
    logs, key_rows = lax.optimization_barrier((logs, key_rows))
    message = (NZ, ROWS + EXTRA, 2 * HD)
    key_message, own_sums = call(
        send_keys_kernel,
        "vv",
        [("v", message, bf16), ("v", (NX * HEADS, ROWS), f32)],
        [],
        0,
        logs, key_rows,
    )

    key_message, queries, out_grad, span_order, doc_lengths = lax.optimization_barrier(
        (key_message, queries, out_grad, span_order, doc_lengths)
    )
    pair_rows = jnp.concatenate([queries, out_grad], axis=1)
    order4 = span_order.reshape(NZ, NX, NC, 2).transpose(3, 2, 0, 1)
    order_line = jnp.broadcast_to(order4[..., None], (2, NC, NZ, NX, HEADS)).reshape(2, NC * NZ * NX * HEADS)
    order_spans = jnp.broadcast_to(order4.transpose(3, 0, 1, 2)[..., None], (NX, 2, NC, NZ, HEADS)).reshape(NX, 1, HD)
    order_spans = jnp.concatenate([order_spans, jnp.full_like(order_spans, -1)], axis=1).reshape(2 * NX, HD)
    own = lax.all_to_all(key_message, "z", 0, 0)
    query_rows = [pair_rows]
    for k in range(1, NX):
        query_rows.append(lax.ppermute(pair_rows, "x", [(i, (i + k) % NX) for i in range(NX)]))
    plan = call(
        plan_kernel,
        "ssv",
        [
            ("v", (TARGETS, 2 * SOURCES), bf16),
            ("v", (3 * KEY_ROWS, 2 * HD), bf16),
            ("v", (QSPANS, LANES), i32),
            ("v", (QSPANS, LANES), i32),
            ("s", (PAIRS,), i32),
        ],
        [],
        1 << 28,
        span_order, doc_lengths, order_line,
    )
    own, query_rows, plan, order_spans = lax.optimization_barrier((own, query_rows, plan, order_spans))
    earlier, select, qpos, qdoc, pairs = plan
    peer = lax.ppermute(own, "core", swap)
    rows = call(
        gather_queries_kernel,
        "vvvv",
        [("v", (QSPANS, LANES, 2 * HD), bf16), ("v", (QSPANS, LANES, HD), bf16)],
        [],
        0,
        *query_rows,
    )
    peer, rows = lax.optimization_barrier((peer, rows))

    line = ((QSPANS, LANES), f32)
    stats, key_rows, qdecay, part, part_high = call(
        stats_kernel,
        "ssvvvvvvvvv",
        [
            ("v", (24, LANES), f32),
            ("v", (KSPANS, SPAN, 3 * HD), bf16),
            ("v", (QSPANS, LANES), f32),
            ("v", (CHUNKS, 8, LANES), f32),
            ("v", (CHUNKS, 8, LANES), f32),
        ],
        [((BLOCKS, 8, ROWS), f32), ((BLOCKS, EXTRA, HD), bf16), ((NX * HEADS, ROWS), f32), line, line, line],
        1 << 28,
        span_order, pairs, earlier, select, qpos, qdoc, own_sums, own, peer, *rows,
    )
    all_stats = [stats]
    for k in range(1, NX):
        all_stats.append(lax.ppermute(stats, "x", [(i, (i + k) % NX) for i in range(NX)]))
    total, lse, delta = call(
        totals_kernel,
        "svvvvvv",
        [("v", (8, HD), f32), ("v", (QSPANS, LANES), f32), ("v", (QSPANS, LANES), f32)],
        [],
        0,
        pairs, *all_stats, part, part_high,
    )
    totals = [total]
    for k in range(1, NX):
        totals.append(lax.ppermute(total, "x", [(i, (i + k) % NX) for i in range(NX)]))
    results = call(
        grads_kernel,
        "ssvvvvvvvv",
        [
            *[("v", (ROWS, HEADS * HD), f32)] * NX,
            ("v", (NZ, ROWS, 2 * HD), f32),
            ("v", (NZ, ROWS, 2 * HD), f32),
            ("v", (NZ * HEADS, ROWS), f32),
            ("v", (NZ * HEADS, ROWS), f32),
        ],
        [((KSPANS, SPAN, 2 * HD), f32), ((QSPANS, HD, LANES), f32), ((2, SPAN, HD), f32)],
        1 << 29,
        span_order, pairs, lse, delta, key_rows, *rows, qdecay, qpos, qdoc,
    )
    totals, results = lax.optimization_barrier((totals, results))
    dq0, dq1, dq2, dq3, own_sum, peer_sum, own_col, peer_col = results
    peer_sum = lax.ppermute(peer_sum, "core", swap)
    peer_col = lax.ppermute(peer_col, "core", swap)
    totals = jnp.concatenate(totals, axis=0)
    peer_totals = lax.ppermute(totals, "core", swap)
    (grad_message,) = call(
        send_grads_kernel,
        "vvvvvv",
        [("v", (NZ, ROWS + EXTRA, 2 * HD), bf16)],
        [],
        0,
        own_sum, peer_sum, own_col, peer_col, totals, peer_totals,
    )
    grad_message, dq1, dq2, dq3 = lax.optimization_barrier((grad_message, dq1, dq2, dq3))
    back = lax.all_to_all(grad_message, "z", 0, 0)
    parts = [
        lax.ppermute(part, "x", [(i, (i - k) % NX) for i in range(NX)]) for k, part in ((1, dq1), (2, dq2), (3, dq3))
    ]
    (query_grad,) = call(
        sum_queries_kernel, "vvvv", [("v", (ROWS, HEADS * HD), bf16)], [], 0, dq0, *parts
    )
    back, query_grad = lax.optimization_barrier((back, query_grad))
    key_grad, value_grad, forget_grad = call(
        finish_kernel,
        "svv",
        [
            ("v", (ROWS, HD), bf16),
            ("v", (ROWS, HD), bf16),
            ("v", (HEADS, ROWS), f32),
        ],
        [],
        0,
        span_order, order_spans, back,
    )
    return query_grad, key_grad, value_grad, forget_grad.T


def solution(mesh):
    fine = Mesh(mesh.devices.reshape(NZ, NX, NC, NY), ("z", "x", "core", "head"))
    ctx = ("z", "x", "core")
    rows = P(ctx, "head")
    return jax.shard_map(
        body,
        mesh=fine,
        in_specs=(rows, rows, rows, rows, P((*ctx, "head"), None), P(), P()),
        out_specs=(rows, rows, rows, rows),
        check_vma=False,
    )
```

```python
import functools
import math

import jax
import jax.numpy as jnp
from jax import lax
from jax.experimental import pallas as pl
from jax.experimental.pallas import tpu as pltpu
from jax.sharding import Mesh, PartitionSpec as P

NZ, NX, NC, NY = 8, 4, 2, 4
ROWS, SPAN, HEADS, HD = 128, 64, 4, 128
DOCS = 16
BLOCKS = NC * NZ
KEY_ROWS = BLOCKS * 8
SOURCES = BLOCKS * NX * HEADS
TARGETS = 2 * KEY_ROWS + 2 * NX * HEADS
QSPANS = 2 * NX
LANES = HEADS * SPAN
EXTRA = 16
KSPANS = 2 * BLOCKS
WIDE = 4
DEAD = QSPANS * KSPANS
STREAM = 8192
UNROLL = 4
PAIRS = DEAD + WIDE * UNROLL + 1
CHUNKS = DEAD // WIDE + UNROLL
TOGETHER = 12
NEG = -1e30
SCALE = 1.0 / math.sqrt(HD)
f32, bf16, i32 = jnp.float32, jnp.bfloat16, jnp.int32
VMEM_LIMIT = 16 * 1024 * 1024
NT = (((1,), (1,)), ((), ()))
TN = (((0,), (0,)), ((), ()))


def three_terms(a):
    high = a.astype(bf16).astype(f32)
    rest = a - high
    middle = rest.astype(bf16).astype(f32)
    return high, middle, rest - middle


def exact_dot(a, ones):
    terms = jnp.concatenate(three_terms(a), axis=0).astype(bf16)
    terms = jnp.dot(terms, ones.astype(bf16), preferred_element_type=f32)
    rows = a.shape[0]
    return terms[0:rows] + terms[rows : 2 * rows] + terms[2 * rows : 3 * rows]


def iota(shape, dim):
    return lax.broadcasted_iota(i32, shape, dim)


def same_span_upto(n):
    row, column = iota((n, n), 0), iota((n, n), 1)
    return jnp.where((row <= column) & (row // SPAN == column // SPAN), 1.0, 0.0).astype(f32)


def same_span_from(n):
    row, column = iota((n, n), 0), iota((n, n), 1)
    return jnp.where((row >= column) & (row // SPAN == column // SPAN), 1.0, 0.0).astype(f32)


def send_gates_kernel(gate_ref, out_ref):
    gates = gate_ref[...]
    small = jnp.exp(-jnp.abs(gates))
    w = 1.0 + small
    one = w == 1.0
    log_one_plus = jnp.where(one, small, jnp.log(w) * (small / jnp.where(one, 1.0, w - 1.0)))
    logs = jnp.minimum(gates, 0.0) - log_one_plus
    logs = jnp.concatenate([logs, jnp.zeros((NY * HEADS, HD - logs.shape[1]), f32)], axis=1)
    row = iota((8, HD), 0)
    for y in range(NY):
        group = logs[8 * (y // 2) : 8 * (y // 2) + 8]
        if y % 2:
            group = pltpu.roll(group, HEADS, 0)
        group = jnp.where(row < HEADS, group, 0.0)
        for x in range(NX):
            out_ref[x * NY + y] = group


def send_keys_kernel(log_ref, rows_ref, out_ref, sums_ref):
    parts = []
    for x in range(NX):
        total = log_ref[x * NY]
        for y in range(1, NY):
            total = total + pltpu.roll(log_ref[x * NY + y], 32 * y, 1)
        parts.append(total)
    logs = jnp.concatenate(
        [parts[0] + pltpu.roll(parts[1], HEADS, 0), parts[2] + pltpu.roll(parts[3], HEADS, 0)], axis=0
    )
    sums = exact_dot(logs, same_span_upto(ROWS))
    sums_ref[...] = sums
    x = lax.axis_index("x")
    row = iota((8, HD), 0)
    own = jnp.zeros((8, HD), f32)
    for h in range(HEADS):
        own = jnp.where(row == h, sums_ref[pl.ds(x * HEADS + h, 1), :], own)
    high, middle, low = three_terms(own)
    left = jnp.concatenate([high + pltpu.roll(middle, HEADS, 0), low], axis=0)
    terms = jnp.concatenate(three_terms(sums), axis=1).astype(bf16)
    row, column = iota((3 * HD, HD), 0), iota((3 * HD, HD), 1)
    wanted = (column // 2) * HD + (column % 2) * SPAN + SPAN - 1
    pick = jnp.where((row == wanted) & (column < 6), 1.0, 0.0).astype(bf16)
    right = jnp.dot(terms, pick, preferred_element_type=f32)
    extra = jnp.concatenate([left, right], axis=1).astype(bf16)
    rows = rows_ref[...]
    for i in range(NZ):
        out_ref[i, 0:ROWS, :] = rows
        out_ref[i, ROWS : ROWS + EXTRA, :] = extra


def gather_queries(refs, queries_ref, grads_ref):
    heads = jnp.where(iota((LANES, HD), 1) % HEADS == iota((LANES, HD), 0) // SPAN, 1.0, 0.0).astype(bf16)
    for k, ref in enumerate(refs):
        for half in range(2):
            rows = slice(half * SPAN, (half + 1) * SPAN)
            queries_ref[2 * k + half, :, HD : 2 * HD] = heads
            for h in range(HEADS):
                to = slice(h * SPAN, (h + 1) * SPAN)
                queries_ref[2 * k + half, to, 0:HD] = ref[rows, h * HD : (h + 1) * HD]
                grads_ref[2 * k + half, to, :] = ref[rows, (HEADS + h) * HD : (HEADS + h + 1) * HD]


def shared_span(x, q):
    return 2 * ((x + NX - q // 2) % NX) + q % 2


def spans_of_block(order_ref, x, block):
    first = ((block % NZ) * (NX * NC) + x * NC + block // NZ) * 2
    return order_ref[first], order_ref[first + 1]


def order_of_key(order_ref, x, span):
    block = span // 2
    return order_ref[((block % NZ) * (NX * NC) + x * NC + block // NZ) * 2 + span % 2]


def span_of_query(order_ref, z, x, c, q):
    return order_ref[((z * NX + (x + NX - q // 2) % NX) * NC + c) * 2 + q % 2]


def chunk_scores(order_ref, pairs_ref, t, x, keys_ref, queries_ref, grads_ref, qpos_ref, qdoc_ref):
    pairs = [pairs_ref[WIDE * t + u] for u in range(WIDE)]
    spans = [pair % KSPANS for pair in pairs]
    qspan = (pairs[0] % DEAD) // KSPANS
    keys = jnp.concatenate([keys_ref[span, :, 0 : 2 * HD] for span in spans], axis=0)
    values = jnp.concatenate([keys_ref[span, :, 2 * HD : 3 * HD] for span in spans], axis=0)
    scores = lax.dot_general(keys, queries_ref[qspan], NT, preferred_element_type=f32)
    slopes = lax.dot_general(values, grads_ref[qspan], NT, preferred_element_type=f32)
    at = pl.ds(qspan, 1)
    qpos, qdoc = qpos_ref[at, :][:, 0:HD], qdoc_ref[at, :][:, 0:HD]
    row = iota((SPAN, HD), 0)
    live = []
    for pair, span in zip(pairs, spans):
        key_pos = row + jnp.where(pair < DEAD, order_of_key(order_ref, x, span), 2 * STREAM) * SPAN
        half = (key_pos <= qpos) & (key_pos >= qdoc)
        live.append(jnp.concatenate([half, half], axis=1))
    return qspan, spans, keys, jnp.concatenate(live, axis=0), scores, slopes


def plan_kernel(order_ref, length_ref, line_ref, earlier_ref, select_ref, qpos_ref, qdoc_ref, pairs_ref):
    z, x, c = lax.axis_index("z"), lax.axis_index("x"), lax.axis_index("core")
    row = iota((KEY_ROWS, 1), 0)
    targets = []
    for half in range(2):
        target = jnp.zeros((KEY_ROWS, 1), i32)
        for block in range(BLOCKS):
            target = jnp.where(row // 8 == block, spans_of_block(order_ref, x, block)[half], target)
        targets.append(target)
    row = iota((NX * HEADS, 1), 0)
    for half in range(2):
        target = jnp.zeros((NX * HEADS, 1), i32)
        for i in range(NX):
            target = jnp.where(row // HEADS == i, order_ref[((z * NX + i) * NC + c) * 2 + half], target)
        targets.append(target)
    target = jnp.concatenate(targets, axis=0)
    source = jnp.concatenate([line_ref[0:1, :], line_ref[1:2, :]], axis=1)
    shape = (TARGETS, 2 * SOURCES)
    earlier = (source < target) & (iota(shape, 0) % HEADS == iota(shape, 1) % HEADS)
    earlier_ref[...] = jnp.where(earlier, 1.0, 0.0).astype(bf16)
    row, column = iota((3 * KEY_ROWS, 2 * HD), 0), iota((3 * KEY_ROWS, 2 * HD), 1)
    term = (column % 16) // HEADS
    wanted = term * KEY_ROWS + (column // 16) * 8 + column % HEADS
    select_ref[...] = jnp.where((row == wanted) & (term < 3), 1.0, 0.0).astype(bf16)
    row, column = iota((QSPANS, LANES), 0), iota((QSPANS, LANES), 1)
    qpos = column % SPAN
    spans = []
    for q in range(QSPANS):
        spans.append(span_of_query(order_ref, z, x, c, q))
        qpos = qpos + jnp.where(row == q, spans[q] * SPAN, 0)
    starts = [jnp.int32(0)]
    for doc in range(DOCS - 1):
        starts.append(starts[-1] + length_ref[doc])
    qdoc = jnp.zeros((QSPANS, LANES), i32)
    for start in starts:
        qdoc = jnp.where(qpos >= start, start, qdoc)
    qpos_ref[...] = qpos
    qdoc_ref[...] = qdoc
    found = jnp.int32(0)
    for q in range(QSPANS):
        mine, begin = spans[q], jnp.int32(0)
        for start in starts:
            begin = jnp.where(mine * SPAN >= start, start, begin)

        def scan(span, found, q=q, mine=mine, begin=begin):
            order = order_of_key(order_ref, x, span)
            pairs_ref[found] = q * KSPANS + span
            return found + ((order <= mine) & (order * SPAN + SPAN > begin)).astype(i32)

        found = lax.fori_loop(0, KSPANS, scan, found, unroll=8)
        for i in range(WIDE - 1):
            pairs_ref[found + i] = DEAD + q * KSPANS
        found = (found + WIDE - 1) // WIDE * WIDE
    for i in range(WIDE * UNROLL):
        pairs_ref[found + i] = DEAD
    pairs_ref[PAIRS - 1] = found


def stats_kernel(
    order_ref, pairs_ref, earlier_ref, select_ref, qpos_ref, qdoc_ref, sums_ref, own_ref, peer_ref, qd0, qd1, qd2, qd3,
    stats_ref, keys_ref, queries_ref, grads_ref, qdecay_ref, part_ref, part_high_ref,
    decay, totals, qsums, high_s, mass_s, cross_s,
):
    z, x, c = lax.axis_index("z"), lax.axis_index("x"), lax.axis_index("core")
    gather_queries((qd0, qd1, qd2, qd3), queries_ref, grads_ref)
    for i in range(NZ):
        for ref, core in ((own_ref, c), (peer_ref, 1 - c)):
            block = core * NZ + i
            for half in range(2):
                rows = slice(half * SPAN, (half + 1) * SPAN)
                keys_ref[2 * block + half, :, 0:HD] = ref[i, rows, 0:HD]
                keys_ref[2 * block + half, :, 2 * HD : 3 * HD] = ref[i, rows, HD : 2 * HD]
            totals[block] = ref[i, ROWS : ROWS + EXTRA, HD : 2 * HD]
            terms = ref[i, ROWS : ROWS + EXTRA, 0:HD].astype(f32)
            decay[block] = terms[0:8] + pltpu.roll(terms[0:8], HEADS, 0) + terms[8:16]
    sources = totals[...].reshape(SOURCES, HD)
    first = jnp.dot(earlier_ref[:, 0:SOURCES], sources, preferred_element_type=f32)
    second = jnp.dot(earlier_ref[:, SOURCES : 2 * SOURCES], sources, preferred_element_type=f32)
    lane = iota((TARGETS, HD), 1)
    both = jnp.where(lane < 6, jnp.where(lane % 2 == 0, first, second), 0.0)
    before = jnp.sum(both, axis=1, keepdims=True)
    left = iota((KEY_ROWS, ROWS), 1) < SPAN
    sums = decay[...].reshape(KEY_ROWS, ROWS) + jnp.where(left, before[0:KEY_ROWS], before[KEY_ROWS : 2 * KEY_ROWS])
    own, rows = before[2 * KEY_ROWS :], NX * HEADS
    qsums[...] = sums_ref[...] + jnp.where(iota((rows, ROWS), 1) < SPAN, own[0:rows], own[rows : 2 * rows])
    terms = jnp.concatenate(three_terms(sums * (-1.0 / SCALE)), axis=0).astype(bf16)
    terms = lax.dot_general(terms, select_ref[...], TN, preferred_element_type=f32)
    group = iota((ROWS, HD), 1) // 16
    for block in range(BLOCKS):
        tile = terms[:, (block // 8) * HD : (block // 8 + 1) * HD]
        tile = jnp.where(group == block % 8, tile, 0.0).astype(bf16)
        for half in range(2):
            keys_ref[2 * block + half, :, HD : 2 * HD] = tile[half * SPAN : (half + 1) * SPAN]
    for k in range(NX):
        for h in range(HEADS):
            own = qsums[pl.ds(((x + NX - k) % NX) * HEADS + h, 1), :]
            for half in range(2):
                qdecay_ref[2 * k + half : 2 * k + half + 1, h * SPAN : (h + 1) * SPAN] = own[
                    :, half * SPAN : (half + 1) * SPAN
                ]
    high_s[...] = jnp.full((QSPANS, LANES), NEG, f32)
    mass_s[...] = jnp.zeros((QSPANS, LANES), f32)
    cross_s[...] = jnp.zeros((QSPANS, LANES), f32)

    def step(t, carry):
        parts = []
        for u in range(UNROLL):
            qspan, _, _, live, scores, slopes = chunk_scores(
                order_ref, pairs_ref, UNROLL * t + u, x, keys_ref, queries_ref, grads_ref, qpos_ref, qdoc_ref
            )
            scores = jnp.where(live, scores * SCALE + qdecay_ref[pl.ds(qspan, 1), :], NEG)
            high = jnp.max(scores, axis=0, keepdims=True)
            weights = jnp.exp(scores - high)
            sums, row = jnp.zeros((8, LANES), f32), iota((8, LANES), 0)
            for first, array in ((0, weights), (4, weights * slopes)):
                for i in range(4):
                    one = jnp.sum(array[i * SPAN : (i + 1) * SPAN], axis=0, keepdims=True)
                    sums = jnp.where(row == first + i, one, sums)
            part_ref[UNROLL * t + u] = sums
            part_high_ref[UNROLL * t + u] = jnp.broadcast_to(high, (8, LANES))
            parts.append(
                (qspan, high, jnp.sum(sums[0:4], axis=0, keepdims=True), jnp.sum(sums[4:8], axis=0, keepdims=True))
            )
        for qspan, high, mass, cross in parts:
            at = pl.ds(shared_span(x, qspan), 1)
            old = high_s[at, :]
            new = jnp.maximum(old, high)
            before, now = jnp.exp(old - new), jnp.exp(high - new)
            high_s[at, :] = new
            mass_s[at, :] = mass_s[at, :] * before + mass * now
            cross_s[at, :] = cross_s[at, :] * before + cross * now
        return carry

    lax.fori_loop(0, (pairs_ref[PAIRS - 1] // WIDE + UNROLL - 1) // UNROLL, step, 0)
    stats_ref[0:8, :] = high_s[...]
    stats_ref[8:16, :] = mass_s[...]
    stats_ref[16:24, :] = cross_s[...]


def totals_kernel(pairs_ref, stats0, stats1, stats2, stats3, part_ref, part_high_ref, total_ref, lse_ref, delta_ref):
    x = lax.axis_index("x")
    stats = [(ref[0:8, :], ref[8:16, :], ref[16:24, :]) for ref in (stats0, stats1, stats2, stats3)]
    high = stats[0][0]
    for one, _, _ in stats[1:]:
        high = jnp.maximum(high, one)
    mass, cross = jnp.zeros_like(high), jnp.zeros_like(high)
    for one, one_mass, one_cross in stats:
        factor = jnp.exp(one - high)
        mass = mass + one_mass * factor
        cross = cross + one_cross * factor
    lse_ref[...] = high + jnp.log(mass)
    delta_ref[...] = cross / mass
    heads = jnp.where(iota((LANES, HD), 1) % HEADS == iota((LANES, HD), 0) // SPAN, 1.0, 0.0).astype(f32)
    chunks = pairs_ref[PAIRS - 1] // WIDE
    row = iota((8, LANES), 0)
    group = iota((1, HD), 1) // HEADS

    def step(t, total):
        rows, places = [], []
        for u in range(TOGETHER):
            chunk = jnp.minimum(TOGETHER * t + u, chunks - 1)
            at = pl.ds(shared_span(x, (pairs_ref[WIDE * chunk] % DEAD) // KSPANS), 1)
            scale = jnp.exp(part_high_ref[chunk] - lse_ref[at, :])
            rows.append(scale * part_ref[chunk] * jnp.where(row < 4, -delta_ref[at, :], 1.0))
            none = jnp.where(TOGETHER * t + u < chunks, 0, HD)
            spans = [pairs_ref[WIDE * chunk + i] % KSPANS for i in range(WIDE)]
            places.append([span // 2 + (span % 2) * BLOCKS + none for span in spans])
        sums = exact_dot(jnp.concatenate(rows, axis=0), heads)
        for u in range(TOGETHER):
            for i in range(WIDE):
                one = sums[8 * u + i : 8 * u + i + 1] + sums[8 * u + i + 4 : 8 * u + i + 5]
                total = total + jnp.where(group == places[u][i], one, 0.0)
        return total

    total = lax.fori_loop(0, (chunks + TOGETHER - 1) // TOGETHER, step, jnp.zeros((1, HD), f32))
    total_ref[...] = jnp.broadcast_to(total, total_ref.shape)


def grads_kernel(
    order_ref, pairs_ref, lse_ref, delta_ref, keys_ref, queries_ref, grads_ref, qdecay_ref, qpos_ref, qdoc_ref,
    dq0, dq1, dq2, dq3, own_out, peer_out, own_col, peer_col,
    acc, dqt, col,
):
    x, c = lax.axis_index("x"), lax.axis_index("core")
    acc[...] = jnp.zeros_like(acc)
    dqt[...] = jnp.zeros_like(dqt)
    col[...] = jnp.zeros_like(col)

    def step(t, carry):
        parts = []
        for u in range(UNROLL):
            qspan, spans, keys, live, scores, slopes = chunk_scores(
                order_ref, pairs_ref, UNROLL * t + u, x, keys_ref, queries_ref, grads_ref, qpos_ref, qdoc_ref
            )
            at = pl.ds(shared_span(x, qspan), 1)
            shift = qdecay_ref[pl.ds(qspan, 1), :] - lse_ref[at, :]
            probs = jnp.exp(jnp.where(live, scores * SCALE + shift, NEG))
            dscores = probs * (slopes - delta_ref[at, :])
            upper = dscores.astype(bf16)
            lower = (dscores - upper.astype(f32)).astype(bf16)
            queries = queries_ref[qspan]
            both = jnp.dot(upper, queries, preferred_element_type=f32)
            dv = jnp.dot(probs.astype(bf16), grads_ref[qspan], preferred_element_type=f32)
            column = both[:, HD : 2 * HD] + jnp.dot(lower, queries[:, HD : 2 * HD], preferred_element_type=f32)
            dq = lax.dot_general(
                jnp.concatenate([keys[:, 0:HD], keys[:, 0:HD]], axis=0),
                jnp.concatenate([upper, lower], axis=0),
                TN,
                preferred_element_type=f32,
            )
            parts.append((qspan, spans, both[:, 0:HD], dv, column, dq))
        group = iota((SPAN, HD), 1) // HEADS
        for qspan, spans, dk, dv, column, dq in parts:
            dqt[qspan] += dq
            for u, span in enumerate(spans):
                rows = slice(u * SPAN, (u + 1) * SPAN)
                acc[span, :, 0:HD] += dk[rows]
                acc[span, :, HD : 2 * HD] += dv[rows]
                col[span % 2] += jnp.where(group == span // 2, column[rows], 0.0)
        return carry

    lax.fori_loop(0, (pairs_ref[PAIRS - 1] // WIDE + UNROLL - 1) // UNROLL, step, 0)
    for q in range(QSPANS):
        whole = dqt[q].T
        begin = (q % 2) * SPAN
        for h in range(HEADS):
            (dq0, dq1, dq2, dq3)[q // 2][begin : begin + SPAN, h * HD : (h + 1) * HD] = whole[h * SPAN : (h + 1) * SPAN]
    turned = col[...].reshape(ROWS, HD).T.reshape(2, SPAN, HD)
    col[...] = turned
    half = NZ * HEADS
    own_col[...] = col[0, pl.ds(pl.multiple_of(c * half, half), half), :]
    peer_col[...] = col[0, pl.ds(pl.multiple_of((1 - c) * half, half), half), :]
    for i in range(NZ):
        for part in range(2):
            rows = slice(part * SPAN, (part + 1) * SPAN)
            own_out[i, rows, :] = acc[2 * (c * NZ + i) + part]
            peer_out[i, rows, :] = acc[2 * ((1 - c) * NZ + i) + part]


def send_grads_kernel(own_ref, peer_ref, own_col, peer_col, mine_ref, other_ref, out_ref):
    x = lax.axis_index("x")
    row = iota((8, HD), 0)
    totals = jnp.zeros((8, HD), f32)
    for k in range(NX):
        both = mine_ref[8 * k : 8 * k + 8, :] + other_ref[8 * k : 8 * k + 8, :]
        totals = jnp.where(row == 2 * ((x + NX - k) % NX), both, totals)
    high, middle, low = three_terms(totals)
    right = jnp.concatenate([high + pltpu.roll(middle, 1, 0), low], axis=0)
    columns = own_col[...] + peer_col[...]
    for i in range(NZ):
        out_ref[i, 0:ROWS, :] = (own_ref[i] + peer_ref[i]).astype(bf16)
        group = columns[8 * (i // 2) : 8 * (i // 2) + 8]
        if i % 2:
            group = pltpu.roll(group, HEADS, 0)
        high, middle, low = three_terms(group)
        left = jnp.concatenate([jnp.where(row < HEADS, high, pltpu.roll(middle, HEADS, 0)), low], axis=0)
        out_ref[i, ROWS : ROWS + EXTRA, :] = jnp.concatenate([left, right], axis=1).astype(bf16)


def sum_queries_kernel(dq0, dq1, dq2, dq3, query_ref):
    query_ref[...] = (((dq0[...] + dq1[...]) + (dq2[...] + dq3[...])) * SCALE).astype(bf16)


def finish_kernel(order_ref, span_ref, in_ref, key_ref, value_ref, forget_ref):
    first = ((lax.axis_index("z") * NX + lax.axis_index("x")) * NC + lax.axis_index("core")) * 2
    total = in_ref[0].astype(f32)
    for i in range(1, NZ):
        total = total + in_ref[i].astype(f32)
    key_ref[...] = (total[0:ROWS, 0:HD] * SCALE).astype(bf16)
    value_ref[...] = total[0:ROWS, HD : 2 * HD].astype(bf16)
    extra = total[ROWS : ROWS + EXTRA]
    left, right = extra[:, 0:HD], extra[:, HD : 2 * HD]
    columns = left[0:8] + pltpu.roll(left[0:8], HEADS, 0) + left[8:16]
    totals = right[0:8] + pltpu.roll(right[0:8], 7, 0) + right[8:16]
    row, column = iota((8, HD), 0), iota((8, HD), 1)
    after = []
    for h in range(2):
        later = span_ref[...] > order_ref[first + h]
        line = jnp.sum(jnp.where(later, totals, 0.0), axis=0, keepdims=True)
        after.append(jnp.sum(jnp.where(column % HEADS == row, line, 0.0), axis=1, keepdims=True))
    within = exact_dot(columns, same_span_from(ROWS))
    within = within + jnp.where(column < SPAN, after[0], after[1])
    forget_ref[...] = -within[0:HEADS]


def call(kernel, specs, outs, scratch, flops, *args):
    place = {"s": pl.BlockSpec(memory_space=pltpu.SMEM), "v": pl.BlockSpec(memory_space=pltpu.VMEM)}
    return pl.pallas_call(
        kernel,
        in_specs=[place[k] for k in specs],
        out_specs=[place[k] for k, _, _ in outs],
        out_shape=[jax.ShapeDtypeStruct(shape, dtype) for _, shape, dtype in outs],
        scratch_shapes=[pltpu.VMEM(shape, dtype) for shape, dtype in scratch],
        compiler_params=pltpu.CompilerParams(vmem_limit_bytes=VMEM_LIMIT),
        cost_estimate=pl.CostEstimate(flops=flops, bytes_accessed=4 << 20, transcendentals=0),
    )(*args)


def body(queries, keys, values, out_grad, gate_logits, doc_lengths, span_order):
    swap = [(0, 1), (1, 0)]
    (log_forget,) = call(send_gates_kernel, "v", [("v", (NX * NY, 8, HD), f32)], [], 0, gate_logits.T)
    log_forget, keys, values = lax.optimization_barrier((log_forget, keys, values))
    logs = lax.all_to_all(log_forget, ("x", "head"), 0, 0)
    key_rows = jnp.concatenate([keys, values], axis=1)
    logs, key_rows = lax.optimization_barrier((logs, key_rows))
    message = (NZ, ROWS + EXTRA, 2 * HD)
    key_message, own_sums = call(
        send_keys_kernel,
        "vv",
        [("v", message, bf16), ("v", (NX * HEADS, ROWS), f32)],
        [],
        0,
        logs, key_rows,
    )

    key_message, queries, out_grad, span_order, doc_lengths = lax.optimization_barrier(
        (key_message, queries, out_grad, span_order, doc_lengths)
    )
    pair_rows = jnp.concatenate([queries, out_grad], axis=1)
    order4 = span_order.reshape(NZ, NX, NC, 2).transpose(3, 2, 0, 1)
    order_line = jnp.broadcast_to(order4[..., None], (2, NC, NZ, NX, HEADS)).reshape(2, NC * NZ * NX * HEADS)
    order_spans = jnp.broadcast_to(order4.transpose(3, 0, 1, 2)[..., None], (NX, 2, NC, NZ, HEADS)).reshape(NX, 1, HD)
    order_spans = jnp.concatenate([order_spans, jnp.full_like(order_spans, -1)], axis=1).reshape(2 * NX, HD)
    own = lax.all_to_all(key_message, "z", 0, 0)
    query_rows = [pair_rows]
    for k in range(1, NX):
        query_rows.append(lax.ppermute(pair_rows, "x", [(i, (i + k) % NX) for i in range(NX)]))
    plan = call(
        plan_kernel,
        "ssv",
        [
            ("v", (TARGETS, 2 * SOURCES), bf16),
            ("v", (3 * KEY_ROWS, 2 * HD), bf16),
            ("v", (QSPANS, LANES), i32),
            ("v", (QSPANS, LANES), i32),
            ("s", (PAIRS,), i32),
        ],
        [],
        1 << 28,
        span_order, doc_lengths, order_line,
    )
    own, query_rows, plan, order_spans = lax.optimization_barrier((own, query_rows, plan, order_spans))
    earlier, select, qpos, qdoc, pairs = plan
    peer = lax.ppermute(own, "core", swap)

    line = ((QSPANS, LANES), f32)
    stats, *rows, qdecay, part, part_high = call(
        stats_kernel,
        "ssvvvvvvvvvvv",
        [
            ("v", (24, LANES), f32),
            ("v", (KSPANS, SPAN, 3 * HD), bf16),
            ("v", (QSPANS, LANES, 2 * HD), bf16),
            ("v", (QSPANS, LANES, HD), bf16),
            ("v", (QSPANS, LANES), f32),
            ("v", (CHUNKS, 8, LANES), f32),
            ("v", (CHUNKS, 8, LANES), f32),
        ],
        [((BLOCKS, 8, ROWS), f32), ((BLOCKS, EXTRA, HD), bf16), ((NX * HEADS, ROWS), f32), line, line, line],
        1 << 28,
        span_order, pairs, earlier, select, qpos, qdoc, own_sums, own, peer, *query_rows,
    )
    all_stats = [stats]
    for k in range(1, NX):
        all_stats.append(lax.ppermute(stats, "x", [(i, (i + k) % NX) for i in range(NX)]))
    total, lse, delta = call(
        totals_kernel,
        "svvvvvv",
        [("v", (8, HD), f32), ("v", (QSPANS, LANES), f32), ("v", (QSPANS, LANES), f32)],
        [],
        0,
        pairs, *all_stats, part, part_high,
    )
    totals = [total]
    for k in range(1, NX):
        totals.append(lax.ppermute(total, "x", [(i, (i + k) % NX) for i in range(NX)]))
    results = call(
        grads_kernel,
        "ssvvvvvvvv",
        [
            *[("v", (ROWS, HEADS * HD), f32)] * NX,
            ("v", (NZ, ROWS, 2 * HD), f32),
            ("v", (NZ, ROWS, 2 * HD), f32),
            ("v", (NZ * HEADS, ROWS), f32),
            ("v", (NZ * HEADS, ROWS), f32),
        ],
        [((KSPANS, SPAN, 2 * HD), f32), ((QSPANS, HD, LANES), f32), ((2, SPAN, HD), f32)],
        1 << 29,
        span_order, pairs, lse, delta, *rows, qdecay, qpos, qdoc,
    )
    totals, results = lax.optimization_barrier((totals, results))
    dq0, dq1, dq2, dq3, own_sum, peer_sum, own_col, peer_col = results
    peer_sum = lax.ppermute(peer_sum, "core", swap)
    peer_col = lax.ppermute(peer_col, "core", swap)
    totals = jnp.concatenate(totals, axis=0)
    peer_totals = lax.ppermute(totals, "core", swap)
    (grad_message,) = call(
        send_grads_kernel,
        "vvvvvv",
        [("v", (NZ, ROWS + EXTRA, 2 * HD), bf16)],
        [],
        0,
        own_sum, peer_sum, own_col, peer_col, totals, peer_totals,
    )
    grad_message, dq1, dq2, dq3 = lax.optimization_barrier((grad_message, dq1, dq2, dq3))
    back = lax.all_to_all(grad_message, "z", 0, 0)
    parts = [
        lax.ppermute(part, "x", [(i, (i - k) % NX) for i in range(NX)]) for k, part in ((1, dq1), (2, dq2), (3, dq3))
    ]
    (query_grad,) = call(
        sum_queries_kernel, "vvvv", [("v", (ROWS, HEADS * HD), bf16)], [], 0, dq0, *parts
    )
    back, query_grad = lax.optimization_barrier((back, query_grad))
    key_grad, value_grad, forget_grad = call(
        finish_kernel,
        "svv",
        [
            ("v", (ROWS, HD), bf16),
            ("v", (ROWS, HD), bf16),
            ("v", (HEADS, ROWS), f32),
        ],
        [],
        0,
        span_order, order_spans, back,
    )
    return query_grad, key_grad, value_grad, forget_grad.T


def solution(mesh):
    fine = Mesh(mesh.devices.reshape(NZ, NX, NC, NY), ("z", "x", "core", "head"))
    ctx = ("z", "x", "core")
    rows = P(ctx, "head")
    return jax.shard_map(
        body,
        mesh=fine,
        in_specs=(rows, rows, rows, rows, P((*ctx, "head"), None), P(), P()),
        out_specs=(rows, rows, rows, rows),
        check_vma=False,
    )
```
